32 devices in a mesh: dp: 8 (over y, x, core), fsdp: 4 (over z).
Axes of the slice: x: 2, y: 2, z: 4, core: 2. Of those that a mesh axis runs over, the one named last changes fastest.
Arguments:
- images: bfloat16 [64, 197, 768], P(('dp', 'fsdp')), may hold values from -6 to 6
- gain_one: bfloat16 [768], P(('dp', 'fsdp')), may hold values from 0.5 to 1.5
- w_qkv: bfloat16 [768, 2304], P(('dp', 'fsdp')), may hold values from -0.21875 to 0.21875
- w_out: bfloat16 [768, 768], P(('dp', 'fsdp')), may hold values from -1.75 to 1.75
- gain_two: bfloat16 [768], P(('dp', 'fsdp')), may hold values from 0.5 to 1.5
- w_router: bfloat16 [768, 4], P(('dp', 'fsdp')), may hold values from -0.16992188 to 0.16992188
- w_in: bfloat16 [4, 768, 3072], P('fsdp', 'dp'), may hold values from -0.21875 to 0.21875
- w_back: bfloat16 [4, 3072, 768], P('fsdp', 'dp'), may hold values from -1.25 to 1.25
- choices: int32 [64, 197, 2], P(('dp', 'fsdp')), may hold values from 0 to 3, all different within a row
- priority: int32 [64, 197], P(('dp', 'fsdp')), may hold values from 0 to 196, each once within a row
- cotangent: bfloat16 [64, 197, 768], P(('dp', 'fsdp')), may hold values from -6 to 6
Outputs:
- output: bfloat16 [64, 197, 768], P(('dp', 'fsdp'))
- input_grad: float32 [64, 197, 768], P(('dp', 'fsdp'))
- grad_gain_one: float32 [768], P(('dp', 'fsdp'))
- grad_qkv: float32 [768, 2304], P(('dp', 'fsdp'))
- grad_out: float32 [768, 768], P(('dp', 'fsdp'))
- grad_gain_two: float32 [768], P(('dp', 'fsdp'))
- grad_router: float32 [768, 4], P(('dp', 'fsdp'))
- grad_in: float32 [4, 768, 3072], P('fsdp', 'dp')
- grad_back: float32 [4, 3072, 768], P('fsdp', 'dp')
The draws below stay inside these ranges and needn't reach their ends.
Inputs may be any that keep to these rules, and one draw needn't show every extreme that they name: `choices`: the two experts of a token differ. `priority`: each row orders the 197 tokens of one routing group, each number once.
All inputs are finite; a program needn't handle non-finite values.
Results may differ from the reference program's by a relative error of at most 0.018.
Values may be sent and summed in bfloat16 or wider, within the bound.
A program may use at most 192 MiB of HBM per device.

```python
import jax
import jax.numpy as jnp
from jax import lax

D = 768
HEADS = 12
HEAD_DIM = 64
FF = 3072
SEQ = 197
IMG_MB = 1
TOK_MB = 197
IMAGES = 64
GROUPS = 64
EXPERTS = 4
CAP = 104


def shard_levels(stream_key, shape, shards, smallest, top_value):
    gain = 1.0
    for dim, blocks in shards:
        draws = jax.random.uniform(jax.random.fold_in(jax.random.fold_in(stream_key, 6), dim), (blocks,), jnp.float32, smallest / len(shards), top_value / len(shards))
        gain = gain * jnp.repeat(jnp.exp(draws), shape[dim] // blocks).reshape((-1,) + (1,) * (len(shape) - 1 - dim))
    return gain


def different_ones(rng, rows, amount, top, lift):
    order = jax.random.permutation(jax.random.fold_in(rng, 1), amount)
    favour = order
    for power in range(3):
        favour = favour * favour // amount
    favour = favour * lift // amount
    chance = jax.random.randint(jax.random.fold_in(rng, 2), (rows, amount), 0, 4096) + favour
    fixed_rows = jax.random.permutation(jax.random.fold_in(rng, 3), rows)[jnp.arange(amount) % rows]
    chance = jnp.where(jnp.arange(rows)[:, None] == fixed_rows[None, :], 1 << 14, chance)
    score = chance * amount + jnp.arange(amount)
    return lax.top_k(score.astype(jnp.int32), top)[1].astype(jnp.int32)


def centred(key, dims, deviation, bound, split=(), kind=jnp.bfloat16):
    factor_of = shard_levels(key, dims, split, -0.22, 0.18) if split else 1.0
    array = jax.random.normal(key, dims, jnp.float32) * deviation * factor_of
    return jnp.minimum(jnp.maximum(array, -bound), bound).astype(kind)


def setup_inputs(seed: int = 0) -> dict:
    seeds = jax.random.split(jax.random.key(seed), 12)
    return {
        "images": centred(seeds[0], (IMAGES, SEQ, D), 1.0, 6.0, ((0, 32),)),
        "gain_one": jnp.clip(1.0 + 0.1 * jax.random.normal(seeds[1], (D,), jnp.float32), 0.5, 1.5).astype(jnp.bfloat16),
        "w_qkv": centred(seeds[2], (D, 3 * D), D ** -0.5, 0.21875, ((0, 32),)),
        "w_out": centred(seeds[3], (D, D), (D // 64) ** -0.5, 1.75, ((0, 32),)),
        "gain_two": jnp.clip(1.0 + 0.1 * jax.random.normal(seeds[4], (D,), jnp.float32), 0.5, 1.5).astype(jnp.bfloat16),
        "w_router": centred(seeds[5], (D, EXPERTS), 0.029, 0.16992188, ((0, 32),)),
        "w_in": centred(seeds[6], (EXPERTS, D, FF), D ** -0.5, 0.21875, ((0, 4), (1, 8))),
        "w_back": centred(seeds[7], (EXPERTS, FF, D), (max(FF // 128, 1)) ** -0.5, 1.25, ((0, 4), (1, 8))),
        "choices": different_ones(seeds[8], IMAGES * SEQ, EXPERTS, 2, 8192).reshape((IMAGES, SEQ, 2)),
        "priority": jax.vmap(lambda own: jax.random.permutation(own, TOK_MB))(jax.random.split(seeds[9], GROUPS)).reshape((GROUPS, TOK_MB)).astype(jnp.int32),
        "cotangent": centred(seeds[10], (IMAGES, SEQ, D), 1.0, 6.0, ((0, 32),)),
    }


highest = lax.Precision.HIGHEST
epsilon = 1e-06

@jax.custom_vjp
def low(v):
    return lax.optimization_barrier(v.astype(jnp.bfloat16)).astype(jnp.float32)

@jax.custom_vjp
def low_back(v):
    return v

def low_keep(v):
    return (low(v), None)

def low_pass(kept, grad):
    return (grad,)

def back_keep(v):
    return (v, None)

def back_low(kept, grad):
    return (low(grad),)
low.defvjp(low_keep, low_pass)
low_back.defvjp(back_keep, back_low)

def layer_norm(token_rows, gain_vec):
    centre = token_rows - lax.optimization_barrier(jnp.mean(token_rows, axis=-1, keepdims=True))
    spread = lax.optimization_barrier(jnp.mean(centre * centre, axis=-1, keepdims=True))
    return centre * lax.rsqrt(spread + epsilon) * gain_vec

def route_slots(chosen, ranking, expert_count, capacity):
    earlier_mask = ranking[None, :] < ranking[:, None]
    first_same = chosen[None, :, 0] == chosen[:, None, 0]
    second_same = chosen[None, :, 1] == chosen[:, None, 1]
    first_rank = lax.optimization_barrier(jnp.sum((earlier_mask & first_same).astype(jnp.int32), axis=1))
    second_rank = lax.optimization_barrier(jnp.sum((earlier_mask & second_same).astype(jnp.int32), axis=1))
    first_load = lax.optimization_barrier(jnp.sum((chosen[None, :, 0] == chosen[:, None, 1]).astype(jnp.int32), axis=1))
    position = jnp.stack([first_rank, second_rank + first_load], axis=1)
    kept_mask = position < capacity
    slot_index = jnp.where(kept_mask, chosen * capacity + position, expert_count * capacity)
    return slot_index.astype(jnp.int32)

def group_forward(params, tokens, chosen, ranking):
    gain_one, w_qkv, w_out, gain_two, w_router, w_in, w_back = params
    token_rows = tokens.reshape(-1, D)
    first_in = low(layer_norm(token_rows, gain_one))
    mixed_rows = low(low_back(jnp.dot(first_in, w_qkv, precision=highest)))
    mixed_rows = mixed_rows.reshape(IMG_MB, SEQ, 3, HEADS, HEAD_DIM)
    queries = mixed_rows[:, :, 0]
    key_rows = mixed_rows[:, :, 1]
    value_rows = mixed_rows[:, :, 2]
    scores = low_back(jnp.einsum('bqhd,bkhd->bhqk', queries, key_rows, precision=highest) * HEAD_DIM ** (-0.5))
    probs = low(jax.nn.softmax(scores, axis=-1))
    attended = jnp.einsum('bhqk,bkhd->bqhd', probs, value_rows, precision=highest).reshape(-1, D)
    attended = low(low_back(attended))
    residual = token_rows + low_back(jnp.dot(attended, w_out, precision=highest))
    second_in = low(layer_norm(residual, gain_two))
    logits = jnp.dot(second_in, w_router, precision=highest)
    router_probs = jax.nn.softmax(logits, axis=-1)
    gate_values = jnp.take_along_axis(router_probs, chosen, axis=1)
    slot_index = route_slots(chosen, ranking, EXPERTS, CAP)
    buffer = jnp.zeros((EXPERTS * CAP + 1, D), jnp.float32)
    buffer = buffer.at[slot_index.reshape(-1)].set(jnp.repeat(second_in, 2, axis=0))
    buffer = low_back(buffer[:-1].reshape(EXPERTS, CAP, D))
    hidden = low_back(jnp.einsum('ecd,edf->ecf', buffer, w_in, precision=highest))
    activated = low(jax.nn.gelu(hidden, approximate=True))
    expert_out = low(low_back(jnp.einsum('ecf,efd->ecd', activated, w_back, precision=highest)))
    padded = jnp.concatenate([expert_out.reshape(-1, D), jnp.zeros((1, D), jnp.float32)], axis=0)
    picked = padded[slot_index]
    combined = lax.optimization_barrier(jnp.sum(picked * gate_values[:, :, None], axis=1))
    return (residual + combined).reshape(IMG_MB, SEQ, D)

def reference(images, gain_one, w_qkv, w_out, gain_two, w_router, w_in, w_back, choices, priority, cotangent):
    params = (gain_one.astype(jnp.float32), w_qkv.astype(jnp.float32), w_out.astype(jnp.float32), gain_two.astype(jnp.float32), w_router.astype(jnp.float32), w_in.astype(jnp.float32), w_back.astype(jnp.float32))
    groups = images.astype(jnp.float32).reshape(-1, IMG_MB, SEQ, D)
    chosen_all = choices.reshape(-1, IMG_MB * SEQ, 2).astype(jnp.int32)
    group_step = jax.checkpoint(group_forward)

    def forward(param_set, group_tokens):

        def scan_body(scan_carry, packed):
            return (scan_carry, group_step(param_set, packed[0], packed[1], packed[2]))
        stacked = lax.scan(scan_body, jnp.float32(0.0), (group_tokens, chosen_all, priority))[1]
        return stacked
    result, pullback = jax.vjp(forward, params, groups)
    grad_params, grad_groups = pullback(cotangent.astype(jnp.float32).reshape(groups.shape))
    return (result.reshape(images.shape).astype(jnp.bfloat16), grad_groups.reshape(images.shape), grad_params[0], grad_params[1], grad_params[2], grad_params[3], grad_params[4], grad_params[5], grad_params[6])
```

```python
import math
from functools import partial

import jax
import jax.numpy as jnp
from jax import lax
from jax.experimental import pallas as pl
from jax.experimental.pallas import tpu as pltpu
from jax.sharding import PartitionSpec as P

f32, bf16 = jnp.float32, jnp.bfloat16

MESH = pl.DeviceIdType.MESH
ANY = pl.BlockSpec(memory_space=pl.ANY)
VM = pl.BlockSpec(memory_space=pltpu.VMEM)


class Place:
    def __init__(self, ndp, nz):
        self.ndp, self.nz, self.chips = ndp, nz, ndp // 2
        self.dp = lax.axis_index("dp")
        self.z = lax.axis_index("fsdp")
        self.core = lax.rem(self.dp, 2)
        self.chip = self.dp // 2
        self.square = self.chips == 4
        if self.square:
            a, b, c = self.chip // 2, lax.rem(self.chip, 2), self.core
            self.near = lax.rem(a + 1 - c, 2) * 2 + lax.rem(b + c, 2)
            self.side = lax.rem(a + c, 2) * 2 + lax.rem(b + 1 - c, 2)
            self.far = (1 - a) * 2 + (1 - b)
            self.mates = [self.near, self.side, self.far]
        else:
            self.mates = [lax.rem(self.chip + k, self.chips) for k in range(1, self.chips)]

    def at_chip(self, chip):
        return (chip * 2 + self.core, self.z)

    def sibling(self):
        return (self.chip * 2 + 1 - self.core, self.z)

    def at_z(self, k):
        return (self.dp, lax.rem(self.z + k, self.nz))

    def z_from(self, k):
        return lax.rem(self.z + self.nz - k, self.nz)

    def greet(self, line, plane):
        bar = pltpu.get_barrier_semaphore()
        there = []
        if plane:
            there.append(self.sibling())
            there += [self.at_chip(m) for m in (self.mates[:2] if self.square else self.mates)]
        if line:
            there += [self.at_z(k) for k in range(1, self.nz)]
        for dev in there:
            pl.semaphore_signal(bar, inc=1, device_id=dev, device_id_type=MESH)
        pl.semaphore_wait(bar, len(there))


def remote(src, dst, send, recv, dev):
    return pltpu.make_async_remote_copy(
        src_ref=src, dst_ref=dst, send_sem=send, recv_sem=recv, device_id=dev, device_id_type=MESH
    )


class PlaneGather:
    def __init__(self, place, own, slot, send, recv):
        self.p, self.own, self.slot = place, own, slot
        self.send, self.recv = send, recv
        p = place
        mine = slot(p.dp)
        self.to_sib = remote(own, mine, send(0), recv(0), p.sibling())
        if p.square:
            self.first = [
                remote(own, mine, send(1), recv(1), p.at_chip(p.near)),
                remote(own, mine, send(2), recv(2), p.at_chip(p.side)),
            ]
            at = lambda m: slot(m * 2 + p.core)
            self.relay = remote(at(p.side), at(p.side), send(3), recv(3), p.at_chip(p.near))
            self.share = [
                remote(at(m), at(m), send(4 + i), recv(4 + i), p.sibling())
                for i, m in enumerate(p.mates)
            ]
        else:
            at = lambda m: slot(m * 2 + p.core)
            n = len(p.mates)
            self.first = [
                remote(own, mine, send(1 + i), recv(1 + i), p.at_chip(m)) for i, m in enumerate(p.mates)
            ]
            back = [lax.rem(p.chip + p.chips - k, p.chips) for k in range(1, p.chips)]
            self.share = [
                remote(at(m), at(m), send(1 + n + i), recv(1 + n + i), p.sibling())
                for i, m in enumerate(back)
            ]

    @staticmethod
    def sems(ndp):
        chips = ndp // 2
        return 7 if chips == 4 else 1 + 2 * (chips - 1)

    def start(self):
        for cp in self.first:
            cp.start()
        self.to_sib.start()

    def middle(self):
        if self.p.square:
            self.first[1].wait_recv()
            self.relay.start()
            self.share[1].start()
            self.first[0].wait_recv()
            self.share[0].start()
        else:
            for f, s in zip(self.first, self.share):
                f.wait_recv()
                s.start()

    def last(self):
        if self.p.square:
            self.relay.wait_recv()
            self.share[2].start()

    def finish(self):
        self.to_sib.wait()
        for s in self.share:
            s.wait()
        for f in self.first:
            f.wait_send()
        if self.p.square:
            self.relay.wait_send()


def layer_gather_kernel(ndp, nz, x_ref, g_ref, send, recv, zsend, zrecv, lsem):
    p = Place(ndp, nz)
    p.greet(True, True)
    me = p.dp * nz + p.z
    local = pltpu.make_async_copy(x_ref, g_ref.at[me], lsem)
    local.start()
    line = {
        k: remote(x_ref, g_ref.at[me], zsend.at[k], zrecv.at[k], p.at_z(k)) for k in range(1, nz)
    }

    def unit(k):
        zk = p.z_from(k)
        own = x_ref if k == 0 else g_ref.at[p.dp * nz + zk]
        return PlaneGather(
            p, own, lambda d: g_ref.at[d * nz + zk], lambda i: send.at[k, i], lambda i: recv.at[k, i]
        )

    units = [unit(k) for k in range(nz)]
    for k in range(1, nz):
        line[k].start()
    units[0].start()
    for k in range(1, nz):
        line[k].wait_recv()
        units[k].start()
        units[k - 1].middle()
        if k >= 2:
            units[k - 2].last()
    units[nz - 1].middle()
    if nz >= 2:
        units[nz - 2].last()
    units[nz - 1].last()
    for u in units:
        u.finish()
    for k in range(1, nz):
        line[k].wait_send()
    local.wait()


def layer_gather(ndp, nz, shard, cid):
    ns = PlaneGather.sems(ndp)
    return pl.pallas_call(
        partial(layer_gather_kernel, ndp, nz),
        out_shape=jax.ShapeDtypeStruct((ndp * nz,) + shard.shape, shard.dtype),
        in_specs=[ANY],
        out_specs=ANY,
        scratch_shapes=[
            pltpu.SemaphoreType.DMA((nz, ns)),
            pltpu.SemaphoreType.DMA((nz, ns)),
            pltpu.SemaphoreType.DMA((nz,)),
            pltpu.SemaphoreType.DMA((nz,)),
            pltpu.SemaphoreType.DMA,
        ],
        compiler_params=pltpu.CompilerParams(collective_id=cid, has_side_effects=True),
        name="layer_gather",
    )(shard)


HEAD_DIM = 64
EPS = 1e-6


def norm_parts(rows):
    centred = rows - jnp.mean(rows, axis=-1, keepdims=True)
    inverse = lax.rsqrt(jnp.mean(centred * centred, axis=-1, keepdims=True) + EPS)
    return centred * inverse, inverse


def dot(a, b):
    return lax.dot_general(a, b, (((1,), (0,)), ((), ())), preferred_element_type=f32)


def dot_nt(a, b):
    return lax.dot_general(a, b, (((1,), (1,)), ((), ())), preferred_element_type=f32)


def dot_tn(a, b):
    return lax.dot_general(a, b, (((0,), (0,)), ((), ())), preferred_element_type=f32)


class Exchange:
    def __init__(self, p, src, dst, send, recv):
        self.copies = []
        for k in range(1, p.nz):
            dev = p.at_z(k)
            self.copies.append(remote(src.at[dev[1]], dst.at[p.z], send.at[k], recv.at[k], dev))
        self.local = pltpu.make_async_copy(src.at[p.z], dst.at[p.z], send.at[0])

    def start(self):
        for cp in self.copies:
            cp.start()
        self.local.start()

    def wait(self):
        for cp in self.copies:
            cp.wait()
        self.local.wait()


def route(info, place_ref, image, cap, slots, experts):
    cols = jnp.transpose(info)
    rank_c, one_c, two_c = cols[:, 0:1], cols[:, 1:2], cols[:, 2:3]
    rank_r, one_r, two_r = info[0:1, :], info[1:2, :], info[2:3, :]
    lanes = info.shape[1]
    earlier = rank_c < rank_r
    count = lambda m: jnp.sum(jnp.where(m, 1.0, 0.0), axis=0, keepdims=True)
    pos_one = count(earlier & (one_c == one_r))
    pos_two = count(earlier & (two_c == two_r)) + count(one_c == two_r)
    code = lambda pos, pick: jnp.where(
        (pos < cap) & (pick >= 0), pick * slots + (pos + image * cap), -1.0
    ).astype(jnp.int32)
    code_one, code_two = code(pos_one, one_r), code(pos_two, two_r)
    for e in range(experts):
        slot = lax.broadcasted_iota(jnp.int32, (slots, lanes), 0) + e * slots
        hit = (slot == code_one) | (slot == code_two)
        place_ref[e * slots : (e + 1) * slots, image * lanes : (image + 1) * lanes] = jnp.where(
            hit, 1.0, 0.0
        ).astype(bf16)


def attend_kernel(
    ndp, nz, cap, seq, experts, images,
    x_ref, dy_ref, info_ref, gain_ref, wqkv_ref, wout_ref, win_ref, wback_ref,
    wi_ref, wb_ref, rtok_ref, rdy_ref, place_ref, mixed_ref, probs_ref, att_ref, res_ref,
    tok_ref, stok_ref, sdy_ref, gsend, grecv, tsend, trecv, ysend, yrecv, lsem,
):
    p = Place(ndp, nz)
    rows, d = x_ref.shape[1], x_ref.shape[2]
    lanes = info_ref.shape[2]
    slots = stok_ref.shape[1]
    pairs = d // 128
    p.greet(True, True)
    units, locals_ = [], []
    for t in range(win_ref.shape[0]):
        for w, (own, full) in enumerate(((win_ref, wi_ref), (wback_ref, wb_ref))):
            n = t * 2 + w
            units.append(
                PlaneGather(
                    p, own.at[t], lambda dd, full=full, t=t: full.at[t, dd],
                    lambda i, n=n: gsend.at[n, i], lambda i, n=n: grecv.at[n, i],
                )
            )
            locals_.append(pltpu.make_async_copy(own.at[t], full.at[t, p.dp], lsem.at[n]))
    for u, lc in zip(units, locals_):
        u.start()
        lc.start()

    tok_ref[...] = jnp.zeros_like(tok_ref)
    for i in range(images):
        route(info_ref[i], place_ref, i, cap, slots, experts)
        tok_ref[i * lanes : i * lanes + rows, :] = dy_ref[i]

    def dispatch(out_ref):
        @pl.loop(0, experts)
        def _(e):
            out_ref[e] = dot(
                place_ref[pl.ds(pl.multiple_of(e * slots, slots), slots), :], tok_ref[...]
            ).astype(bf16)

    dispatch(sdy_ref)
    send_dy = Exchange(p, sdy_ref, rdy_ref, ysend, yrecv)
    send_dy.start()

    gain_one, gain_two = gain_ref[0:1, :], gain_ref[1:2, :]
    if mixed_ref.shape[1] > rows:
        for i in range(images):
            mixed_ref[i, rows:, :] = jnp.zeros((mixed_ref.shape[1] - rows, 3 * d), bf16)

    @pl.loop(0, images)
    def _(i):
        normed, _inv = norm_parts(x_ref[i].astype(f32))
        first = (normed * gain_one).astype(bf16)
        for part in range(3):
            mixed_ref[i, :rows, part * d : (part + 1) * d] = dot(
                first, wqkv_ref[:, part * d : (part + 1) * d]
            ).astype(bf16)

    low_half = lax.broadcasted_iota(jnp.int32, (1, 128), 1) < HEAD_DIM
    valid = lax.broadcasted_iota(jnp.int32, (1, lanes), 1) < seq

    @pl.loop(0, images * pairs)
    def _(n):
        i = n // pairs
        at = lambda part: pl.ds(pl.multiple_of(part * d + (n - i * pairs) * 128, 128), 128)
        q, k, v = mixed_ref[i, :rows, at(0)], mixed_ref[i, :, at(1)], mixed_ref[i, :, at(2)]
        got = []
        for h in range(2):
            mask = low_half if h == 0 else ~low_half
            scores = dot_nt(jnp.where(mask, q, jnp.zeros_like(q)), k) * HEAD_DIM**-0.5
            scores = jnp.where(valid, scores, -1e30)
            e = jnp.exp(scores - jnp.max(scores, axis=-1, keepdims=True))
            prob = (e / jnp.sum(e, axis=-1, keepdims=True)).astype(bf16)
            probs_ref[n * 2 + h] = prob
            got.append(dot(prob, v))
        att_ref[i, :, at(0)] = jnp.where(low_half, got[0], got[1]).astype(bf16)

    @pl.loop(0, images)
    def _(i):
        residual = x_ref[i].astype(f32) + dot(att_ref[i], wout_ref[...])
        res_ref[i] = residual
        normed, _inv = norm_parts(residual)
        tok_ref[pl.ds(pl.multiple_of(i * lanes, lanes), rows), :] = (normed * gain_two).astype(bf16)

    dispatch(stok_ref)
    send_tok = Exchange(p, stok_ref, rtok_ref, tsend, trecv)
    send_tok.start()
    for u in units:
        u.middle()
    for u in units:
        u.last()
    for u, lc in zip(units, locals_):
        u.finish()
        lc.wait()
    send_dy.wait()
    send_tok.wait()


def attend(ndp, nz, cap, slots, seq, experts, cid, x, dy, info, gain, wqkv, wout, win, wback):
    images, rows, d = x.shape
    lanes = info.shape[2]
    tiles = win.shape[0]
    ns = PlaneGather.sems(ndp)
    shape = jax.ShapeDtypeStruct
    dma = pltpu.SemaphoreType.DMA
    return pl.pallas_call(
        partial(attend_kernel, ndp, nz, cap, seq, experts, images),
        out_shape=(
            shape((tiles, ndp) + win.shape[1:], bf16),
            shape((tiles, ndp) + wback.shape[1:], bf16),
            shape((nz, slots, d), bf16),
            shape((nz, slots, d), bf16),
            shape((experts * slots, images * lanes), bf16),
            shape((images, lanes, 3 * d), bf16),
            shape((images * d // HEAD_DIM, rows, lanes), bf16),
            shape((images, rows, d), bf16),
            shape((images, rows, d), f32),
        ),
        in_specs=[VM] * 6 + [ANY] * 2,
        out_specs=(ANY,) * 4 + (VM,) * 5,
        scratch_shapes=[
            pltpu.VMEM((images * lanes, d), bf16),
            pltpu.VMEM((experts, slots, d), bf16),
            pltpu.VMEM((experts, slots, d), bf16),
            dma((2 * tiles, ns)), dma((2 * tiles, ns)),
            dma((nz,)), dma((nz,)), dma((nz,)), dma((nz,)),
            dma((2 * tiles,)),
        ],
        compiler_params=pltpu.CompilerParams(
            collective_id=cid, has_side_effects=True, vmem_limit_bytes=60 << 20
        ),
        name="attend",
    )(x, dy, info, gain, wqkv, wout, win, wback)


class PlaneScatter:
    def __init__(self, place, part, sib, got, out, send, recv):
        self.p, self.part, self.sib, self.got, self.out = place, part, sib, got, out
        p = place
        self.pair = remote(part.at[:, 1 - p.core], sib, send(0), recv(0), p.sibling())
        at = lambda m: part.at[m, p.core]
        if p.square:
            self.first = [
                remote(at(p.far), got.at[0], send(1), recv(1), p.at_chip(p.near)),
                remote(at(p.near), got.at[1], send(2), recv(2), p.at_chip(p.near)),
            ]
            self.second = remote(at(p.side), got.at[2], send(3), recv(3), p.at_chip(p.side))
        else:
            self.first = [
                remote(at(m), got.at[i], send(1 + i), recv(1 + i), p.at_chip(m))
                for i, m in enumerate(p.mates)
            ]

    @staticmethod
    def sems(ndp):
        chips = ndp // 2
        return 4 if chips == 4 else chips

    @staticmethod
    def blocks(ndp):
        return ndp // 2 - 1

    def add(self, m, more):
        here = self.part.at[m, self.p.core]
        here[...] = (here[...].astype(f32) + more.astype(f32)).astype(here.dtype)

    def start(self):
        self.pair.start()

    def middle(self):
        p = self.p
        self.pair.wait_recv()
        if p.square:
            self.add(p.far, self.sib[p.far])
            self.first[0].start()
            self.add(p.near, self.sib[p.near])
            self.first[1].start()
            self.add(p.side, self.sib[p.side])
        else:
            for m, cp in zip(p.mates, self.first):
                self.add(m, self.sib[m])
                cp.start()

    def last(self):
        if self.p.square:
            self.first[0].wait_recv()
            self.add(self.p.side, self.got[0])
            self.second.start()

    def finish(self):
        p = self.p
        total = self.part[p.chip, p.core].astype(f32) + self.sib[p.chip].astype(f32)
        if p.square:
            self.first[1].wait_recv()
            total += self.got[1].astype(f32)
            self.second.wait_recv()
            total += self.got[2].astype(f32)
        else:
            for i, cp in enumerate(self.first):
                cp.wait_recv()
                total += self.got[i].astype(f32)
        self.out[...] = total
        for cp in [self.pair] + self.first + ([self.second] if p.square else []):
            cp.wait_send()


def expert_kernel(
    ndp, nz, experts,
    wi_ref, wb_ref, buf_ref, dy_ref, wr_ref,
    rgrad_ref, eo_ref, gi_ref, gb_ref, gr_ref,
    gs_ref, buft_ref, act_ref, gh_ref, oacc_ref, gacc_ref, pin_ref, pback_ref,
    sin_ref, sback_ref, xin_ref, xback_ref, sgrad_ref, rp_ref,
    ssend, srecv, esend, erecv,
):
    p = Place(ndp, nz)
    tiles, d, width = wi_ref.shape
    slots = buf_ref.shape[1]
    rows = nz * slots
    p.greet(True, True)

    lane = lax.broadcasted_iota(jnp.int32, (1, 128), 1)

    @pl.loop(0, nz)
    def _(s):
        logits = dot(buf_ref[s], wr_ref[...])
        logits = jnp.where(lane < experts, logits, -1e30)
        ex = jnp.exp(logits - jnp.max(logits, axis=-1, keepdims=True))
        rp = ex / jnp.sum(ex, axis=-1, keepdims=True)
        rp_ref[s] = rp
        gate = jnp.sum(jnp.where(lane == p.z, rp, 0.0), axis=-1, keepdims=True)
        gs_ref[s] = (gate * dy_ref[s].astype(f32)).astype(bf16)

    buft_ref[...] = jnp.transpose(buf_ref[...].reshape(rows, d))

    scatters = []
    for t in range(tiles):
        for w, (part, sib, got, out) in enumerate(
            ((pin_ref, sin_ref, xin_ref, gi_ref), (pback_ref, sback_ref, xback_ref, gb_ref))
        ):
            n = t * 2 + w
            scatters.append(
                PlaneScatter(
                    p, part.at[t], sib.at[t], got.at[t], out.at[t],
                    lambda i, n=n: ssend.at[n, i], lambda i, n=n: srecv.at[n, i],
                )
            )
    both = lambda t: scatters[2 * t : 2 * t + 2]

    step = min(256, width)
    per_in, per_back = d // ndp, width // ndp

    for t in range(tiles):

        @pl.loop(0, nz * (width // step))
        def _(n):
            s = n // (width // step)
            cols = pl.ds(pl.multiple_of((n - s * (width // step)) * step, step), step)
            h = dot(buf_ref[s], wi_ref[t, :, cols])
            grad = dot_nt(gs_ref[s], wb_ref[t, cols, :])
            k0, k1 = 0.7978845608028654, 0.044715 * 0.7978845608028654
            h2 = h * h
            th = jnp.tanh(h * (k0 + k1 * h2))
            half = 0.5 * (1.0 + th)
            act_ref[s, :, cols] = (h * half).astype(bf16)
            slope = half + 0.5 * h * (1.0 - th * th) * (k0 + 3.0 * k1 * h2)
            gh_ref[s, :, cols] = (grad * slope).astype(bf16)

        @pl.loop(0, nz)
        def _(s):
            o = dot(act_ref[s], wb_ref[t])
            g = dot_nt(gh_ref[s], wi_ref[t])
            if t == 0:
                oacc_ref[s] = o
                gacc_ref[s] = g
            else:
                oacc_ref[s] += o
                gacc_ref[s] += g

        @pl.loop(0, width // step)
        def _(n):
            cols = pl.ds(pl.multiple_of(n * step, step), step)
            got = dot(buft_ref[...], gh_ref[:, :, cols].reshape(rows, step)).astype(bf16)
            pin_ref[t, :, :, :, cols] = got.reshape(ndp // 2, 2, per_in, step)
            gotb = dot_tn(
                act_ref[:, :, cols].reshape(rows, step), gs_ref[...].reshape(rows, d)
            ).astype(bf16)
            many = step // per_back // 2
            pback_ref[t, pl.ds(n * many, many)] = gotb.reshape(many, 2, per_back, d)

        if t >= 2:
            for u in both(t - 2):
                u.last()
        if t >= 1:
            for u in both(t - 1):
                u.middle()
        for u in both(t):
            u.start()

    gr_ref[...] = jnp.zeros_like(gr_ref)

    @pl.loop(0, nz)
    def _(s):
        out = oacc_ref[s].astype(bf16)
        eo_ref[s] = out
        rp = rp_ref[s]
        mine = jnp.where(lane == p.z, 1.0, 0.0)
        gate = jnp.sum(mine * rp, axis=-1, keepdims=True)
        ggate = jnp.sum(out.astype(f32) * dy_ref[s].astype(f32), axis=-1, keepdims=True)
        contrib = (ggate * gate) * (mine - rp)
        hi = contrib.astype(bf16)
        lo = (contrib - hi.astype(f32)).astype(bf16)
        sgrad_ref[s] = (gacc_ref[s] + dot_nt(hi, wr_ref[...]) + dot_nt(lo, wr_ref[...])).astype(bf16)
        gr_ref[...] += dot_tn(buf_ref[s], hi) + dot_tn(buf_ref[s], lo)

    back = Exchange(p, sgrad_ref, rgrad_ref, esend, erecv)
    back.start()
    for u in both(tiles - 2):
        u.last()
    for u in both(tiles - 1):
        u.middle()
    for u in both(tiles - 1):
        u.last()
    for u in scatters:
        u.finish()
    back.wait()


def expert(ndp, nz, experts, cid, wi, wb, buf, dy, wr):
    tiles, d, width = wi.shape
    slots = buf.shape[1]
    rows = nz * slots
    per_in, per_back = d // ndp, width // ndp
    chips = ndp // 2
    shape = jax.ShapeDtypeStruct
    dma = pltpu.SemaphoreType.DMA
    nb = PlaneScatter.blocks(ndp)
    return pl.pallas_call(
        partial(expert_kernel, ndp, nz, experts),
        out_shape=(
            shape((nz, slots, d), bf16),
            shape((nz, slots, d), bf16),
            shape((tiles, per_in, width), f32),
            shape((tiles, per_back, d), f32),
            shape((d, 128), f32),
        ),
        in_specs=[VM] * 5,
        out_specs=(ANY, VM, VM, VM, VM),
        scratch_shapes=[
            pltpu.VMEM((nz, slots, d), bf16),
            pltpu.VMEM((d, rows), bf16),
            pltpu.VMEM((nz, slots, width), bf16),
            pltpu.VMEM((nz, slots, width), bf16),
            pltpu.VMEM((nz, slots, d), f32),
            pltpu.VMEM((nz, slots, d), f32),
            pltpu.VMEM((tiles, chips, 2, per_in, width), bf16),
            pltpu.VMEM((tiles, chips, 2, per_back, d), bf16),
            pltpu.VMEM((tiles, chips, per_in, width), bf16),
            pltpu.VMEM((tiles, chips, per_back, d), bf16),
            pltpu.VMEM((tiles, nb, per_in, width), bf16),
            pltpu.VMEM((tiles, nb, per_back, d), bf16),
            pltpu.VMEM((nz, slots, d), bf16),
            pltpu.VMEM((nz, slots, 128), f32),
            dma((2 * tiles, PlaneScatter.sems(ndp))), dma((2 * tiles, PlaneScatter.sems(ndp))),
            dma((nz,)), dma((nz,)),
        ],
        compiler_params=pltpu.CompilerParams(
            collective_id=cid, has_side_effects=True, vmem_limit_bytes=62 << 20
        ),
        name="expert",
    )(wi, wb, buf, dy, wr)


def norm_back(grad, normed, inverse):
    first = jnp.mean(grad, axis=-1, keepdims=True)
    second = normed * jnp.mean(grad * normed, axis=-1, keepdims=True)
    return inverse * (grad - first - second)


class LineScatter:
    def __init__(self, place, total, sent, got, out, send, recv):
        self.p, self.total, self.sent, self.got, self.out = place, total, sent, got, out
        self.copies = []
        for k in range(1, place.nz):
            dev = place.at_z(k)
            self.copies.append(
                remote(sent.at[dev[1]], got.at[place.z], send(k), recv(k), dev)
            )

    def start(self):
        count = self.out.shape[0]
        for k in range(self.p.nz):
            self.sent[k, :count, :] = self.total[k * count : (k + 1) * count, :].astype(
                self.sent.dtype
            )
        for cp in self.copies:
            cp.start()

    def finish(self):
        p, count = self.p, self.out.shape[0]
        for cp in self.copies:
            cp.wait()
        total = self.sent[p.z].astype(f32)
        for k in range(1, p.nz):
            total += self.got[p.z_from(k)].astype(f32)
        self.out[...] = total[:count]


def back_kernel(
    ndp, nz, experts,
    rg_ref, eo_ref, place_ref, x_ref, dy_ref, mixed_ref, probs_ref, att_ref, res_ref,
    gain_ref, wqkv_ref, wout_ref, wr_ref, gr_ref,
    out_ref, gin_ref, gl_ref, gsm_ref,
    ro_ref, gres_ref, branch_ref, gatt_ref, gmix_ref, first_ref, vec_ref,
    part_ref, sib_ref, got_ref, tot_ref, psm_ref, ssm_ref, xsm_ref, tsm_ref,
    zsent_ref, zgot_ref, zssm_ref, zgsm_ref,
    ysend, yrecv, ssend, srecv, zsend, zrecv,
):
    p = Place(ndp, nz)
    images, rows, d = x_ref.shape
    lanes = place_ref.shape[1] // images
    slots = rg_ref.shape[0] // experts
    pairs = d // 128
    chips, per = ndp // 2, d // ndp
    p.greet(True, True)
    outs = Exchange(p, eo_ref, ro_ref, ysend, yrecv)
    outs.start()

    scatters, lines = [], []
    for n in range(5):
        part, sib, got, tot, zs, zg, out = (
            (part_ref.at[n], sib_ref.at[n], got_ref.at[n], tot_ref.at[n],
             zsent_ref.at[n], zgot_ref.at[n], gl_ref.at[n])
            if n < 4
            else (psm_ref, ssm_ref, xsm_ref, tsm_ref, zssm_ref, zgsm_ref, gsm_ref)
        )
        scatters.append(
            PlaneScatter(p, part, sib, got, tot, lambda i, n=n: ssend.at[n, i], lambda i, n=n: srecv.at[n, i])
        )
        lines.append(
            LineScatter(p, tot, zs, zg, out, lambda i, n=n: zsend.at[n, i], lambda i, n=n: zrecv.at[n, i])
        )

    gain_one, gain_two = gain_ref[0:1, :], gain_ref[1:2, :]
    vec_ref[...] = jnp.zeros_like(vec_ref)

    @pl.loop(0, images)
    def _(i):
        hits = place_ref[:, pl.ds(pl.multiple_of(i * lanes, lanes), lanes)]
        grad_second = dot_tn(hits, rg_ref[...])[:rows]
        normed, inverse = norm_parts(res_ref[i])
        vec_ref[1:2, :] += jnp.sum(grad_second * normed, axis=0, keepdims=True)
        grad = dy_ref[i].astype(f32) + norm_back(grad_second * gain_two, normed, inverse)
        gres_ref[i] = grad
        branch = grad.astype(bf16)
        branch_ref[i] = branch
        gatt_ref[i] = dot_nt(branch, wout_ref[...]).astype(bf16)
        normed_one, _inv = norm_parts(x_ref[i].astype(f32))
        first_ref[i] = (normed_one * gain_one).astype(bf16)

    part_ref[3] = (
        dot_tn(att_ref[...].reshape(images * rows, d), branch_ref[...].reshape(images * rows, d))
        .astype(bf16)
        .reshape(chips, 2, per, d)
    )
    scatters[3].start()

    low_half = lax.broadcasted_iota(jnp.int32, (1, 128), 1) < HEAD_DIM
    scale = HEAD_DIM**-0.5

    @pl.loop(0, images * pairs)
    def _(n):
        i = n // pairs
        at = lambda part: pl.ds(pl.multiple_of(part * d + (n - i * pairs) * 128, 128), 128)
        q, k, v = mixed_ref[i, :rows, at(0)], mixed_ref[i, :, at(1)], mixed_ref[i, :, at(2)]
        ga = gatt_ref[i, :, at(0)]
        gq, gk, gv = [], [], []
        for h in range(2):
            mask = low_half if h == 0 else ~low_half
            prob = probs_ref[n * 2 + h]
            gv.append(dot_tn(prob, ga)[:rows])
            weighting = dot_nt(jnp.where(mask, ga, jnp.zeros_like(ga)), v)
            wide = prob.astype(f32)
            scores = wide * (weighting - jnp.sum(wide * weighting, axis=-1, keepdims=True))
            scores = scores.astype(bf16)
            gq.append(dot(scores, k))
            gk.append(dot_tn(scores, q)[:rows])
        pick = lambda pair, by: jnp.where(low_half, pair[0], pair[1]) * by
        gmix_ref[i, :, at(0)] = pick(gq, scale).astype(bf16)
        gmix_ref[i, :, at(1)] = pick(gk, scale).astype(bf16)
        gmix_ref[i, :, at(2)] = pick(gv, 1.0).astype(bf16)

    scatters[3].middle()
    for n in range(3):
        part_ref[n] = (
            dot_tn(
                first_ref[...].reshape(images * rows, d),
                gmix_ref[:, :, n * d : (n + 1) * d].reshape(images * rows, d),
            )
            .astype(bf16)
            .reshape(chips, 2, per, d)
        )
        scatters[n].start()

    scatters[3].last()

    @pl.loop(0, images)
    def _(i):
        grad_first = dot_nt(gmix_ref[i], wqkv_ref[...])
        normed, inverse = norm_parts(x_ref[i].astype(f32))
        vec_ref[0:1, :] += jnp.sum(grad_first * normed, axis=0, keepdims=True)
        gin_ref[i] = gres_ref[i] + norm_back(grad_first * gain_one, normed, inverse)

    lane = lax.broadcasted_iota(jnp.int32, (1, 128), 1)
    cols = jnp.transpose(vec_ref[...])
    small = jnp.where(
        lane == experts, cols[:, 0:1], jnp.where(lane == experts + 1, cols[:, 1:2], gr_ref[...])
    )
    psm_ref[...] = small.reshape(chips, 2, per, 128)
    scatters[4].start()
    order = (0, 1, 2, 4)
    for n in order:
        scatters[n].middle()
    scatters[3].finish()
    lines[3].start()
    for n in order:
        scatters[n].last()
    outs.wait()

    @pl.loop(0, images)
    def _(i):
        normed, _inv = norm_parts(res_ref[i])
        logits = dot((normed * gain_two).astype(bf16), wr_ref[...])
        logits = jnp.where(lane < experts, logits, -1e30)
        ex = jnp.exp(logits - jnp.max(logits, axis=-1, keepdims=True))
        rp = ex / jnp.sum(ex, axis=-1, keepdims=True)
        total = res_ref[i]
        for e in range(experts):
            hits = place_ref[e * slots : (e + 1) * slots, pl.ds(pl.multiple_of(i * lanes, lanes), lanes)]
            gate = jnp.sum(jnp.where(lane == e, rp, 0.0), axis=-1, keepdims=True)
            total = total + gate * dot_tn(hits, ro_ref[e])[:rows]
        out_ref[i] = total.astype(bf16)

    for n in order:
        scatters[n].finish()
        lines[n].start()
    for n in (3,) + order:
        lines[n].finish()


def back(ndp, nz, experts, cid, rgrad, eo, place, x, dy, mixed, probs, att, res, gain, wqkv, wout, wr, gr):
    images, rows, d = x.shape
    lanes = place.shape[1] // images
    chips, per = ndp // 2, d // ndp
    group = per // nz
    tall, short = -(-group // 16) * 16, -(-group // 8) * 8
    nb = PlaneScatter.blocks(ndp)
    slots = rgrad.shape[1]
    shape = jax.ShapeDtypeStruct
    dma = pltpu.SemaphoreType.DMA
    vm = pltpu.VMEM
    ns = PlaneScatter.sems(ndp)
    return pl.pallas_call(
        partial(back_kernel, ndp, nz, experts),
        out_shape=(
            shape((images, rows, d), bf16),
            shape((images, rows, d), f32),
            shape((4, group, d), f32),
            shape((group, 128), f32),
        ),
        in_specs=[VM, ANY] + [VM] * 12,
        out_specs=(VM,) * 4,
        scratch_shapes=[
            vm((nz, slots, d), bf16),
            vm((images, rows, d), f32),
            vm((images, rows, d), bf16),
            vm((images, rows, d), bf16),
            vm((images, rows, 3 * d), bf16),
            vm((images, rows, d), bf16),
            vm((8, d), f32),
            vm((4, chips, 2, per, d), bf16),
            vm((4, chips, per, d), bf16),
            vm((4, nb, per, d), bf16),
            vm((4, per, d), f32),
            vm((chips, 2, per, 128), f32),
            vm((chips, per, 128), f32),
            vm((nb, per, 128), f32),
            vm((per, 128), f32),
            vm((4, nz, tall, d), bf16),
            vm((4, nz, tall, d), bf16),
            vm((nz, short, 128), f32),
            vm((nz, short, 128), f32),
            dma((nz,)), dma((nz,)),
            dma((5, ns)), dma((5, ns)),
            dma((5, nz)), dma((5, nz)),
        ],
        compiler_params=pltpu.CompilerParams(
            collective_id=cid, has_side_effects=True, vmem_limit_bytes=62 << 20
        ),
        name="back",
    )(rgrad.reshape(experts * slots, d), eo, place, x, dy, mixed, probs, att, res, gain, wqkv, wout, wr, gr)


def up(value, unit):
    return -(-value // unit) * unit


def per_device(ndp, nz, images, gain_one, w_qkv, w_out, gain_two, w_router, w_in, w_back, choices, priority, cotangent):
    count, seq, d = images.shape
    experts, ff = w_router.shape[1], w_in.shape[2]
    devices = ndp * nz
    group = d // devices
    cap = (42 * seq + 20 * experts - 1) // (20 * experts)
    slots = up(count * cap, 16)
    rows, lanes = up(seq, 16), up(seq, 128)
    tiles = 3
    chunk = ff // ndp // tiles

    fold = 16 // math.gcd(group, 16)
    thin = 4 * d // fold
    small = jnp.concatenate([gain_one[:, None], gain_two[:, None], w_router], axis=1)
    flat = jnp.pad(small.reshape(-1), (0, group * fold * 128 - small.size)).reshape(group * fold, 128)
    main = jnp.concatenate([w_qkv, w_out], axis=1)
    main = main.reshape(group, fold, thin).transpose(1, 0, 2).reshape(group * fold, thin)
    layers = layer_gather(ndp, nz, jnp.concatenate([main, flat], axis=1), 0)
    main = layers[:, :, :thin].reshape(devices, fold, group, thin).transpose(0, 2, 1, 3).reshape(d, 4 * d)
    wqkv, wout = main[:, : 3 * d], main[:, 3 * d :]
    small = layers[:, :, thin:].reshape(devices, -1)[:, : group * (2 + experts)].reshape(d, 2 + experts)
    gain = jnp.pad(small[:, :2].astype(f32).T, ((0, 6), (0, 0)))
    wr = jnp.pad(small[:, 2:], ((0, 0), (0, 128 - experts)))

    x = jnp.pad(images, ((0, 0), (0, rows - seq), (0, 0)))
    dy = jnp.pad(cotangent, ((0, 0), (0, rows - seq), (0, 0)))
    info = jnp.stack([priority, choices[:, :, 0], choices[:, :, 1]], axis=1).astype(f32)
    info = jnp.concatenate(
        [
            jnp.pad(info[:, :1], ((0, 0), (0, 0), (0, lanes - seq)), constant_values=1e6),
            jnp.pad(info[:, 1:2], ((0, 0), (0, 0), (0, lanes - seq)), constant_values=-1.0),
            jnp.pad(info[:, 2:], ((0, 0), (0, 0), (0, lanes - seq)), constant_values=-2.0),
            jnp.zeros((count, 5, lanes), f32),
        ],
        axis=1,
    )
    win = w_in[0].reshape(d // ndp, ndp, tiles, chunk).transpose(2, 0, 1, 3).reshape(tiles, d // ndp, ndp * chunk)
    wback = w_back[0].reshape(tiles, chunk, d)
    wi, wb, rtok, rdy, place, mixed, probs, att, res = attend(
        ndp, nz, cap, slots, seq, experts, 1, x, dy, info, gain, wqkv, wout, win, wback
    )
    rgrad, eo, gi, gb, gr = expert(
        ndp, nz, experts, 2,
        wi.reshape(tiles, d, ndp * chunk), wb.reshape(tiles, ndp * chunk, d), rtok, rdy, wr,
    )
    out, gin, gl, gsm = back(
        ndp, nz, experts, 3, rgrad, eo, place, x, dy, mixed, probs, att, res, gain, wqkv, wout, wr, gr
    )
    grad_qkv = jnp.concatenate([gl[0], gl[1], gl[2]], axis=1)
    grad_in = gi.reshape(tiles, d // ndp, ndp, chunk).transpose(1, 2, 0, 3).reshape(1, d // ndp, ff)
    return (
        out[:, :seq], gin[:, :seq], gsm[:, experts], grad_qkv, gl[3], gsm[:, experts + 1], gsm[:, :experts],
        grad_in, gb.reshape(1, ff // ndp, d),
    )


def solution(mesh):
    ndp, nz = mesh.shape["dp"], mesh.shape["fsdp"]
    both = ("dp", "fsdp")
    tokens, rows, expert_rows = P(both, None, None), P(both, None), P("fsdp", "dp", None)
    return jax.shard_map(
        partial(per_device, ndp, nz),
        mesh=mesh,
        in_specs=(tokens, P(both), rows, rows, P(both), rows, expert_rows, expert_rows, tokens, rows, tokens),
        out_specs=(tokens, tokens, P(both), rows, rows, P(both), rows, expert_rows, expert_rows),
        check_vma=False,
    )
```

```python
import math
from functools import partial

import jax
import jax.numpy as jnp
from jax import lax
from jax.experimental import pallas as pl
from jax.experimental.pallas import tpu as pltpu
from jax.sharding import PartitionSpec as P

f32, bf16 = jnp.float32, jnp.bfloat16
MESH = pl.DeviceIdType.MESH
ANY = pl.BlockSpec(memory_space=pl.ANY)
VM = pl.BlockSpec(memory_space=pltpu.VMEM)
HEAD_DIM = 64
EPS = 1e-6
TILES = 3
VMEM_BYTES = 63 << 20


def up(value, unit):
    return -(-value // unit) * unit


class Place:
    def __init__(self, ndp, nz):
        self.ndp, self.nz, self.chips = ndp, nz, ndp // 2
        self.dp = lax.axis_index("dp")
        self.z = lax.axis_index("fsdp")
        self.core = lax.rem(self.dp, 2)
        self.chip = self.dp // 2
        self.square = self.chips == 4
        if self.square:
            a, b, c = self.chip // 2, lax.rem(self.chip, 2), self.core
            self.near = lax.rem(a + 1 - c, 2) * 2 + lax.rem(b + c, 2)
            self.side = lax.rem(a + c, 2) * 2 + lax.rem(b + 1 - c, 2)
            self.far = (1 - a) * 2 + (1 - b)
            self.mates = [self.near, self.side, self.far]
        else:
            self.mates = [lax.rem(self.chip + k, self.chips) for k in range(1, self.chips)]

    def at_chip(self, chip):
        return (chip * 2 + self.core, self.z)

    def sibling(self):
        return (self.chip * 2 + 1 - self.core, self.z)

    def at_z(self, k):
        return (self.dp, lax.rem(self.z + k, self.nz))

    def z_from(self, k):
        return lax.rem(self.z + self.nz - k, self.nz)

    def plane(self):
        return [self.sibling()] + [self.at_chip(m) for m in (self.mates[:2] if self.square else self.mates)]

    def greet(self):
        bar = pltpu.get_barrier_semaphore()
        there = self.plane() + [self.at_z(k) for k in range(1, self.nz)]
        for dev in there:
            pl.semaphore_signal(bar, inc=1, device_id=dev, device_id_type=MESH)
        pl.semaphore_wait(bar, len(there))


def remote(src, dst, send, recv, dev):
    return pltpu.make_async_remote_copy(
        src_ref=src, dst_ref=dst, send_sem=send, recv_sem=recv, device_id=dev, device_id_type=MESH
    )


class PlaneGather:
    def __init__(self, place, own, slot, send, recv):
        self.p = p = place
        mine = slot(p.dp)
        at = lambda m: slot(m * 2 + p.core)
        self.to_sib = remote(own, mine, send(0), recv(0), p.sibling())
        if p.square:
            self.first = [
                remote(own, mine, send(1), recv(1), p.at_chip(p.near)),
                remote(own, mine, send(2), recv(2), p.at_chip(p.side)),
            ]
            self.relay = remote(at(p.side), at(p.side), send(3), recv(3), p.at_chip(p.near))
            self.share = [
                remote(at(m), at(m), send(4 + i), recv(4 + i), p.sibling())
                for i, m in enumerate(p.mates)
            ]
        else:
            n = len(p.mates)
            self.first = [
                remote(own, mine, send(1 + i), recv(1 + i), p.at_chip(m)) for i, m in enumerate(p.mates)
            ]
            back = [lax.rem(p.chip + p.chips - k, p.chips) for k in range(1, p.chips)]
            self.share = [
                remote(at(m), at(m), send(1 + n + i), recv(1 + n + i), p.sibling())
                for i, m in enumerate(back)
            ]

    @staticmethod
    def sems(ndp):
        chips = ndp // 2
        return 7 if chips == 4 else 1 + 2 * (chips - 1)

    def start(self):
        for cp in self.first:
            cp.start()
        self.to_sib.start()

    def middle(self):
        if self.p.square:
            self.first[1].wait_recv()
            self.relay.start()
            self.share[1].start()
            self.first[0].wait_recv()
            self.share[0].start()
        else:
            for f, s in zip(self.first, self.share):
                f.wait_recv()
                s.start()

    def last(self):
        if self.p.square:
            self.relay.wait_recv()
            self.share[2].start()

    def arrive(self):
        self.to_sib.wait_recv()
        for s in self.share:
            s.wait_recv()

    def leave(self):
        for cp in [self.to_sib] + self.share + self.first + ([self.relay] if self.p.square else []):
            cp.wait_send()


class PlaneScatter:
    def __init__(self, place, part, sib, got, out, send, recv):
        self.p, self.part, self.sib, self.got, self.out = place, part, sib, got, out
        p = place
        self.pair = remote(part.at[:, 1 - p.core], sib, send(0), recv(0), p.sibling())
        at = lambda m: part.at[m, p.core]
        if p.square:
            self.first = [
                remote(at(p.far), got.at[0], send(1), recv(1), p.at_chip(p.near)),
                remote(at(p.near), got.at[1], send(2), recv(2), p.at_chip(p.near)),
            ]
            self.second = remote(at(p.side), got.at[2], send(3), recv(3), p.at_chip(p.side))
        else:
            self.first = [
                remote(at(m), got.at[i], send(1 + i), recv(1 + i), p.at_chip(m))
                for i, m in enumerate(p.mates)
            ]

    @staticmethod
    def sems(ndp):
        chips = ndp // 2
        return 4 if chips == 4 else chips

    def add(self, m, more):
        here = self.part.at[m, self.p.core]
        here[...] = (here[...].astype(f32) + more.astype(f32)).astype(here.dtype)

    def start(self):
        self.pair.start()

    def middle(self):
        p = self.p
        self.pair.wait_recv()
        if p.square:
            self.add(p.far, self.sib[p.far])
            self.first[0].start()
            self.add(p.near, self.sib[p.near])
            self.first[1].start()
            self.add(p.side, self.sib[p.side])
        else:
            for m, cp in zip(p.mates, self.first):
                self.add(m, self.sib[m])
                cp.start()

    def last(self):
        if self.p.square:
            self.first[0].wait_recv()
            self.add(self.p.side, self.got[0])
            self.second.start()

    def finish(self):
        p = self.p
        total = self.part[p.chip, p.core].astype(f32) + self.sib[p.chip].astype(f32)
        if p.square:
            self.first[1].wait_recv()
            total += self.got[1].astype(f32)
            self.second.wait_recv()
            total += self.got[2].astype(f32)
        else:
            for i, cp in enumerate(self.first):
                cp.wait_recv()
                total += self.got[i].astype(f32)
        self.out[...] = total
        for cp in [self.pair] + self.first + ([self.second] if p.square else []):
            cp.wait_send()


class Exchange:
    def __init__(self, p, src, dst, rows, send, recv):
        self.copies = [
            remote(src.at[dev[1], rows], dst.at[p.z, rows], send.at[k], recv.at[k], dev)
            for k, dev in ((k, p.at_z(k)) for k in range(1, p.nz))
        ]
        self.local = pltpu.make_async_copy(src.at[p.z, rows], dst.at[p.z, rows], send.at[0])

    def start(self):
        for cp in self.copies:
            cp.start()
        self.local.start()

    def wait(self):
        for cp in self.copies:
            cp.wait()
        self.local.wait()


def dot(a, b):
    return lax.dot_general(a, b, (((1,), (0,)), ((), ())), preferred_element_type=f32)


def dot_nt(a, b):
    return lax.dot_general(a, b, (((1,), (1,)), ((), ())), preferred_element_type=f32)


def dot_tn(a, b):
    return lax.dot_general(a, b, (((0,), (0,)), ((), ())), preferred_element_type=f32)


def norm_parts(rows):
    centred = rows - jnp.mean(rows, axis=-1, keepdims=True)
    inverse = lax.rsqrt(jnp.mean(centred * centred, axis=-1, keepdims=True) + EPS)
    return centred * inverse, inverse


def norm_back(grad, normed, inverse):
    first = jnp.mean(grad, axis=-1, keepdims=True)
    second = normed * jnp.mean(grad * normed, axis=-1, keepdims=True)
    return inverse * (grad - first - second)


def regroup(per, group, nz, block, j):
    row = lax.broadcasted_iota(jnp.int32, (per, nz * block), 0).astype(f32)
    col = lax.broadcasted_iota(jnp.int32, (per, nz * block), 1).astype(f32)
    plane = jnp.floor((row + 0.5) * (1.0 / group))
    return jnp.where(col == row + plane * (block - group) + j * group, 1.0, 0.0).astype(bf16)


def router_softmax(rows, wr, experts):
    lane = lax.broadcasted_iota(jnp.int32, (1, 128), 1)
    logits = jnp.where(lane < experts, dot(rows, wr), -1e30)
    ex = jnp.exp(logits - jnp.max(logits, axis=-1, keepdims=True))
    return ex / jnp.sum(ex, axis=-1, keepdims=True)


def padded(value, rows):
    return jnp.concatenate([value, jnp.zeros((rows - value.shape[0], value.shape[1]), value.dtype)], axis=0)


def layer_columns(wqkv_ref, wout_ref, lo, hi):
    wide = wqkv_ref.shape[1]
    parts = []
    if lo < wide:
        parts.append(wqkv_ref[:, lo : min(hi, wide)])
    if hi > wide:
        parts.append(wout_ref[:, max(lo, wide) - wide : hi - wide])
    return parts[0] if len(parts) == 1 else jnp.concatenate(parts, axis=1)


def route(info, place_ref, image, cap, slots, experts, seq):
    lanes = info.shape[1]
    row = lax.broadcasted_iota(jnp.int32, info.shape, 0)
    lane = lax.broadcasted_iota(jnp.int32, info.shape, 1)
    info = jnp.where(lane < seq, info, jnp.where(row == 0, 1e6, -1.0 - row.astype(f32)))
    cols = jnp.transpose(info)
    rank_c, one_c, two_c = cols[:, 0:1], cols[:, 1:2], cols[:, 2:3]
    rank_r, one_r, two_r = info[0:1, :], info[1:2, :], info[2:3, :]
    earlier = rank_c < rank_r
    count = lambda m: jnp.sum(jnp.where(m, 1.0, 0.0), axis=0, keepdims=True)
    pos_one = count(earlier & (one_c == one_r))
    pos_two = count(earlier & (two_c == two_r)) + count(one_c == two_r)
    code = lambda pos, pick: jnp.where(
        (pos < cap) & (pick >= 0), pick * slots + (pos + image * cap), -1.0
    ).astype(jnp.int32)
    code_one, code_two = code(pos_one, one_r), code(pos_two, two_r)
    for e in range(experts):
        slot = lax.broadcasted_iota(jnp.int32, (slots, lanes), 0) + e * slots
        hit = (slot == code_one) | (slot == code_two)
        place_ref[e * slots : (e + 1) * slots, image * lanes : (image + 1) * lanes] = jnp.where(
            hit, 1.0, 0.0
        ).astype(bf16)


def attend_kernel(
    ndp, nz, cap, experts, fold,
    img_ref, cot_ref, info_ref, small_ref, wqkv_ref, wout_ref, win_ref, wback_ref,
    wi_out, wb_out, wl_out, rtok_out, rdy_out, place_out, mixed_out, probs_out, att_out, res_out, sg_ref,
    zs_ref, zsm_ref, wl_ref, wt_ref, tok_ref, stok_ref, sdy_ref, x_ref,
    place_ref, mixed_ref, probs_ref, att_ref, res_ref,
    lsend, lrecv, zsend, zrecv, gsend, grecv, tsend, trecv, ysend, yrecv, osem,
):
    p = Place(ndp, nz)
    images, seq, d = img_ref.shape
    rows, lanes = x_ref.shape[1], info_ref.shape[2]
    slots = stok_ref.shape[1]
    pairs = d // 128
    group, per = wqkv_ref.shape[0], d // ndp
    width = wl_ref.shape[3]
    thin, block = width // fold, zs_ref.shape[2]
    chunk = width // ndp
    saves = []

    def save(src, dst):
        cp = pltpu.make_async_copy(src, dst, osem.at[len(saves)])
        cp.start()
        saves.append(cp)

    zsm_ref[p.z] = small_ref[...]
    for n in range(TILES):
        if block == fold * group:
            pieces = [
                layer_columns(wqkv_ref, wout_ref, n * width + j * thin, n * width + (j + 1) * thin).astype(f32)
                for j in range(fold)
            ]
            zs_ref[n, p.z] = jnp.concatenate(pieces, axis=0).astype(bf16)
        else:
            zs_ref[n, p.z] = jnp.zeros((block, thin), bf16)
            zs_ref[n, p.z, :group] = layer_columns(wqkv_ref, wout_ref, n * width, (n + 1) * width)
    p.greet()

    lines = []
    for n in range(TILES + 1):
        ref = zs_ref.at[n] if n < TILES else zsm_ref
        lines.append(
            [remote(ref.at[p.z], ref.at[p.z], zsend.at[n, k], zrecv.at[n, k], p.at_z(k)) for k in range(1, nz)]
        )
    for n in (TILES,) + tuple(range(TILES)):
        for cp in lines[n]:
            cp.start()

    layer_units = []
    for n in range(TILES + 1):
        full = wl_ref.at[n] if n < TILES else sg_ref
        layer_units.append(
            PlaneGather(
                p, full.at[p.dp], lambda dd, full=full: full.at[dd],
                lambda i, n=n: lsend.at[n, i], lambda i, n=n: lrecv.at[n, i],
            )
        )
    expert_units = []
    for t in range(TILES):
        for w, (own, full) in enumerate(((wt_ref, wi_out), (wback_ref, wb_out))):
            n = t * 2 + w
            expert_units.append(
                PlaneGather(
                    p, own.at[t], lambda dd, full=full, t=t: full.at[t, dd],
                    lambda i, n=n: gsend.at[n, i], lambda i, n=n: grecv.at[n, i],
                )
            )
    for t in range(TILES):
        for i in range(ndp):
            wt_ref[t, :, i * chunk : (i + 1) * chunk] = win_ref[
                :, (i * TILES + t) * chunk : (i * TILES + t + 1) * chunk
            ]

    tok_ref[...] = jnp.zeros_like(tok_ref)
    for i in range(images):
        route(info_ref[i], place_ref, i, cap, slots, experts, seq)
        tok_ref[i * lanes : i * lanes + rows, :] = padded(cot_ref[i].astype(f32), rows).astype(bf16)

    cuts = [i * cap // 16 * 16 for i in range(images)] + [slots]

    def dispatch(out_ref, lo, hi, upto):
        for e in range(experts):
            out_ref[e, lo:hi, :] = dot(
                place_ref[e * slots + lo : e * slots + hi, :upto], tok_ref[:upto, :]
            ).astype(bf16)

    dispatch(sdy_ref, 0, slots, images * lanes)
    send_dy = Exchange(p, sdy_ref, rdy_out, pl.ds(0, slots), ysend, yrecv)
    send_dy.start()
    save(place_ref, place_out)

    def line_done(n):
        for cp in lines[n]:
            cp.wait_recv()
        if n == TILES:
            tall = zsm_ref.shape[1]
            sg_ref[p.dp] = dot(regroup(per, group, nz, tall, 0), zsm_ref[...].reshape(nz * tall, 128)).astype(bf16)
        else:
            flat = zs_ref[n].reshape(nz * block, thin)
            for j in range(fold):
                wl_ref[n, p.dp, :, j * thin : (j + 1) * thin] = dot(
                    regroup(per, group, nz, block, j), flat
                ).astype(bf16)
        layer_units[n].start()

    order = (TILES,) + tuple(range(TILES))
    for i, n in enumerate(order):
        line_done(n)
        if i >= 1:
            layer_units[order[i - 1]].middle()
        if i >= 2:
            layer_units[order[i - 2]].last()
    layer_units[order[-1]].middle()
    layer_units[order[-2]].last()
    layer_units[order[-1]].last()
    for t in range(TILES):
        for w, (own, full) in enumerate(((wt_ref, wi_out), (wback_ref, wb_out))):
            expert_units[t * 2 + w].start()
            save(own.at[t], full.at[t, p.dp])

    layer_units[TILES].arrive()
    gains = jnp.transpose(sg_ref[...].reshape(d, 128).astype(f32))
    gain_one, gain_two = gains[experts : experts + 1, :], gains[experts + 1 : experts + 2, :]
    normed = []
    for i in range(images):
        x_ref[i] = padded(img_ref[i].astype(f32), rows)
        normed.append((norm_parts(x_ref[i])[0] * gain_one).astype(bf16))
        mixed_ref[i, rows:, :] = jnp.zeros((lanes - rows, 3 * d), bf16)
    first = jnp.concatenate(normed, axis=0)
    for n in range(TILES):
        layer_units[n].arrive()
        save(wl_ref.at[n], wl_out.at[n])
        cols = min((n + 1) * width, 3 * d) - n * width
        got = dot(first, wl_ref[n].reshape(d, width)[:, :cols]).astype(bf16)
        mixed_ref[:, :rows, n * width : n * width + cols] = got.reshape(images, rows, cols)

    low_half = lax.broadcasted_iota(jnp.int32, (1, 128), 1) < HEAD_DIM
    valid = lax.broadcasted_iota(jnp.int32, (1, lanes), 1) < seq
    save(mixed_ref, mixed_out)

    sends = []
    for i in range(images):

        @pl.loop(0, pairs // 2)
        def _(m):
            for u in range(2):
                n = m * 2 + u
                at = lambda part: pl.ds(pl.multiple_of(part * d + n * 128, 128), 128)
                q, k, v = mixed_ref[i, :rows, at(0)], mixed_ref[i, :, at(1)], mixed_ref[i, :, at(2)]
                got = []
                for h in range(2):
                    mask = low_half if h == 0 else ~low_half
                    scores = dot_nt(jnp.where(mask, q, jnp.zeros_like(q)), k) * HEAD_DIM**-0.5
                    scores = jnp.where(valid, scores, -1e30)
                    e = jnp.exp(scores - jnp.max(scores, axis=-1, keepdims=True))
                    prob = (e * (1.0 / jnp.sum(e, axis=-1, keepdims=True))).astype(bf16)
                    probs_ref[i, n * 2 + h] = prob
                    got.append(dot(prob, v))
                att_ref[i, :, at(0)] = jnp.where(low_half, got[0], got[1]).astype(bf16)

        wout = wl_ref[TILES - 1].reshape(d, width)[:, width - d :]
        residual = x_ref[i] + dot(att_ref[i], wout)
        res_ref[i] = residual
        tok_ref[i * lanes : i * lanes + rows, :] = (norm_parts(residual)[0] * gain_two).astype(bf16)
        dispatch(stok_ref, cuts[i], cuts[i + 1], (i + 1) * lanes)
        ex = Exchange(
            p, stok_ref, rtok_out, pl.ds(cuts[i], cuts[i + 1] - cuts[i]), tsend.at[i], trecv.at[i]
        )
        ex.start()
        sends.append(ex)
        save(probs_ref.at[i], probs_out.at[i])
        save(att_ref.at[i], att_out.at[i])
        save(res_ref.at[i], res_out.at[i])

    for u in expert_units:
        u.middle()
    for u in expert_units:
        u.last()
    for u in expert_units:
        u.arrive()
        u.leave()
    for u in layer_units:
        u.leave()
    for n in range(TILES + 1):
        for cp in lines[n]:
            cp.wait_send()
    send_dy.wait()
    for ex in sends:
        ex.wait()
    for cp in saves:
        cp.wait()


def attend(ndp, nz, cap, slots, experts, images, cotangent, info, small, wqkv, wout, win, wback):
    count, seq, d = images.shape
    rows, lanes = up(seq, 16), info.shape[2]
    group, per, width = wqkv.shape[0], d // ndp, 4 * d // TILES
    fold = 16 // math.gcd(group, 16)
    if width // fold % 128:
        fold = 1
    block = fold * group if fold * group % 16 == 0 else up(group, 16)
    shape, dma, vm = jax.ShapeDtypeStruct, pltpu.SemaphoreType.DMA, pltpu.VMEM
    ns = PlaneGather.sems(ndp)
    heads = d // HEAD_DIM
    return pl.pallas_call(
        partial(attend_kernel, ndp, nz, cap, experts, fold),
        out_shape=(
            shape((TILES, ndp, per, width), bf16),
            shape((TILES, ndp) + wback.shape[1:], bf16),
            shape((TILES, ndp, per, width), bf16),
            shape((nz, slots, d), bf16),
            shape((nz, slots, d), bf16),
            shape((experts * slots, count * lanes), bf16),
            shape((count, lanes, 3 * d), bf16),
            shape((count, heads, rows, lanes), bf16),
            shape((count, rows, d), bf16),
            shape((count, rows, d), f32),
            shape((ndp, per, 128), bf16),
        ),
        in_specs=[VM] * 8,
        out_specs=(ANY,) * 10 + (VM,),
        scratch_shapes=[
            vm((TILES, nz, block, width // fold), bf16),
            vm((nz,) + small.shape, bf16),
            vm((TILES, ndp, per, width), bf16),
            vm((TILES, per, width), bf16),
            vm((count * lanes, d), bf16),
            vm((experts, slots, d), bf16),
            vm((experts, slots, d), bf16),
            vm((count, rows, d), f32),
            vm((experts * slots, count * lanes), bf16),
            vm((count, lanes, 3 * d), bf16),
            vm((count, heads, rows, lanes), bf16),
            vm((count, rows, d), bf16),
            vm((count, rows, d), f32),
            dma((TILES + 1, ns)), dma((TILES + 1, ns)),
            dma((TILES + 1, nz)), dma((TILES + 1, nz)),
            dma((2 * TILES, ns)), dma((2 * TILES, ns)),
            dma((count, nz)), dma((count, nz)),
            dma((nz,)), dma((nz,)),
            dma((3 * TILES + 2 + 3 * count,)),
        ],
        compiler_params=pltpu.CompilerParams(
            collective_id=0, has_side_effects=True, vmem_limit_bytes=VMEM_BYTES
        ),
        name="attend",
    )(images, cotangent, info, small, wqkv, wout, win, wback)


class LineScatter:
    def __init__(self, place, fold, sent, got, send, recv):
        self.p, self.fold, self.sent, self.got = place, fold, sent, got
        self.copies = []
        for k in range(1, place.nz):
            dev = place.at_z(k)
            self.copies.append(remote(sent.at[dev[1]], got.at[place.z], send.at[k], recv.at[k], dev))

    def start(self, total, group):
        per, thin = total.shape[0], total.shape[1] // self.fold
        nz, block = self.sent.shape[0], self.sent.shape[1]
        low = total.astype(bf16)
        acc = None
        for j in range(self.fold):
            more = dot_tn(regroup(per, group, nz, block, j), low[:, j * thin : (j + 1) * thin])
            acc = more if acc is None else acc + more
        self.sent[...] = acc.astype(bf16).reshape(self.sent.shape)
        for cp in self.copies:
            cp.start()

    def finish(self, group):
        p = self.p
        for cp in self.copies:
            cp.wait()
        total = self.sent[p.z].astype(f32)
        for k in range(1, p.nz):
            total += self.got[p.z_from(k)].astype(f32)
        return jnp.concatenate([total[j * group : (j + 1) * group] for j in range(self.fold)], axis=1)


def expert_rows(p, experts, nz, wi_ref, wb_ref, buf_ref, dy_ref, wr, gs_ref, act_ref, gh_ref, rp_ref, loads):
    slots, d = buf_ref.shape[1], buf_ref.shape[2]
    rows = nz * slots
    width = wi_ref.shape[3]
    lane = lax.broadcasted_iota(jnp.int32, (1, 128), 1)
    buf = buf_ref[...].reshape(rows, d)
    rp = router_softmax(buf, wr, experts)
    rp_ref[...] = rp
    gate = jnp.sum(jnp.where(lane == p.z, rp, 0.0), axis=-1, keepdims=True)
    gs_ref[...] = (gate * dy_ref[...].reshape(rows, d).astype(f32)).astype(bf16)
    step = min(256, width)
    k0, k1 = 0.7978845608028654, 0.044715 * 0.7978845608028654
    for t in range(TILES):
        loads(t)
        wi = wi_ref[t].reshape(d, width)
        wb = wb_ref[t].reshape(width, d)
        for n in range(width // step):
            lo, hi = n * step, (n + 1) * step
            h = dot(buf_ref[...].reshape(rows, d), wi[:, lo:hi])
            grad = dot_nt(gs_ref[...], wb[lo:hi])
            h2 = h * h
            th = jnp.tanh(h * (k0 + k1 * h2))
            half = 0.5 * (1.0 + th)
            act_ref[t, :, lo:hi] = (h * half).astype(bf16)
            slope = half + 0.5 * h * (1.0 - th * th) * (k0 + 3.0 * k1 * h2)
            gh_ref[t, :, lo:hi] = (grad * slope).astype(bf16)


def learn_kernel(
    ndp, nz, experts, fold, rows,
    wi_in, wb_in, wl_in, rtok_in, rdy_in, place_in, mixed_in, probs_in, att_in, res_in,
    sg_ref, img_ref, cot_ref,
    out_ref, gin_ref, gl_ref, gsm_ref, gi_ref, gb_ref,
    pin_ref, pback_ref, sin_ref, sback_ref, xin_ref, xback_ref, sgrad_ref, rgrad_ref, eo_ref, ro_ref,
    tot_ref, gr_ref, psm_ref, ssm_ref, xsm_ref, tsm_ref, zsent_ref, zgot_ref, zssm_ref, zgsm_ref, vec_ref,
    esend, erecv, lsend, lrecv, zsend, zrecv, rsend, rrecv, osend, orecv, free, isem,
):
    p = Place(ndp, nz)
    images, seq, d = img_ref.shape
    slots = rtok_in.shape[1]
    lanes = mixed_in.shape[1]
    per, width = wi_in.shape[2], wi_in.shape[3]
    per_back = wb_in.shape[2]
    chips = ndp // 2
    pairs = d // 128
    group = per // nz
    p.greet()
    lane = lax.broadcasted_iota(jnp.int32, (1, 128), 1)
    wr = sg_ref[...].reshape(d, 128)

    experts_sums = []
    for t in range(TILES):
        for w, (part, sib, got, out) in enumerate(
            ((pin_ref, sin_ref, xin_ref, gi_ref), (pback_ref, sback_ref, xback_ref, gb_ref))
        ):
            n = t * 2 + w
            experts_sums.append(
                PlaneScatter(
                    p, part.at[t], sib.at[t], got.at[t], out.at[t],
                    lambda i, n=n: esend.at[n, i], lambda i, n=n: erecv.at[n, i],
                )
            )
    both = lambda t: experts_sums[2 * t : 2 * t + 2]
    back = Exchange(p, sgrad_ref, rgrad_ref, pl.ds(0, slots), rsend, rrecv)
    outs = Exchange(p, eo_ref, ro_ref, pl.ds(0, slots), osend, orecv)

    def expert_part(wi_ref, wb_ref, buf_ref, dy_ref, gs_ref, act_ref, gh_ref, rp_ref):
        copies = [
            pltpu.make_async_copy(rtok_in, buf_ref, isem.at[0]),
            pltpu.make_async_copy(rdy_in, dy_ref, isem.at[1]),
        ]
        for t in range(TILES):
            copies.append(pltpu.make_async_copy(wi_in.at[t], wi_ref.at[t], isem.at[2 + 2 * t]))
            copies.append(pltpu.make_async_copy(wb_in.at[t], wb_ref.at[t], isem.at[3 + 2 * t]))
        for cp in copies:
            cp.start()
        copies[0].wait()
        copies[1].wait()

        def loads(t):
            copies[2 + 2 * t].wait()
            copies[3 + 2 * t].wait()

        expert_rows(p, experts, nz, wi_ref, wb_ref, buf_ref, dy_ref, wr, gs_ref, act_ref, gh_ref, rp_ref, loads)

        gr_ref[...] = jnp.zeros_like(gr_ref)
        some = max(nz // 2, 1)
        count = some * slots
        mine = jnp.where(lane == p.z, 1.0, 0.0)
        for q in range(nz // some):
            lo, hi = q * count, (q + 1) * count
            out = sum(dot(act_ref[t, lo:hi, :], wb_ref[t].reshape(width, d)) for t in range(TILES)).astype(bf16)
            eo_ref[q * some : (q + 1) * some] = out.reshape(some, slots, d)
            rp = rp_ref[lo:hi, :]
            gate = jnp.sum(mine * rp, axis=-1, keepdims=True)
            rows_dy = dy_ref[q * some : (q + 1) * some].reshape(count, d).astype(f32)
            ggate = jnp.sum(out.astype(f32) * rows_dy, axis=-1, keepdims=True)
            contrib = (ggate * gate) * (mine - rp)
            top = contrib.astype(bf16)
            low = (contrib - top.astype(f32)).astype(bf16)
            grad = sum(dot_nt(gh_ref[t, lo:hi, :], wi_ref[t].reshape(d, width)) for t in range(TILES))
            grad = grad + dot_nt(top, wr) + dot_nt(low, wr)
            sgrad_ref[q * some : (q + 1) * some] = grad.astype(bf16).reshape(some, slots, d)
            rows_buf = buf_ref[q * some : (q + 1) * some].reshape(count, d)
            gr_ref[...] += dot_tn(rows_buf, top) + dot_tn(rows_buf, low)
        back.start()

        buf = buf_ref[...].reshape(nz * slots, d)
        for t in range(TILES):
            pin_ref[t] = dot_tn(buf, gh_ref[t]).astype(bf16).reshape(chips, 2, per, width)
            both(t)[0].start()
            pback_ref[t] = dot_tn(act_ref[t], gs_ref[...]).astype(bf16).reshape(chips, 2, per_back, d)
            both(t)[1].start()
            if t >= 1:
                for u in both(t - 1):
                    u.middle()
            if t >= 2:
                for u in both(t - 2):
                    u.last()

    shared = nz * slots
    pl.run_scoped(
        expert_part,
        pltpu.VMEM((TILES, ndp, per, width), bf16),
        pltpu.VMEM((TILES, ndp, per_back, d), bf16),
        pltpu.VMEM((nz, slots, d), bf16),
        pltpu.VMEM((nz, slots, d), bf16),
        pltpu.VMEM((shared, d), bf16),
        pltpu.VMEM((TILES, shared, width), bf16),
        pltpu.VMEM((TILES, shared, width), bf16),
        pltpu.VMEM((shared, 128), f32),
    )

    layer_sums, lines = [], []
    for n in range(TILES + 1):
        part, sib, got, tot, zs, zg = (
            (pin_ref.at[n], sin_ref.at[n], xin_ref.at[n], tot_ref.at[n], zsent_ref.at[n], zgot_ref.at[n])
            if n < TILES
            else (psm_ref, ssm_ref, xsm_ref, tsm_ref, zssm_ref, zgsm_ref)
        )
        layer_sums.append(
            PlaneScatter(p, part, sib, got, tot, lambda i, n=n: lsend.at[n, i], lambda i, n=n: lrecv.at[n, i])
        )
        lines.append(LineScatter(p, fold if n < TILES else 1, zs, zg, zsend.at[n], zrecv.at[n]))

    def attend_part(
        wl_ref, place_ref, mixed_ref, probs_ref, att_ref, res_ref,
        gres_ref, branch_ref, gatt_ref, gmix_ref, first_ref,
    ):
        copies = [
            pltpu.make_async_copy(src, dst, isem.at[n])
            for n, (src, dst) in enumerate(
                (
                    (place_in, place_ref), (res_in, res_ref), (wl_in, wl_ref), (att_in, att_ref),
                    (mixed_in, mixed_ref), (probs_in, probs_ref),
                )
            )
        ]
        for cp in copies:
            cp.start()
        for u in both(TILES - 2):
            u.last()
        for u in both(TILES - 1):
            u.middle()
        gains = jnp.transpose(wr.astype(f32))
        gain_one, gain_two = gains[experts : experts + 1, :], gains[experts + 1 : experts + 2, :]
        normed_one = lambda i: norm_parts(padded(img_ref[i].astype(f32), rows))
        for i in range(images):
            first_ref[i] = (normed_one(i)[0] * gain_one).astype(bf16)
        for cp in copies:
            cp.wait()
        wout = wl_ref[TILES - 1].reshape(d, width)[:, width - d :]
        back.wait()
        outs.start()
        vec_two = jnp.zeros((1, d), f32)
        for i in range(images):
            hits = place_ref[:, i * lanes : (i + 1) * lanes]
            grad_second = dot_tn(hits, rgrad_ref[...].reshape(experts * slots, d))[:rows]
            normed, inverse = norm_parts(res_ref[i])
            vec_two += jnp.sum(grad_second * normed, axis=0, keepdims=True)
            grad = padded(cot_ref[i].astype(f32), rows) + norm_back(grad_second * gain_two, normed, inverse)
            gres_ref[i] = grad
            branch = grad.astype(bf16)
            branch_ref[i] = branch
            gatt_ref[i] = dot_nt(branch, wout).astype(bf16)
        for u in both(TILES - 1):
            u.last()

        low_half = lax.broadcasted_iota(jnp.int32, (1, 128), 1) < HEAD_DIM
        scale = HEAD_DIM**-0.5

        @pl.loop(0, pairs)
        def _(n):
            at = lambda part: pl.ds(pl.multiple_of(part * d + n * 128, 128), 128)
            for i in range(images):
                q, k, v = mixed_ref[i, :rows, at(0)], mixed_ref[i, :, at(1)], mixed_ref[i, :, at(2)]
                ga = gatt_ref[i, :, at(0)]
                gq, gk, gv = [], [], []
                for h in range(2):
                    mask = low_half if h == 0 else ~low_half
                    prob = probs_ref[i, n * 2 + h]
                    gv.append(dot_tn(prob, ga)[:rows])
                    weighting = dot_nt(jnp.where(mask, ga, jnp.zeros_like(ga)), v)
                    wide = prob.astype(f32)
                    scores = wide * (weighting - jnp.sum(wide * weighting, axis=-1, keepdims=True))
                    scores = scores.astype(bf16)
                    gq.append(dot(scores, k))
                    gk.append(dot_tn(scores, q)[:rows])
                pick = lambda pair, by: jnp.where(low_half, pair[0], pair[1]) * by
                gmix_ref[i, :, at(0)] = pick(gq, scale).astype(bf16)
                gmix_ref[i, :, at(1)] = pick(gk, scale).astype(bf16)
                gmix_ref[i, :, at(2)] = pick(gv, 1.0).astype(bf16)

        for u in experts_sums:
            u.finish()
        for dev in p.plane():
            pl.semaphore_signal(free, inc=1, device_id=dev, device_id_type=MESH)
        pl.semaphore_wait(free, len(p.plane()))

        flat = lambda v: v.reshape(images * rows, v.shape[-1])
        for n in range(TILES):
            cols = min((n + 1) * width, 3 * d) - n * width
            got = dot_tn(flat(first_ref[...]), flat(gmix_ref[:, :, n * width : n * width + cols]))
            got = got.astype(bf16).reshape(chips, 2, per, cols)
            if cols == width:
                pin_ref[n] = got
            else:
                pin_ref[n, :, :, :, :cols] = got
                more = dot_tn(flat(att_ref[...]), flat(branch_ref[...]))
                pin_ref[n, :, :, :, cols:] = more.astype(bf16).reshape(chips, 2, per, d)
            layer_sums[n].start()
            if n >= 1:
                layer_sums[n - 1].middle()

        vec_one = jnp.zeros((1, d), f32)
        for i in range(images):
            grad_first = None
            for n in range(TILES):
                cols = min((n + 1) * width, 3 * d) - n * width
                more = dot_nt(gmix_ref[i, :, n * width : n * width + cols], wl_ref[n].reshape(d, width)[:, :cols])
                grad_first = more if grad_first is None else grad_first + more
            normed, inverse = normed_one(i)
            vec_one += jnp.sum(grad_first * normed, axis=0, keepdims=True)
            gin_ref[i] = (gres_ref[i] + norm_back(grad_first * gain_one, normed, inverse))[:seq]
            if i == 0:
                layer_sums[TILES - 1].middle()
                for n in range(TILES - 1):
                    layer_sums[n].last()

        vec_ref[0:1, :] = vec_one
        vec_ref[1:2, :] = vec_two
        cols = jnp.transpose(vec_ref[...])
        small = jnp.where(
            lane == experts, cols[:, 0:1], jnp.where(lane == experts + 1, cols[:, 1:2], gr_ref[...])
        )
        psm_ref[...] = small.reshape(chips, 2, per, 128)
        layer_sums[TILES].start()
        layer_sums[TILES - 1].last()
        layer_sums[TILES].middle()
        outs.wait()

        def output(i):
            second = (norm_parts(res_ref[i])[0] * gain_two).astype(bf16)
            rp = router_softmax(second, wr, experts)
            total = res_ref[i]
            for e in range(experts):
                hits = place_ref[e * slots : (e + 1) * slots, i * lanes : (i + 1) * lanes]
                gate = jnp.sum(jnp.where(lane == e, rp, 0.0), axis=-1, keepdims=True)
                total = total + gate * dot_tn(hits, ro_ref[e])[:rows]
            out_ref[i] = total.astype(bf16)[:seq]

        def to_line(n):
            layer_sums[n].finish()
            ref = tot_ref.at[n] if n < TILES else tsm_ref
            if n < TILES:
                lines[n].start(ref[...], group)
            else:
                for k in range(nz):
                    zssm_ref[k, :group, :] = tsm_ref[k * group : (k + 1) * group, :]
                for cp in lines[n].copies:
                    cp.start()

        output(0)
        to_line(0)
        for i in range(1, images):
            output(i)
        layer_sums[TILES].last()
        for n in range(1, TILES + 1):
            to_line(n)
        for n in range(TILES):
            gl_ref[:, n * width : (n + 1) * width] = lines[n].finish(group)[:group]
        gsm_ref[...] = lines[TILES].finish(zssm_ref.shape[1])[:group]

    pl.run_scoped(
        attend_part,
        pltpu.VMEM((TILES, ndp, per, width), bf16),
        pltpu.VMEM(place_in.shape, bf16),
        pltpu.VMEM(mixed_in.shape, bf16),
        pltpu.VMEM(probs_in.shape, bf16),
        pltpu.VMEM((images, rows, d), bf16),
        pltpu.VMEM((images, rows, d), f32),
        pltpu.VMEM((images, rows, d), f32),
        pltpu.VMEM((images, rows, d), bf16),
        pltpu.VMEM((images, rows, d), bf16),
        pltpu.VMEM((images, rows, 3 * d), bf16),
        pltpu.VMEM((images, rows, d), bf16),
    )


def learn(ndp, nz, experts, front, images, cotangent):
    wi, wb, wl, rtok, rdy, place, mixed, probs, att, res, sg = front
    count, seq, d = images.shape
    rows = res.shape[1]
    per, width, per_back = wi.shape[2], wi.shape[3], wb.shape[2]
    chips, group = ndp // 2, per // nz
    fold = 16 // math.gcd(group, 16)
    if width // fold % 128:
        fold = 1
    block = fold * group if fold * group % 16 == 0 else up(group, 16)
    short = up(group, 8)
    nb = ndp // 2 - 1
    slots = rtok.shape[1]
    shape, dma, vm = jax.ShapeDtypeStruct, pltpu.SemaphoreType.DMA, pltpu.VMEM
    ns = PlaneScatter.sems(ndp)
    return pl.pallas_call(
        partial(learn_kernel, ndp, nz, experts, fold, rows),
        out_shape=(
            shape((count, seq, d), bf16),
            shape((count, seq, d), f32),
            shape((group, 4 * d), f32),
            shape((group, 128), f32),
            shape((TILES, per, width), f32),
            shape((TILES, per_back, d), f32),
        ),
        in_specs=[ANY] * 10 + [VM] * 3,
        out_specs=(VM,) * 6,
        scratch_shapes=[
            vm((TILES, chips, 2, per, width), bf16),
            vm((TILES, chips, 2, per_back, d), bf16),
            vm((TILES, chips, per, width), bf16),
            vm((TILES, chips, per_back, d), bf16),
            vm((TILES, nb, per, width), bf16),
            vm((TILES, nb, per_back, d), bf16),
            vm((nz, slots, d), bf16),
            vm((nz, slots, d), bf16),
            vm((nz, slots, d), bf16),
            vm((nz, slots, d), bf16),
            vm((TILES, per, width), f32),
            vm((d, 128), f32),
            vm((chips, 2, per, 128), f32),
            vm((chips, per, 128), f32),
            vm((nb, per, 128), f32),
            vm((per, 128), f32),
            vm((TILES, nz, block, width // fold), bf16),
            vm((TILES, nz, block, width // fold), bf16),
            vm((nz, short, 128), f32),
            vm((nz, short, 128), f32),
            vm((8, d), f32),
            dma((2 * TILES, ns)), dma((2 * TILES, ns)),
            dma((TILES + 1, ns)), dma((TILES + 1, ns)),
            dma((TILES + 1, nz)), dma((TILES + 1, nz)),
            dma((nz,)), dma((nz,)),
            dma((nz,)), dma((nz,)),
            pltpu.SemaphoreType.REGULAR,
            dma((2 + 2 * TILES,)),
        ],
        compiler_params=pltpu.CompilerParams(
            collective_id=1, has_side_effects=True, vmem_limit_bytes=VMEM_BYTES
        ),
        name="learn",
    )(wi, wb, wl, rtok, rdy, place, mixed, probs, att, res, sg, images, cotangent)


def per_device(ndp, nz, images, gain_one, w_qkv, w_out, gain_two, w_router, w_in, w_back, choices, priority, cotangent):
    count, seq, d = images.shape
    group, experts = w_router.shape
    ff = w_in.shape[2]
    cap = (42 * seq + 20 * experts - 1) // (20 * experts)
    slots, lanes = up(count * cap, 16), up(seq, 128)
    chunk = ff // ndp // TILES
    small = jnp.concatenate([w_router, gain_one[:, None], gain_two[:, None]], axis=1)
    small = jnp.pad(small, ((0, up(group, 16) - group), (0, 128 - small.shape[1])))
    info = jnp.concatenate([priority[:, None, :], choices.transpose(0, 2, 1)], axis=1).astype(f32)
    info = jnp.pad(info, ((0, 0), (0, 5), (0, lanes - seq)))
    front = attend(
        ndp, nz, cap, slots, experts, images, cotangent, info, small,
        w_qkv, w_out, w_in[0], w_back[0].reshape(TILES, chunk, d),
    )
    out, gin, gl, gsm, gi, gb = learn(ndp, nz, experts, front, images, cotangent)
    grad_in = gi.reshape(TILES, d // ndp, ndp, chunk).transpose(1, 2, 0, 3).reshape(1, d // ndp, ff)
    return (
        out, gin, gsm[:, experts], gl[:, : 3 * d], gl[:, 3 * d :], gsm[:, experts + 1], gsm[:, :experts],
        grad_in, gb.reshape(1, ff // ndp, d),
    )


def solution(mesh):
    ndp, nz = mesh.shape["dp"], mesh.shape["fsdp"]
    both = ("dp", "fsdp")
    tokens, rows, expert_rows = P(both, None, None), P(both, None), P("fsdp", "dp", None)
    return jax.shard_map(
        partial(per_device, ndp, nz),
        mesh=mesh,
        in_specs=(tokens, P(both), rows, rows, P(both), rows, expert_rows, expert_rows, tokens, rows, tokens),
        out_specs=(tokens, tokens, P(both), rows, rows, P(both), rows, expert_rows, expert_rows),
        check_vma=False,
    )
```

```python
import math
from functools import partial

import jax
import jax.numpy as jnp
from jax import lax
from jax.experimental import pallas as pl
from jax.experimental.pallas import tpu as pltpu
from jax.sharding import PartitionSpec as P

f32, bf16 = jnp.float32, jnp.bfloat16
MESH = pl.DeviceIdType.MESH
ANY = pl.BlockSpec(memory_space=pl.ANY)
VM = pl.BlockSpec(memory_space=pltpu.VMEM)
HEAD_DIM = 64
EPS = 1e-6
TILES = 3
VMEM_BYTES = 63 << 20


def up(value, unit):
    return -(-value // unit) * unit


class Place:
    def __init__(self, ndp, nz):
        self.ndp, self.nz, self.chips = ndp, nz, ndp // 2
        self.dp = lax.axis_index("dp")
        self.z = lax.axis_index("fsdp")
        self.core = lax.rem(self.dp, 2)
        self.chip = self.dp // 2
        self.square = self.chips == 4
        if self.square:
            a, b, c = self.chip // 2, lax.rem(self.chip, 2), self.core
            self.near = lax.rem(a + 1 - c, 2) * 2 + lax.rem(b + c, 2)
            self.side = lax.rem(a + c, 2) * 2 + lax.rem(b + 1 - c, 2)
            self.far = (1 - a) * 2 + (1 - b)
            self.mates = [self.near, self.side, self.far]
        else:
            self.mates = [lax.rem(self.chip + k, self.chips) for k in range(1, self.chips)]

    def at_chip(self, chip):
        return (chip * 2 + self.core, self.z)

    def sibling(self):
        return (self.chip * 2 + 1 - self.core, self.z)

    def at_z(self, k):
        return (self.dp, lax.rem(self.z + k, self.nz))

    def z_from(self, k):
        return lax.rem(self.z + self.nz - k, self.nz)

    def plane(self):
        return [self.sibling()] + [self.at_chip(m) for m in (self.mates[:2] if self.square else self.mates)]

    def greet(self):
        bar = pltpu.get_barrier_semaphore()
        there = self.plane() + [self.at_z(k) for k in range(1, self.nz)]
        for dev in there:
            pl.semaphore_signal(bar, inc=1, device_id=dev, device_id_type=MESH)
        pl.semaphore_wait(bar, len(there))


def remote(src, dst, send, recv, dev):
    return pltpu.make_async_remote_copy(
        src_ref=src, dst_ref=dst, send_sem=send, recv_sem=recv, device_id=dev, device_id_type=MESH
    )


class PlaneGather:
    def __init__(self, place, own, slot, send, recv):
        self.p = p = place
        mine = slot(p.dp)
        at = lambda m: slot(m * 2 + p.core)
        self.to_sib = remote(own, mine, send(0), recv(0), p.sibling())
        if p.square:
            self.first = [
                remote(own, mine, send(1), recv(1), p.at_chip(p.near)),
                remote(own, mine, send(2), recv(2), p.at_chip(p.side)),
            ]
            self.relay = remote(at(p.side), at(p.side), send(3), recv(3), p.at_chip(p.near))
            self.share = [
                remote(at(m), at(m), send(4 + i), recv(4 + i), p.sibling())
                for i, m in enumerate(p.mates)
            ]
        else:
            n = len(p.mates)
            self.first = [
                remote(own, mine, send(1 + i), recv(1 + i), p.at_chip(m)) for i, m in enumerate(p.mates)
            ]
            back = [lax.rem(p.chip + p.chips - k, p.chips) for k in range(1, p.chips)]
            self.share = [
                remote(at(m), at(m), send(1 + n + i), recv(1 + n + i), p.sibling())
                for i, m in enumerate(back)
            ]

    @staticmethod
    def sems(ndp):
        chips = ndp // 2
        return 7 if chips == 4 else 1 + 2 * (chips - 1)

    def start(self):
        for cp in self.first:
            cp.start()
        self.to_sib.start()

    def middle(self):
        if self.p.square:
            self.first[1].wait_recv()
            self.relay.start()
            self.share[1].start()
            self.first[0].wait_recv()
            self.share[0].start()
        else:
            for f, s in zip(self.first, self.share):
                f.wait_recv()
                s.start()

    def last(self):
        if self.p.square:
            self.relay.wait_recv()
            self.share[2].start()

    def arrive(self):
        self.to_sib.wait_recv()
        for s in self.share:
            s.wait_recv()

    def leave(self):
        for cp in [self.to_sib] + self.share + self.first + ([self.relay] if self.p.square else []):
            cp.wait_send()


class PlaneScatter:
    def __init__(self, place, part, sib, got, out, send, recv):
        self.p, self.part, self.sib, self.got, self.out = place, part, sib, got, out
        p = place
        self.pair = remote(part.at[:, 1 - p.core], sib, send(0), recv(0), p.sibling())
        at = lambda m: part.at[m, p.core]
        if p.square:
            self.first = [
                remote(at(p.far), got.at[0], send(1), recv(1), p.at_chip(p.near)),
                remote(at(p.near), got.at[1], send(2), recv(2), p.at_chip(p.near)),
            ]
            self.second = remote(at(p.side), got.at[2], send(3), recv(3), p.at_chip(p.side))
        else:
            self.first = [
                remote(at(m), got.at[i], send(1 + i), recv(1 + i), p.at_chip(m))
                for i, m in enumerate(p.mates)
            ]

    @staticmethod
    def sems(ndp):
        chips = ndp // 2
        return 4 if chips == 4 else chips

    def add(self, m, more):
        here = self.part.at[m, self.p.core]
        here[...] = (here[...].astype(f32) + more.astype(f32)).astype(here.dtype)

    def start(self):
        self.pair.start()

    @staticmethod
    def middle(*units):
        p = units[0].p
        for u in units:
            u.pair.wait_recv()
        if p.square:
            for n, m in enumerate((p.far, p.near)):
                for u in units:
                    u.add(m, u.sib[m])
                    u.first[n].start()
            for u in units:
                u.add(p.side, u.sib[p.side])
        else:
            for n, m in enumerate(p.mates):
                for u in units:
                    u.add(m, u.sib[m])
                    u.first[n].start()

    @staticmethod
    def last(*units):
        p = units[0].p
        if p.square:
            for u in units:
                u.first[0].wait_recv()
                u.add(p.side, u.got[0])
                u.second.start()

    def finish(self):
        p = self.p
        total = self.part[p.chip, p.core].astype(f32) + self.sib[p.chip].astype(f32)
        if p.square:
            self.first[1].wait_recv()
            total += self.got[1].astype(f32)
            self.second.wait_recv()
            total += self.got[2].astype(f32)
        else:
            for i, cp in enumerate(self.first):
                cp.wait_recv()
                total += self.got[i].astype(f32)
        self.out[...] = total
        for cp in [self.pair] + self.first + ([self.second] if p.square else []):
            cp.wait_send()


class Exchange:
    def __init__(self, p, src, dst, rows, send, recv):
        self.copies = [
            remote(src.at[dev[1], rows], dst.at[p.z, rows], send.at[k], recv.at[k], dev)
            for k, dev in ((k, p.at_z(k)) for k in range(1, p.nz))
        ]
        self.local = pltpu.make_async_copy(src.at[p.z, rows], dst.at[p.z, rows], send.at[0])

    def start(self, local=True):
        for cp in self.copies:
            cp.start()
        if local:
            self.local.start()

    def wait(self, local=True):
        for cp in self.copies:
            cp.wait()
        if local:
            self.local.wait()


def dot(a, b):
    return lax.dot_general(a, b, (((1,), (0,)), ((), ())), preferred_element_type=f32)


def dot_nt(a, b):
    return lax.dot_general(a, b, (((1,), (1,)), ((), ())), preferred_element_type=f32)


def dot_tn(a, b):
    return lax.dot_general(a, b, (((0,), (0,)), ((), ())), preferred_element_type=f32)


def norm_parts(rows):
    centred = rows - jnp.mean(rows, axis=-1, keepdims=True)
    inverse = lax.rsqrt(jnp.mean(centred * centred, axis=-1, keepdims=True) + EPS)
    return centred * inverse, inverse


def norm_back(grad, normed, inverse):
    first = jnp.mean(grad, axis=-1, keepdims=True)
    second = normed * jnp.mean(grad * normed, axis=-1, keepdims=True)
    return inverse * (grad - first - second)


def regroup(per, group, nz, block, j):
    row = lax.broadcasted_iota(jnp.int32, (per, nz * block), 0).astype(f32)
    col = lax.broadcasted_iota(jnp.int32, (per, nz * block), 1).astype(f32)
    plane = jnp.floor((row + 0.5) * (1.0 / group))
    return jnp.where(col == row + plane * (block - group) + j * group, 1.0, 0.0).astype(bf16)


def router_softmax(rows, wr, experts):
    lane = lax.broadcasted_iota(jnp.int32, (1, 128), 1)
    logits = jnp.where(lane < experts, dot(rows, wr), -1e30)
    ex = jnp.exp(logits - jnp.max(logits, axis=-1, keepdims=True))
    return ex / jnp.sum(ex, axis=-1, keepdims=True)


def padded(value, rows):
    return jnp.concatenate([value, jnp.zeros((rows - value.shape[0], value.shape[1]), value.dtype)], axis=0)


def layer_tile(wqkv_ref, wout_ref, t):
    d = wout_ref.shape[1]
    part = d // TILES
    return jnp.concatenate(
        [wqkv_ref[:, j * d + t * part : j * d + (t + 1) * part] for j in range(3)]
        + [wout_ref[:, t * part : (t + 1) * part]],
        axis=1,
    )


def route(info, place_ref, image, cap, slots, experts, seq):
    lanes = info.shape[1]
    row = lax.broadcasted_iota(jnp.int32, info.shape, 0)
    lane = lax.broadcasted_iota(jnp.int32, info.shape, 1)
    info = jnp.where(lane < seq, info, jnp.where(row == 0, 1e6, -1.0 - row.astype(f32)))
    cols = jnp.transpose(info)
    rank_c, one_c, two_c = cols[:, 0:1], cols[:, 1:2], cols[:, 2:3]
    rank_r, one_r, two_r = info[0:1, :], info[1:2, :], info[2:3, :]
    earlier = rank_c < rank_r
    count = lambda m: jnp.sum(jnp.where(m, 1.0, 0.0), axis=0, keepdims=True)
    pos_one = count(earlier & (one_c == one_r))
    pos_two = count(earlier & (two_c == two_r)) + count(one_c == two_r)
    code = lambda pos, pick: jnp.where(
        (pos < cap) & (pick >= 0), pick * slots + (pos + image * cap), -1.0
    ).astype(jnp.int32)
    code_one, code_two = code(pos_one, one_r), code(pos_two, two_r)
    for e in range(experts):
        slot = lax.broadcasted_iota(jnp.int32, (slots, lanes), 0) + e * slots
        hit = (slot == code_one) | (slot == code_two)
        place_ref[e * slots : (e + 1) * slots, image * lanes : (image + 1) * lanes] = jnp.where(
            hit, 1.0, 0.0
        ).astype(bf16)


def attend_kernel(
    ndp, nz, cap, experts, fold,
    img_ref, cot_ref, priority_ref, choices_ref, router_ref, gain_one_ref, gain_two_ref,
    wqkv_ref, wout_ref, win_ref, wback_ref,
    wi_out, wb_out, wl_out, rtok_out, rdy_out, place_out, mixed_out, probs_out, att_out, res_out, sg_ref,
    zs_ref, zsm_ref, wl_ref, wt_ref, tok_ref, stok_ref, sdy_ref, x_ref,
    place_ref, mixed_ref, probs_ref, att_ref, res_ref, info_ref, small_ref,
    lsend, lrecv, zsend, zrecv, gsend, grecv, tsend, trecv, ysend, yrecv, osem,
):
    p = Place(ndp, nz)
    seq, images, d = img_ref.shape
    rows, lanes = x_ref.shape[1], info_ref.shape[2]
    slots = stok_ref.shape[1]
    some = d // 128 // TILES
    group, per = wqkv_ref.shape[0], d // ndp
    width = wl_ref.shape[3]
    thin, block = width // fold, zs_ref.shape[2]
    chunk = width // ndp
    saves = []

    def save(src, dst):
        cp = pltpu.make_async_copy(src, dst, osem.at[len(saves)])
        cp.start()
        saves.append(cp)

    small_ref[...] = jnp.zeros_like(small_ref)
    small_ref[:experts, :group] = router_ref[...].astype(f32)
    small_ref[experts : experts + 1, :group] = gain_one_ref[...].astype(f32)
    small_ref[experts + 1 : experts + 2, :group] = gain_two_ref[...].astype(f32)
    zsm_ref[p.z] = jnp.transpose(small_ref[...])[: zsm_ref.shape[1]].astype(bf16)
    for n in range(TILES):
        tile = layer_tile(wqkv_ref, wout_ref, n)
        if block == fold * group:
            tile = tile.astype(f32)
            pieces = [tile[:, j * thin : (j + 1) * thin] for j in range(fold)]
            zs_ref[n, p.z] = jnp.concatenate(pieces, axis=0).astype(bf16)
        else:
            zs_ref[n, p.z] = jnp.zeros((block, thin), bf16)
            zs_ref[n, p.z, :group] = tile
    p.greet()

    lines = []
    for n in range(TILES + 1):
        ref = zs_ref.at[n] if n < TILES else zsm_ref
        lines.append(
            [remote(ref.at[p.z], ref.at[p.z], zsend.at[n, k], zrecv.at[n, k], p.at_z(k)) for k in range(1, nz)]
        )
    for n in (TILES,) + tuple(range(TILES)):
        for cp in lines[n]:
            cp.start()

    layer_units = []
    for n in range(TILES + 1):
        full = wl_ref.at[n] if n < TILES else sg_ref
        layer_units.append(
            PlaneGather(
                p, full.at[p.dp], lambda dd, full=full: full.at[dd],
                lambda i, n=n: lsend.at[n, i], lambda i, n=n: lrecv.at[n, i],
            )
        )
    expert_units = []
    for t in range(TILES):
        for w, (own, full) in enumerate(((wt_ref, wi_out), (wback_ref, wb_out))):
            n = t * 2 + w
            expert_units.append(
                PlaneGather(
                    p, own.at[t], lambda dd, full=full, t=t: full.at[t, dd],
                    lambda i, n=n: gsend.at[n, i], lambda i, n=n: grecv.at[n, i],
                )
            )
    for t in range(TILES):
        for i in range(ndp):
            wt_ref[t, :, i * chunk : (i + 1) * chunk] = win_ref[
                :, (i * TILES + t) * chunk : (i * TILES + t + 1) * chunk
            ]
        if t == 0:
            for u in expert_units[:2]:
                u.start()

    tok_ref[...] = jnp.zeros_like(tok_ref)
    info_ref[...] = jnp.zeros_like(info_ref)
    for i in range(images):
        info_ref[i, 0:1, :seq] = priority_ref[i : i + 1, :].astype(f32)
        info_ref[i, 1:3, :seq] = choices_ref[i].astype(f32)
        route(info_ref[i], place_ref, i, cap, slots, experts, seq)
        tok_ref[i * lanes : i * lanes + rows, :] = padded(cot_ref[:, i, :].astype(f32), rows).astype(bf16)

    cuts = [i * cap // 16 * 16 for i in range(images)] + [slots]

    def dispatch(out_ref, lo, hi, upto):
        for e in range(experts):
            out_ref[e, lo:hi, :] = dot(
                place_ref[e * slots + lo : e * slots + hi, :upto], tok_ref[:upto, :]
            ).astype(bf16)

    dispatch(sdy_ref, 0, slots, images * lanes)
    send_dy = Exchange(p, sdy_ref, rdy_out, pl.ds(0, slots), ysend, yrecv)
    save(place_ref, place_out)

    def line_done(n):
        for cp in lines[n]:
            cp.wait_recv()
        if n == TILES:
            tall = zsm_ref.shape[1]
            sg_ref[p.dp] = dot(regroup(per, group, nz, tall, 0), zsm_ref[...].reshape(nz * tall, 128)).astype(bf16)
        else:
            flat = zs_ref[n].reshape(nz * block, thin)
            for j in range(fold):
                wl_ref[n, p.dp, :, j * thin : (j + 1) * thin] = dot(
                    regroup(per, group, nz, block, j), flat
                ).astype(bf16)
        layer_units[n].start()

    order = (TILES,) + tuple(range(TILES))
    for n in order:
        line_done(n)
    send_dy.start()
    for i, n in enumerate(order[:-1]):
        layer_units[n].middle()
        if i >= 1:
            layer_units[order[i - 1]].last()
    layer_units[order[-1]].middle()
    layer_units[order[-2]].last()
    layer_units[order[-1]].last()
    for u in expert_units[:2]:
        u.middle()
    for t in range(TILES):
        for w, (own, full) in enumerate(((wt_ref, wi_out), (wback_ref, wb_out))):
            if t > 0:
                expert_units[t * 2 + w].start()
            save(own.at[t], full.at[t, p.dp])
    for u in expert_units[:2]:
        u.last()

    layer_units[TILES].arrive()
    gains = jnp.transpose(sg_ref[...].reshape(d, 128).astype(f32))
    gain_one, gain_two = gains[experts : experts + 1, :], gains[experts + 1 : experts + 2, :]
    normed = []
    for i in range(images):
        x_ref[i] = padded(img_ref[:, i, :].astype(f32), rows)
        normed.append((norm_parts(x_ref[i])[0] * gain_one).astype(bf16))
        mixed_ref[i, rows:, :] = jnp.zeros((lanes - rows, 3 * d), bf16)
    first = jnp.concatenate(normed, axis=0)
    for n in range(TILES):
        layer_units[n].arrive()
        save(wl_ref.at[n], wl_out.at[n])
        got = dot(first, wl_ref[n].reshape(d, width)[:, :d]).astype(bf16)
        mixed_ref[:, :rows, n * d : (n + 1) * d] = got.reshape(images, rows, d)

    low_half = lax.broadcasted_iota(jnp.int32, (1, 128), 1) < HEAD_DIM
    valid = lax.broadcasted_iota(jnp.int32, (1, lanes), 1) < seq
    save(mixed_ref, mixed_out)

    sends = []
    for i in range(images):

        @pl.loop(0, TILES)
        def _(t):
            for u in range(some):
                n = t * some + u
                at = lambda part: pl.ds(pl.multiple_of(t * d + (part * some + u) * 128, 128), 128)
                q, k, v = mixed_ref[i, :rows, at(0)], mixed_ref[i, :, at(1)], mixed_ref[i, :, at(2)]
                got = []
                for h in range(2):
                    mask = low_half if h == 0 else ~low_half
                    scores = dot_nt(jnp.where(mask, q, jnp.zeros_like(q)), k) * HEAD_DIM**-0.5
                    scores = jnp.where(valid, scores, -1e30)
                    e = jnp.exp(scores - jnp.max(scores, axis=-1, keepdims=True))
                    prob = (e * (1.0 / jnp.sum(e, axis=-1, keepdims=True))).astype(bf16)
                    probs_ref[i, n * 2 + h] = prob
                    got.append(dot(prob, v))
                att_ref[i, :, pl.ds(pl.multiple_of(n * 128, 128), 128)] = jnp.where(low_half, got[0], got[1]).astype(bf16)

        added = [dot(att_ref[i], wl_ref[t].reshape(d, width)[:, d:]) for t in range(TILES)]
        residual = x_ref[i] + jnp.concatenate(added, axis=1)
        res_ref[i] = residual
        tok_ref[i * lanes : i * lanes + rows, :] = (norm_parts(residual)[0] * gain_two).astype(bf16)
        dispatch(stok_ref, cuts[i], cuts[i + 1], (i + 1) * lanes)
        ex = Exchange(
            p, stok_ref, rtok_out, pl.ds(cuts[i], cuts[i + 1] - cuts[i]), tsend.at[i], trecv.at[i]
        )
        ex.start()
        sends.append(ex)
        save(probs_ref.at[i], probs_out.at[i])
        save(att_ref.at[i], att_out.at[i])
        save(res_ref.at[i], res_out.at[i])

    for u in expert_units[2:]:
        u.middle()
    for u in expert_units[2:]:
        u.last()
    for u in expert_units:
        u.arrive()
        u.leave()
    for u in layer_units:
        u.leave()
    for n in range(TILES + 1):
        for cp in lines[n]:
            cp.wait_send()
    send_dy.wait()
    for ex in sends:
        ex.wait()
    for cp in saves:
        cp.wait()


def attend(ndp, nz, cap, slots, images, cotangent, priority, choices, router, gain_one, gain_two, wqkv, wout, win, wback):
    seq, count, d = images.shape
    experts = router.shape[0]
    rows, lanes = up(seq, 16), up(seq, 128)
    group, per, width = wqkv.shape[0], d // ndp, 4 * d // TILES
    fold = 16 // math.gcd(group, 16)
    if width // fold % 128:
        fold = 1
    block = fold * group if fold * group % 16 == 0 else up(group, 16)
    shape, dma, vm = jax.ShapeDtypeStruct, pltpu.SemaphoreType.DMA, pltpu.VMEM
    ns = PlaneGather.sems(ndp)
    heads = d // HEAD_DIM
    return pl.pallas_call(
        partial(attend_kernel, ndp, nz, cap, experts, fold),
        out_shape=(
            shape((TILES, ndp, per, width), bf16),
            shape((TILES, ndp) + wback.shape[1:], bf16),
            shape((TILES, ndp, per, width), bf16),
            shape((nz, slots, d), bf16),
            shape((nz, slots, d), bf16),
            shape((experts * slots, count * lanes), bf16),
            shape((count, lanes, 3 * d), bf16),
            shape((count, heads, rows, lanes), bf16),
            shape((count, rows, d), bf16),
            shape((count, rows, d), f32),
            shape((ndp, per, 128), bf16),
        ),
        in_specs=[VM] * 11,
        out_specs=(ANY,) * 10 + (VM,),
        scratch_shapes=[
            vm((TILES, nz, block, width // fold), bf16),
            vm((nz, up(group, 16), 128), bf16),
            vm((TILES, ndp, per, width), bf16),
            vm((TILES, per, width), bf16),
            vm((count * lanes, d), bf16),
            vm((experts, slots, d), bf16),
            vm((experts, slots, d), bf16),
            vm((count, rows, d), f32),
            vm((experts * slots, count * lanes), bf16),
            vm((count, lanes, 3 * d), bf16),
            vm((count, heads, rows, lanes), bf16),
            vm((count, rows, d), bf16),
            vm((count, rows, d), f32),
            vm((count, 8, lanes), f32),
            vm((128, 128), f32),
            dma((TILES + 1, ns)), dma((TILES + 1, ns)),
            dma((TILES + 1, nz)), dma((TILES + 1, nz)),
            dma((2 * TILES, ns)), dma((2 * TILES, ns)),
            dma((count, nz)), dma((count, nz)),
            dma((nz,)), dma((nz,)),
            dma((3 * TILES + 2 + 3 * count,)),
        ],
        compiler_params=pltpu.CompilerParams(
            collective_id=0, has_side_effects=True, vmem_limit_bytes=VMEM_BYTES
        ),
        name="attend",
    )(images, cotangent, priority, choices, router, gain_one, gain_two, wqkv, wout, win, wback)


class LineScatter:
    def __init__(self, place, fold, sent, got, send, recv):
        self.p, self.fold, self.sent, self.got = place, fold, sent, got
        self.copies = []
        for k in range(1, place.nz):
            dev = place.at_z(k)
            self.copies.append(remote(sent.at[dev[1]], got.at[place.z], send.at[k], recv.at[k], dev))

    def start(self, total, group):
        per, thin = total.shape[0], total.shape[1] // self.fold
        nz, block = self.sent.shape[0], self.sent.shape[1]
        low = total.astype(bf16)
        acc = None
        for j in range(self.fold):
            more = dot_tn(regroup(per, group, nz, block, j), low[:, j * thin : (j + 1) * thin])
            acc = more if acc is None else acc + more
        self.sent[...] = acc.astype(bf16).reshape(self.sent.shape)
        for cp in self.copies:
            cp.start()

    def finish(self, group):
        p = self.p
        for cp in self.copies:
            cp.wait()
        total = self.sent[p.z].astype(f32)
        for k in range(1, p.nz):
            total += self.got[p.z_from(k)].astype(f32)
        return jnp.concatenate([total[j * group : (j + 1) * group] for j in range(self.fold)], axis=1)


def expert_gates(p, experts, buf_ref, dy_ref, wr, gs_ref, rp_ref):
    rows, d = gs_ref.shape
    lane = lax.broadcasted_iota(jnp.int32, (1, 128), 1)
    rp = router_softmax(buf_ref[...].reshape(rows, d), wr, experts)
    rp_ref[...] = rp
    gate = jnp.sum(jnp.where(lane == p.z, rp, 0.0), axis=-1, keepdims=True)
    gs_ref[...] = (gate * dy_ref[...].reshape(rows, d).astype(f32)).astype(bf16)


def expert_tile(t, wi_ref, wb_ref, buf_ref, gs_ref, act_ref, gh_ref):
    rows, d = gs_ref.shape
    width = act_ref.shape[2]
    step = min(256, width)
    k0, k1 = 0.7978845608028654, 0.044715 * 0.7978845608028654
    wi = wi_ref[t].reshape(d, width)
    wb = wb_ref[t].reshape(width, d)
    for n in range(width // step):
        lo, hi = n * step, (n + 1) * step
        h = dot(buf_ref[...].reshape(rows, d), wi[:, lo:hi])
        grad = dot_nt(gs_ref[...], wb[lo:hi])
        h2 = h * h
        th = jnp.tanh(h * (k0 + k1 * h2))
        half = 0.5 * (1.0 + th)
        act_ref[t, :, lo:hi] = (h * half).astype(bf16)
        slope = half + 0.5 * h * (1.0 - th * th) * (k0 + 3.0 * k1 * h2)
        gh_ref[t, :, lo:hi] = (grad * slope).astype(bf16)


def learn_kernel(
    ndp, nz, experts, fold, rows,
    wi_in, wb_in, wl_in, rtok_in, rdy_in, place_in, mixed_in, probs_in, att_in, res_in,
    sg_ref, img_ref, cot_ref,
    out_ref, gin_ref, gl_ref, gsm_ref, gi_ref, gb_ref,
    pin_ref, pback_ref, sin_ref, sback_ref, xin_ref, xback_ref, sgrad_ref, rgrad_ref, eo_ref, ro_ref,
    tot_ref, gr_ref, psm_ref, ssm_ref, xsm_ref, tsm_ref, zsent_ref, zgot_ref, zssm_ref, zgsm_ref, vec_ref,
    esend, erecv, lsend, lrecv, zsend, zrecv, rsend, rrecv, osend, orecv, free, isem,
):
    p = Place(ndp, nz)
    seq, images, d = img_ref.shape
    slots = rtok_in.shape[1]
    lanes = mixed_in.shape[1]
    per, width = wi_in.shape[2], wi_in.shape[3]
    per_back = wb_in.shape[2]
    chips = ndp // 2
    some, part = d // 128 // TILES, d // TILES
    group = per // nz
    p.greet()
    lane = lax.broadcasted_iota(jnp.int32, (1, 128), 1)
    wr = sg_ref[...].reshape(d, 128)

    experts_sums = []
    for t in range(TILES):
        for w, (mine, sib, got, out) in enumerate(
            ((pin_ref, sin_ref, xin_ref, gi_ref), (pback_ref, sback_ref, xback_ref, gb_ref))
        ):
            n = t * 2 + w
            experts_sums.append(
                PlaneScatter(
                    p, mine.at[t], sib.at[t], got.at[t], out.at[t],
                    lambda i, n=n: esend.at[n, i], lambda i, n=n: erecv.at[n, i],
                )
            )
    both = lambda t: experts_sums[2 * t : 2 * t + 2]
    back = Exchange(p, sgrad_ref, rgrad_ref, pl.ds(0, slots), rsend, rrecv)
    outs = Exchange(p, eo_ref, ro_ref, pl.ds(0, slots), osend, orecv)

    def expert_part(wi_ref, wb_ref, buf_ref, dy_ref, gs_ref, act_ref, gh_ref, rp_ref):
        copies = [
            pltpu.make_async_copy(rtok_in, buf_ref, isem.at[0]),
            pltpu.make_async_copy(rdy_in, dy_ref, isem.at[1]),
        ]
        for t in range(TILES):
            copies.append(pltpu.make_async_copy(wi_in.at[t], wi_ref.at[t], isem.at[2 + 2 * t]))
            copies.append(pltpu.make_async_copy(wb_in.at[t], wb_ref.at[t], isem.at[3 + 2 * t]))
        for cp in copies:
            cp.start()
        copies[0].wait()
        copies[1].wait()

        def loads(t):
            copies[2 + 2 * t].wait()
            copies[3 + 2 * t].wait()

        def weight_grads(t):
            buf = buf_ref[...].reshape(nz * slots, d)
            pin_ref[t] = dot_tn(buf, gh_ref[t]).astype(bf16).reshape(chips, 2, per, width)
            both(t)[0].start()
            pback_ref[t] = dot_tn(act_ref[t], gs_ref[...]).astype(bf16).reshape(chips, 2, per_back, d)
            both(t)[1].start()

        expert_gates(p, experts, buf_ref, dy_ref, wr, gs_ref, rp_ref)
        for t in range(TILES):
            loads(t)
            expert_tile(t, wi_ref, wb_ref, buf_ref, gs_ref, act_ref, gh_ref)
            if t == 0:
                weight_grads(0)
            if t == 1:
                PlaneScatter.middle(*both(0))

        gr_ref[...] = jnp.zeros_like(gr_ref)
        some = max(nz // 2, 1)
        count = some * slots
        mine = jnp.where(lane == p.z, 1.0, 0.0)
        for q in range(nz // some):
            lo, hi = q * count, (q + 1) * count
            out = sum(dot(act_ref[t, lo:hi, :], wb_ref[t].reshape(width, d)) for t in range(TILES)).astype(bf16)
            eo_ref[q * some : (q + 1) * some] = out.reshape(some, slots, d)
            rp = rp_ref[lo:hi, :]
            gate = jnp.sum(mine * rp, axis=-1, keepdims=True)
            rows_dy = dy_ref[q * some : (q + 1) * some].reshape(count, d).astype(f32)
            ggate = jnp.sum(out.astype(f32) * rows_dy, axis=-1, keepdims=True)
            contrib = (ggate * gate) * (mine - rp)
            top = contrib.astype(bf16)
            low = (contrib - top.astype(f32)).astype(bf16)
            grad = sum(dot_nt(gh_ref[t, lo:hi, :], wi_ref[t].reshape(d, width)) for t in range(TILES))
            grad = grad + dot_nt(top, wr) + dot_nt(low, wr)
            sgrad_ref[q * some : (q + 1) * some] = grad.astype(bf16).reshape(some, slots, d)
            rows_buf = buf_ref[q * some : (q + 1) * some].reshape(count, d)
            gr_ref[...] += dot_tn(rows_buf, top) + dot_tn(rows_buf, low)
        back.start(local=False)
        rgrad_ref[p.z] = sgrad_ref[p.z]

        PlaneScatter.last(*both(0))
        for t in range(1, TILES):
            weight_grads(t)
            if t >= 2:
                PlaneScatter.middle(*both(t - 1))
        for u in both(0):
            u.finish()

    shared = nz * slots
    pl.run_scoped(
        expert_part,
        pltpu.VMEM((TILES, ndp, per, width), bf16),
        pltpu.VMEM((TILES, ndp, per_back, d), bf16),
        pltpu.VMEM((nz, slots, d), bf16),
        pltpu.VMEM((nz, slots, d), bf16),
        pltpu.VMEM((shared, d), bf16),
        pltpu.VMEM((TILES, shared, width), bf16),
        pltpu.VMEM((TILES, shared, width), bf16),
        pltpu.VMEM((shared, 128), f32),
    )

    layer_sums, lines = [], []
    for n in range(TILES + 1):
        mine, sib, got, tot, zs, zg = (
            (pin_ref.at[n], sin_ref.at[n], xin_ref.at[n], tot_ref.at[n], zsent_ref.at[n], zgot_ref.at[n])
            if n < TILES
            else (psm_ref, ssm_ref, xsm_ref, tsm_ref, zssm_ref, zgsm_ref)
        )
        layer_sums.append(
            PlaneScatter(p, mine, sib, got, tot, lambda i, n=n: lsend.at[n, i], lambda i, n=n: lrecv.at[n, i])
        )
        lines.append(LineScatter(p, fold if n < TILES else 1, zs, zg, zsend.at[n], zrecv.at[n]))

    def attend_part(
        wl_ref, place_ref, mixed_ref, probs_ref, att_ref, res_ref,
        gres_ref, branch_ref, gatt_ref, gmix_ref, first_ref,
    ):
        copies = [
            pltpu.make_async_copy(src, dst, isem.at[n])
            for n, (src, dst) in enumerate(
                (
                    (place_in, place_ref), (res_in, res_ref), (wl_in, wl_ref), (att_in, att_ref),
                    (mixed_in, mixed_ref), (probs_in, probs_ref),
                )
            )
        ]
        for cp in copies:
            cp.start()
        PlaneScatter.middle(*both(TILES - 1))
        PlaneScatter.last(*both(TILES - 2))
        gains = jnp.transpose(wr.astype(f32))
        gain_one, gain_two = gains[experts : experts + 1, :], gains[experts + 1 : experts + 2, :]
        normed_one = lambda i: norm_parts(padded(img_ref[:, i, :].astype(f32), rows))
        for i in range(images):
            first_ref[i] = (normed_one(i)[0] * gain_one).astype(bf16)
        for cp in copies:
            cp.wait()
        PlaneScatter.last(*both(TILES - 1))
        back.wait(local=False)
        outs.start(local=False)
        ro_ref[p.z] = eo_ref[p.z]
        vec_two = jnp.zeros((1, d), f32)
        for i in range(images):
            hits = place_ref[:, i * lanes : (i + 1) * lanes]
            grad_second = dot_tn(hits, rgrad_ref[...].reshape(experts * slots, d))[:rows]
            normed, inverse = norm_parts(res_ref[i])
            vec_two += jnp.sum(grad_second * normed, axis=0, keepdims=True)
            grad = padded(cot_ref[:, i, :].astype(f32), rows) + norm_back(grad_second * gain_two, normed, inverse)
            gres_ref[i] = grad
            branch = grad.astype(bf16)
            branch_ref[i] = branch
            gatt_ref[i] = sum(
                dot_nt(branch[:, t * part : (t + 1) * part], wl_ref[t].reshape(d, width)[:, d:])
                for t in range(TILES)
            ).astype(bf16)

        low_half = lax.broadcasted_iota(jnp.int32, (1, 128), 1) < HEAD_DIM
        scale = HEAD_DIM**-0.5

        flat = lambda v: v.reshape(images * rows, v.shape[-1])
        for t in range(TILES):

            @pl.loop(0, some)
            def _(u):
                at = lambda j: pl.ds(pl.multiple_of(t * d + j * part + u * 128, 128), 128)
                here = pl.ds(pl.multiple_of(t * part + u * 128, 128), 128)
                for i in range(images):
                    q, k, v = mixed_ref[i, :rows, at(0)], mixed_ref[i, :, at(1)], mixed_ref[i, :, at(2)]
                    ga = gatt_ref[i, :, here]
                    gq, gk, gv = [], [], []
                    for h in range(2):
                        mask = low_half if h == 0 else ~low_half
                        prob = probs_ref[i, (t * some + u) * 2 + h]
                        gv.append(dot_tn(prob, ga)[:rows])
                        weighting = dot_nt(jnp.where(mask, ga, jnp.zeros_like(ga)), v)
                        wide = prob.astype(f32)
                        scores = wide * (weighting - jnp.sum(wide * weighting, axis=-1, keepdims=True))
                        scores = scores.astype(bf16)
                        gq.append(dot(scores, k))
                        gk.append(dot_tn(scores, q)[:rows])
                    pick = lambda pair, by: jnp.where(low_half, pair[0], pair[1]) * by
                    gmix_ref[i, :, at(0)] = pick(gq, scale).astype(bf16)
                    gmix_ref[i, :, at(1)] = pick(gk, scale).astype(bf16)
                    gmix_ref[i, :, at(2)] = pick(gv, 1.0).astype(bf16)

            if t == 0:
                for n in range(1, TILES):
                    for u in both(n):
                        u.finish()
                for dev in p.plane():
                    pl.semaphore_signal(free, inc=1, device_id=dev, device_id_type=MESH)
                pl.semaphore_wait(free, len(p.plane()))
            got = dot_tn(flat(first_ref[...]), flat(gmix_ref[:, :, t * d : (t + 1) * d]))
            pin_ref[t, :, :, :, :d] = got.astype(bf16).reshape(chips, 2, per, d)
            more = dot_tn(flat(att_ref[...]), flat(branch_ref[:, :, t * part : (t + 1) * part]))
            pin_ref[t, :, :, :, d:] = more.astype(bf16).reshape(chips, 2, per, part)
            layer_sums[t].start()
            if t >= 1:
                PlaneScatter.middle(layer_sums[t - 1])
            if t >= 2:
                PlaneScatter.last(layer_sums[t - 2])

        def to_line(n):
            layer_sums[n].finish()
            ref = tot_ref.at[n] if n < TILES else tsm_ref
            if n < TILES:
                lines[n].start(ref[...], group)
            else:
                for k in range(nz):
                    zssm_ref[k, :group, :] = tsm_ref[k * group : (k + 1) * group, :]
                for cp in lines[n].copies:
                    cp.start()

        vec_one = jnp.zeros((1, d), f32)
        for i in range(images):
            grad_first = sum(
                dot_nt(gmix_ref[i, :, t * d : (t + 1) * d], wl_ref[t].reshape(d, width)[:, :d])
                for t in range(TILES)
            )
            normed, inverse = normed_one(i)
            vec_one += jnp.sum(grad_first * normed, axis=0, keepdims=True)
            gin_ref[i] = gres_ref[i] + norm_back(grad_first * gain_one, normed, inverse)
            if i == 0:
                PlaneScatter.middle(layer_sums[TILES - 1])
                PlaneScatter.last(layer_sums[TILES - 2])
                to_line(0)

        vec_ref[0:1, :] = vec_one
        vec_ref[1:2, :] = vec_two
        cols = jnp.transpose(vec_ref[...])
        small = jnp.where(
            lane == experts, cols[:, 0:1], jnp.where(lane == experts + 1, cols[:, 1:2], gr_ref[...])
        )
        psm_ref[...] = small.reshape(chips, 2, per, 128)
        layer_sums[TILES].start()
        PlaneScatter.last(layer_sums[TILES - 1])
        PlaneScatter.middle(layer_sums[TILES])
        for n in range(1, TILES - 1):
            to_line(n)
        outs.wait(local=False)

        def output(i):
            second = (norm_parts(res_ref[i])[0] * gain_two).astype(bf16)
            rp = router_softmax(second, wr, experts)
            total = res_ref[i]
            for e in range(experts):
                hits = place_ref[e * slots : (e + 1) * slots, i * lanes : (i + 1) * lanes]
                gate = jnp.sum(jnp.where(lane == e, rp, 0.0), axis=-1, keepdims=True)
                total = total + gate * dot_tn(hits, ro_ref[e])[:rows]
            out_ref[i] = total

        output(0)
        PlaneScatter.last(layer_sums[TILES])
        to_line(TILES - 1)
        to_line(TILES)
        for i in range(1, images):
            output(i)
        for n in range(TILES):
            gl_ref[:, n * width : (n + 1) * width] = lines[n].finish(group)[:group]
        gsm_ref[...] = lines[TILES].finish(zssm_ref.shape[1])[:group]

    pl.run_scoped(
        attend_part,
        pltpu.VMEM((TILES, ndp, per, width), bf16),
        pltpu.VMEM(place_in.shape, bf16),
        pltpu.VMEM(mixed_in.shape, bf16),
        pltpu.VMEM(probs_in.shape, bf16),
        pltpu.VMEM((images, rows, d), bf16),
        pltpu.VMEM((images, rows, d), f32),
        pltpu.VMEM((images, rows, d), f32),
        pltpu.VMEM((images, rows, d), bf16),
        pltpu.VMEM((images, rows, d), bf16),
        pltpu.VMEM((images, rows, 3 * d), bf16),
        pltpu.VMEM((images, rows, d), bf16),
    )


def learn(ndp, nz, experts, front, images, cotangent):
    wi, wb, wl, rtok, rdy, place, mixed, probs, att, res, sg = front
    seq, count, d = images.shape
    rows = res.shape[1]
    per, width, per_back = wi.shape[2], wi.shape[3], wb.shape[2]
    chips, group = ndp // 2, per // nz
    fold = 16 // math.gcd(group, 16)
    if width // fold % 128:
        fold = 1
    block = fold * group if fold * group % 16 == 0 else up(group, 16)
    short = up(group, 8)
    nb = ndp // 2 - 1
    slots = rtok.shape[1]
    shape, dma, vm = jax.ShapeDtypeStruct, pltpu.SemaphoreType.DMA, pltpu.VMEM
    ns = PlaneScatter.sems(ndp)
    return pl.pallas_call(
        partial(learn_kernel, ndp, nz, experts, fold, rows),
        out_shape=(
            shape((count, rows, d), f32),
            shape((count, rows, d), f32),
            shape((group, 4 * d), f32),
            shape((group, 128), f32),
            shape((TILES, per, width), f32),
            shape((TILES, per_back, d), f32),
        ),
        in_specs=[ANY] * 10 + [VM] * 3,
        out_specs=(VM,) * 6,
        scratch_shapes=[
            vm((TILES, chips, 2, per, width), bf16),
            vm((TILES, chips, 2, per_back, d), bf16),
            vm((TILES, chips, per, width), bf16),
            vm((TILES, chips, per_back, d), bf16),
            vm((TILES, nb, per, width), bf16),
            vm((TILES, nb, per_back, d), bf16),
            vm((nz, slots, d), bf16),
            vm((nz, slots, d), bf16),
            vm((nz, slots, d), bf16),
            vm((nz, slots, d), bf16),
            vm((TILES, per, width), f32),
            vm((d, 128), f32),
            vm((chips, 2, per, 128), f32),
            vm((chips, per, 128), f32),
            vm((nb, per, 128), f32),
            vm((per, 128), f32),
            vm((TILES, nz, block, width // fold), bf16),
            vm((TILES, nz, block, width // fold), bf16),
            vm((nz, short, 128), f32),
            vm((nz, short, 128), f32),
            vm((8, d), f32),
            dma((2 * TILES, ns)), dma((2 * TILES, ns)),
            dma((TILES + 1, ns)), dma((TILES + 1, ns)),
            dma((TILES + 1, nz)), dma((TILES + 1, nz)),
            dma((nz,)), dma((nz,)),
            dma((nz,)), dma((nz,)),
            pltpu.SemaphoreType.REGULAR,
            dma((2 + 2 * TILES,)),
        ],
        compiler_params=pltpu.CompilerParams(
            collective_id=1, has_side_effects=True, vmem_limit_bytes=VMEM_BYTES
        ),
        name="learn",
    )(wi, wb, wl, rtok, rdy, place, mixed, probs, att, res, sg, images, cotangent)


def settle_kernel(
    experts,
    out_ref, gin_ref, gl_ref, gsm_ref, gi_ref, gb_ref,
    output_ref, input_grad_ref, gain_one_ref, qkv_ref, wout_ref, gain_two_ref, router_ref, in_ref, back_ref,
):
    group, d = wout_ref.shape
    part = d // TILES
    ndp, chunk = d // in_ref.shape[0], in_ref.shape[1] // (d // in_ref.shape[0]) // TILES
    seq, images, _ = output_ref.shape
    for i in range(images):
        output_ref[:, i, :] = out_ref[i, :seq].astype(bf16)
        input_grad_ref[:, i, :] = gin_ref[i, :seq]
    for t in range(TILES):
        for j in range(4):
            piece = gl_ref[:, t * 4 * part + j * part : t * 4 * part + (j + 1) * part]
            if j < 3:
                qkv_ref[:, j * d + t * part : j * d + (t + 1) * part] = piece
            else:
                wout_ref[:, t * part : (t + 1) * part] = piece
        for i in range(ndp):
            in_ref[:, (i * TILES + t) * chunk : (i * TILES + t + 1) * chunk] = gi_ref[
                t, :, i * chunk : (i + 1) * chunk
            ]
    small = jnp.transpose(padded(gsm_ref[...], 128))[:, :group]
    router_ref[...] = small[:experts]
    gain_one_ref[...] = small[experts : experts + 1]
    gain_two_ref[...] = small[experts + 1 : experts + 2]
    back_ref[...] = gb_ref[...]


def settle(experts, seq, out, gin, gl, gsm, gi, gb):
    group, d, count = gl.shape[0], out.shape[2], out.shape[0]
    shape = jax.ShapeDtypeStruct
    return pl.pallas_call(
        partial(settle_kernel, experts),
        out_shape=(
            shape((seq, count, d), bf16), shape((seq, count, d), f32), shape((1, group), f32),
            shape((group, 3 * d), f32), shape((group, d), f32), shape((1, group), f32), shape((experts, group), f32),
            shape((gi.shape[1], gi.shape[0] * gi.shape[2]), f32), shape(gb.shape, f32),
        ),
        in_specs=[VM] * 6,
        out_specs=(VM,) * 9,
        compiler_params=pltpu.CompilerParams(vmem_limit_bytes=VMEM_BYTES),
        name="settle",
    )(out, gin, gl, gsm, gi, gb)


def per_device(ndp, nz, images, gain_one, w_qkv, w_out, gain_two, w_router, w_in, w_back, choices, priority, cotangent):
    count, seq, d = images.shape
    group, experts = w_router.shape
    ff = w_in.shape[2]
    cap = (42 * seq + 20 * experts - 1) // (20 * experts)
    slots = up(count * cap, 16)
    chunk = ff // ndp // TILES
    images, cotangent = images.transpose(1, 0, 2), cotangent.transpose(1, 0, 2)
    front = attend(
        ndp, nz, cap, slots, images, cotangent, priority, choices.transpose(0, 2, 1),
        w_router.T, gain_one[None], gain_two[None],
        w_qkv, w_out, w_in[0], w_back[0].reshape(TILES, chunk, d),
    )
    out, gin, gl, gsm, gi, gb = learn(ndp, nz, experts, front, images, cotangent)
    out, gin, gain_one, qkv, wout, gain_two, router, gi, gb = settle(
        experts, seq, out, gin, gl, gsm, gi, gb
    )
    return (
        out.transpose(1, 0, 2), gin.transpose(1, 0, 2), gain_one[0], qkv, wout, gain_two[0], router.T,
        gi.reshape(1, d // ndp, ff), gb.reshape(1, ff // ndp, d),
    )


def solution(mesh):
    ndp, nz = mesh.shape["dp"], mesh.shape["fsdp"]
    both = ("dp", "fsdp")
    tokens, rows, expert_rows = P(both, None, None), P(both, None), P("fsdp", "dp", None)
    return jax.shard_map(
        partial(per_device, ndp, nz),
        mesh=mesh,
        in_specs=(tokens, P(both), rows, rows, P(both), rows, expert_rows, expert_rows, tokens, rows, tokens),
        out_specs=(tokens, tokens, P(both), rows, rows, P(both), rows, expert_rows, expert_rows),
        check_vma=False,
    )
```

```python
import math
from functools import partial

import jax
import jax.numpy as jnp
from jax import lax
from jax.experimental import pallas as pl
from jax.experimental.pallas import tpu as pltpu
from jax.sharding import PartitionSpec as P

f32, bf16 = jnp.float32, jnp.bfloat16
MESH = pl.DeviceIdType.MESH
ANY = pl.BlockSpec(memory_space=pl.ANY)
VM = pl.BlockSpec(memory_space=pltpu.VMEM)
HEAD_DIM = 64
EPS = 1e-6
TILES = 3
VMEM_BYTES = 63 << 20


def up(value, unit):
    return -(-value // unit) * unit


class Place:
    def __init__(self, ndp, nz):
        self.ndp, self.nz, self.chips = ndp, nz, ndp // 2
        self.dp = lax.axis_index("dp")
        self.z = lax.axis_index("fsdp")
        self.core = lax.rem(self.dp, 2)
        self.chip = self.dp // 2
        self.square = self.chips == 4
        if self.square:
            a, b, c = self.chip // 2, lax.rem(self.chip, 2), self.core
            self.near = lax.rem(a + 1 - c, 2) * 2 + lax.rem(b + c, 2)
            self.side = lax.rem(a + c, 2) * 2 + lax.rem(b + 1 - c, 2)
            self.far = (1 - a) * 2 + (1 - b)
            self.mates = [self.near, self.side, self.far]
        else:
            self.mates = [lax.rem(self.chip + k, self.chips) for k in range(1, self.chips)]

        self.other = 1 - self.core
        self.sib = (self.chip * 2 + self.other, self.z)
        self.mate_devs = [(m * 2 + self.core, self.z) for m in self.mates]
        self.plane = [self.sib] + (self.mate_devs[:2] if self.square else self.mate_devs)
        self.behind = [lax.rem(self.chip + self.chips - k, self.chips) for k in range(1, self.chips)]
        self.line = [(self.dp, lax.rem(self.z + k, nz)) for k in range(nz)]
        self.line_from = [lax.rem(self.z + nz - k, nz) for k in range(nz)]

    def greet(self):
        bar = pltpu.get_barrier_semaphore()
        there = self.plane + self.line[1:]
        for dev in there:
            pl.semaphore_signal(bar, inc=1, device_id=dev, device_id_type=MESH)
        pl.semaphore_wait(bar, len(there))


def remote(src, dst, send, recv, dev):
    return pltpu.make_async_remote_copy(
        src_ref=src, dst_ref=dst, send_sem=send, recv_sem=recv, device_id=dev, device_id_type=MESH
    )


class PlaneGather:
    def __init__(self, place, own, slot, send, recv):
        self.p = p = place
        mine = slot(p.chip, p.core)
        self.to_sib = remote(own, mine, send(0), recv(0), p.sib)
        if p.square:
            self.first = [
                remote(own, mine, send(1 + i), recv(1 + i), p.mate_devs[i]) for i in range(2)
            ]
            side = slot(p.side, p.core)
            self.relay = remote(side, side, send(3), recv(3), p.mate_devs[0])
            back, n = p.mates, 4
        else:
            self.first = [
                remote(own, mine, send(1 + i), recv(1 + i), dev) for i, dev in enumerate(p.mate_devs)
            ]
            back, n = p.behind, 1 + len(p.mates)
        self.share = [
            remote(slot(m, p.core), slot(m, p.core), send(n + i), recv(n + i), p.sib)
            for i, m in enumerate(back)
        ]

    @staticmethod
    def sems(ndp):
        chips = ndp // 2
        return 7 if chips == 4 else 1 + 2 * (chips - 1)

    def start(self):
        for cp in self.first:
            cp.start()
        self.to_sib.start()

    def middle(self):
        if self.p.square:
            self.first[1].wait_recv()
            self.relay.start()
            self.share[1].start()
            self.first[0].wait_recv()
            self.share[0].start()
        else:
            for f, s in zip(self.first, self.share):
                f.wait_recv()
                s.start()

    def last(self):
        if self.p.square:
            self.relay.wait_recv()
            self.share[2].start()

    def arrive(self):
        self.to_sib.wait_recv()
        for s in self.share:
            s.wait_recv()

    def leave(self):
        for cp in [self.to_sib] + self.share + self.first + ([self.relay] if self.p.square else []):
            cp.wait_send()


class PlaneScatter:
    def __init__(self, place, part, sib, got, out, send, recv):
        self.p, self.part, self.sib, self.got, self.out = place, part, sib, got, out
        p = place
        self.pair = remote(part.at[:, p.other], sib, send(0), recv(0), p.sib)
        at = lambda m: part.at[m, p.core]
        if p.square:
            self.first = [
                remote(at(p.far), got.at[0], send(1), recv(1), p.mate_devs[0]),
                remote(at(p.near), got.at[1], send(2), recv(2), p.mate_devs[0]),
            ]
            self.second = remote(at(p.side), got.at[2], send(3), recv(3), p.mate_devs[1])
        else:
            self.first = [
                remote(at(m), got.at[i], send(1 + i), recv(1 + i), p.mate_devs[i])
                for i, m in enumerate(p.mates)
            ]

    @staticmethod
    def sems(ndp):
        chips = ndp // 2
        return 4 if chips == 4 else chips

    def add(self, m, more):
        here = self.part.at[m, self.p.core]
        here[...] = (here[...].astype(f32) + more.astype(f32)).astype(here.dtype)

    def start(self):
        self.pair.start()

    @staticmethod
    def middle(*units):
        p = units[0].p
        for u in units:
            u.pair.wait_recv()
        if p.square:
            for n, m in enumerate((p.far, p.near)):
                for u in units:
                    u.add(m, u.sib[m])
                    u.first[n].start()
            for u in units:
                u.add(p.side, u.sib[p.side])
        else:
            for n, m in enumerate(p.mates):
                for u in units:
                    u.add(m, u.sib[m])
                    u.first[n].start()

    @staticmethod
    def last(*units):
        p = units[0].p
        if p.square:
            for u in units:
                u.first[0].wait_recv()
                u.add(p.side, u.got[0])
                u.second.start()

    def finish(self):
        p = self.p
        total = self.part[p.chip, p.core].astype(f32) + self.sib[p.chip].astype(f32)
        if p.square:
            self.first[1].wait_recv()
            total += self.got[1].astype(f32)
            self.second.wait_recv()
            total += self.got[2].astype(f32)
        else:
            for i, cp in enumerate(self.first):
                cp.wait_recv()
                total += self.got[i].astype(f32)
        self.out[...] = total
        for cp in [self.pair] + self.first + ([self.second] if p.square else []):
            cp.wait_send()


class Exchange:
    def __init__(self, p, src, dst, rows, send, recv):
        self.p, self.src, self.dst, self.rows = p, src, dst, rows
        self.copies = [
            remote(src.at[dev[1], rows], dst.at[p.z, rows], send.at[k], recv.at[k], dev)
            for k, dev in enumerate(p.line)
            if k > 0
        ]

    def start(self):
        for cp in self.copies:
            cp.start()
        self.dst[self.p.z, self.rows] = self.src[self.p.z, self.rows]

    def wait(self):
        for cp in self.copies:
            cp.wait()


def dot(a, b):
    return lax.dot_general(a, b, (((1,), (0,)), ((), ())), preferred_element_type=f32)


def dot_nt(a, b):
    return lax.dot_general(a, b, (((1,), (1,)), ((), ())), preferred_element_type=f32)


def dot_tn(a, b):
    return lax.dot_general(a, b, (((0,), (0,)), ((), ())), preferred_element_type=f32)


def norm_parts(rows):
    centred = rows - jnp.mean(rows, axis=-1, keepdims=True)
    inverse = lax.rsqrt(jnp.mean(centred * centred, axis=-1, keepdims=True) + EPS)
    return centred * inverse, inverse


def norm_back(grad, normed, inverse):
    first = jnp.mean(grad, axis=-1, keepdims=True)
    second = normed * jnp.mean(grad * normed, axis=-1, keepdims=True)
    return inverse * (grad - first - second)


def regroup(per, group, nz, block, j):
    row = lax.broadcasted_iota(jnp.int32, (per, nz * block), 0).astype(f32)
    col = lax.broadcasted_iota(jnp.int32, (per, nz * block), 1).astype(f32)
    plane = jnp.floor((row + 0.5) * (1.0 / group))
    return jnp.where(col == row + plane * (block - group) + j * group, 1.0, 0.0).astype(bf16)


def router_softmax(rows, wr, experts):
    lane = lax.broadcasted_iota(jnp.int32, (1, 128), 1)
    logits = jnp.where(lane < experts, dot(rows, wr), -1e30)
    ex = jnp.exp(logits - jnp.max(logits, axis=-1, keepdims=True))
    return ex / jnp.sum(ex, axis=-1, keepdims=True)


def padded(value, rows):
    return jnp.concatenate([value, jnp.zeros((rows - value.shape[0], value.shape[1]), value.dtype)], axis=0)


def layer_tile(wqkv_ref, wout_ref, t):
    d = wout_ref.shape[1]
    part = d // TILES
    return jnp.concatenate(
        [wqkv_ref[:, j * d + t * part : j * d + (t + 1) * part] for j in range(3)]
        + [wout_ref[:, t * part : (t + 1) * part]],
        axis=1,
    )


def route(info, place_ref, image, cap, slots, experts, seq):
    lanes = info.shape[1]
    row = lax.broadcasted_iota(jnp.int32, info.shape, 0)
    lane = lax.broadcasted_iota(jnp.int32, info.shape, 1)
    info = jnp.where(lane < seq, info, jnp.where(row == 0, 1e6, -1.0 - row.astype(f32)))
    cols = jnp.transpose(info)
    rank_c, one_c, two_c = cols[:, 0:1], cols[:, 1:2], cols[:, 2:3]
    rank_r, one_r, two_r = info[0:1, :], info[1:2, :], info[2:3, :]
    earlier = rank_c < rank_r
    count = lambda m: jnp.sum(jnp.where(m, 1.0, 0.0), axis=0, keepdims=True)
    pos_one = count(earlier & (one_c == one_r))
    pos_two = count(earlier & (two_c == two_r)) + count(one_c == two_r)
    code = lambda pos, pick: jnp.where(
        (pos < cap) & (pick >= 0), pick * slots + (pos + image * cap), -1.0
    ).astype(jnp.int32)
    code_one, code_two = code(pos_one, one_r), code(pos_two, two_r)
    for e in range(experts):
        slot = lax.broadcasted_iota(jnp.int32, (slots, lanes), 0) + e * slots
        hit = (slot == code_one) | (slot == code_two)
        place_ref[e * slots : (e + 1) * slots, image * lanes : (image + 1) * lanes] = jnp.where(
            hit, 1.0, 0.0
        ).astype(bf16)


class LineScatter:
    def __init__(self, place, fold, sent, got, send, recv):
        self.p, self.fold, self.sent, self.got = place, fold, sent, got
        self.copies = []
        for k in range(1, place.nz):
            dev = place.line[k]
            self.copies.append(remote(sent.at[dev[1]], got.at[place.z], send.at[k], recv.at[k], dev))

    def start(self, total, group):
        per, thin = total.shape[0], total.shape[1] // self.fold
        nz, block = self.sent.shape[0], self.sent.shape[1]
        low = total.astype(bf16)
        acc = None
        for j in range(self.fold):
            more = dot_tn(regroup(per, group, nz, block, j), low[:, j * thin : (j + 1) * thin])
            acc = more if acc is None else acc + more
        self.sent[...] = acc.astype(bf16).reshape(self.sent.shape)
        for cp in self.copies:
            cp.start()

    def finish(self, group):
        p = self.p
        for cp in self.copies:
            cp.wait()
        total = self.sent[p.z].astype(f32)
        for k in range(1, p.nz):
            total += self.got[p.line_from[k]].astype(f32)
        return jnp.concatenate([total[j * group : (j + 1) * group] for j in range(self.fold)], axis=1)


def expert_gates(p, experts, lo, hi, buf_ref, gs_ref, wr):
    nz, _, d = buf_ref.shape
    count = nz * (hi - lo)
    lane = lax.broadcasted_iota(jnp.int32, (1, 128), 1)
    rp = router_softmax(buf_ref[:, lo:hi, :].reshape(count, d), wr, experts)
    gate = jnp.sum(jnp.where(lane == p.z, rp, 0.0), axis=-1, keepdims=True)
    rows = gs_ref[:, lo:hi, :].reshape(count, d).astype(f32)
    gs_ref[:, lo:hi, :] = (gate * rows).astype(bf16).reshape(nz, hi - lo, d)


def expert_tile(t, lo, hi, wi_ref, wb_ref, buf_ref, gs_ref, act_ref, gh_ref):
    nz, _, d = buf_ref.shape
    count, width = nz * (hi - lo), act_ref.shape[3]
    step = min(256, width)
    k0, k1 = 0.7978845608028654, 0.044715 * 0.7978845608028654
    wi = wi_ref[t].reshape(d, width)
    wb = wb_ref[t].reshape(width, d)
    put = lambda v: v.astype(bf16).reshape(nz, hi - lo, step)
    for n in range(width // step):
        cols = slice(n * step, (n + 1) * step)
        h = dot(buf_ref[:, lo:hi, :].reshape(count, d), wi[:, cols])
        grad = dot_nt(gs_ref[:, lo:hi, :].reshape(count, d), wb[cols])
        h2 = h * h
        th = jnp.tanh(h * (k0 + k1 * h2))
        half = 0.5 * (1.0 + th)
        act_ref[t, :, lo:hi, cols] = put(h * half)
        slope = half + 0.5 * h * (1.0 - th * th) * (k0 + 3.0 * k1 * h2)
        gh_ref[t, :, lo:hi, cols] = put(grad * slope)


def expert_back(
    p, experts, lo, hi, wi_ref, wb_ref, buf_ref, gs_ref, act_ref, gh_ref, wr, eo_ref, sgrad_ref, gr_ref
):
    nz, _, d = buf_ref.shape
    count, width = nz * (hi - lo), act_ref.shape[3]
    lane = lax.broadcasted_iota(jnp.int32, (1, 128), 1)
    mine = jnp.where(lane == p.z, 1.0, 0.0)
    part = lambda ref, *at: ref[at + (slice(None), slice(lo, hi))].reshape(count, ref.shape[-1])
    out = sum(dot(part(act_ref, t), wb_ref[t].reshape(width, d)) for t in range(TILES)).astype(bf16)
    eo_ref[:, lo:hi, :] = out.reshape(nz, hi - lo, d)
    both = jnp.sum(out.astype(f32) * part(gs_ref).astype(f32), axis=-1, keepdims=True)
    contrib = both * (mine - router_softmax(part(buf_ref), wr, experts))
    top = contrib.astype(bf16)
    low = (contrib - top.astype(f32)).astype(bf16)
    grad = sum(dot_nt(part(gh_ref, t), wi_ref[t].reshape(d, width)) for t in range(TILES))
    grad = grad + dot_nt(top, wr) + dot_nt(low, wr)
    sgrad_ref[:, lo:hi, :] = grad.astype(bf16).reshape(nz, hi - lo, d)
    gr_ref[...] += dot_tn(part(buf_ref), top) + dot_tn(part(buf_ref), low)


def block_kernel(
    ndp, nz, cap, experts, fold,
    img_ref, cot_ref, priority_ref, choices_ref, router_ref, gain_one_ref, gain_two_ref,
    wqkv_ref, wout_ref, win_ref, wback_ref,
    wi_hbm, wb_hbm, wl_hbm, mixed_hbm, probs_hbm, att_hbm, res_hbm, out_hbm, gin_hbm, gl_ref, gsm_ref, gi_ref, gb_ref,
    zs_ref, zsm_ref, big_ref, wt_ref, sg_ref, sa_ref, sb_ref, buf_ref, gs_ref, rgrad_ref, ro_ref,
    place_ref,
    pback_ref, sin_ref, sback_ref, xin_ref, xback_ref, lsin_ref, lxin_ref,
    gr_ref, ssm_ref, xsm_ref, zssm_ref, zgsm_ref,
    lsend, lrecv, zsend, zrecv, gsend, grecv, tsend, trecv, ysend, yrecv,
    rsend, rrecv, osend, orecv, esend, erecv, ssend, srecv, usend, urecv, ksem, isem,
):
    p = Place(ndp, nz)
    seq, images, d = img_ref.shape
    rows, lanes = res_hbm.shape[1], place_ref.shape[1] // images
    slots = sa_ref.shape[1]
    chips, part = ndp // 2, d // TILES
    some = d // 128 // TILES
    group, per = wqkv_ref.shape[0], d // ndp
    width = big_ref.shape[4]
    per_back = wback_ref.shape[1]
    lane = lax.broadcasted_iota(jnp.int32, (1, 128), 1)
    low_half = lane < HEAD_DIM
    thin, block = width // fold, zs_ref.shape[2]
    chunk = width // ndp
    saves = []

    def save(src, dst):
        cp = pltpu.make_async_copy(src, dst, ksem.at[2 * TILES + len(saves)])
        cp.start()
        saves.append(cp)
        return cp

    small_ref = gr_ref.at[:128]
    small_ref[...] = jnp.zeros((128, 128), f32)
    small_ref[:experts, :group] = router_ref[...].astype(f32)
    small_ref[experts : experts + 1, :group] = gain_one_ref[...].astype(f32)
    small_ref[experts + 1 : experts + 2, :group] = gain_two_ref[...].astype(f32)
    zsm_ref[p.z] = jnp.transpose(small_ref[...])[: zsm_ref.shape[1]].astype(bf16)
    for n in range(TILES):
        tile = layer_tile(wqkv_ref, wout_ref, n)
        if block == fold * group:
            tile = tile.astype(f32)
            pieces = [tile[:, j * thin : (j + 1) * thin] for j in range(fold)]
            zs_ref[n, p.z] = jnp.concatenate(pieces, axis=0).astype(bf16)
        else:
            zs_ref[n, p.z] = jnp.zeros((block, thin), bf16)
            zs_ref[n, p.z, :group] = tile
    p.greet()

    lines = []
    for n in range(TILES + 1):
        ref = zs_ref.at[n] if n < TILES else zsm_ref
        lines.append(
            [remote(ref.at[p.z], ref.at[p.z], zsend.at[n, k], zrecv.at[n, k], p.line[k]) for k in range(1, nz)]
        )
    for n in (TILES,) + tuple(range(TILES)):
        for cp in lines[n]:
            cp.start()

    layer_units = []
    for n in range(TILES + 1):
        if n < TILES:
            slot = lambda chip, core, n=n: big_ref.at[n, chip, core]
        else:
            slot = lambda chip, core: sg_ref.at[chip * 2 + core]
        layer_units.append(
            PlaneGather(
                p, slot(p.chip, p.core), slot,
                lambda i, n=n: lsend.at[n, i], lambda i, n=n: lrecv.at[n, i],
            )
        )
    expert_units = []
    for t in range(TILES):
        for w, (own, full) in enumerate(((wt_ref, wi_hbm), (wback_ref, wb_hbm))):
            n = t * 2 + w
            expert_units.append(
                PlaneGather(
                    p, own.at[t], lambda chip, core, full=full, t=t: full.at[t, chip * 2 + core],
                    lambda i, n=n: gsend.at[n, i], lambda i, n=n: grecv.at[n, i],
                )
            )
    for t in range(TILES):
        for i in range(ndp):
            wt_ref[t, :, i * chunk : (i + 1) * chunk] = win_ref[
                :, (i * TILES + t) * chunk : (i * TILES + t + 1) * chunk
            ]
        if t == 0:
            for u in expert_units[:2]:
                u.start()

    cuts = [i * cap // 16 * 16 for i in range(images)] + [slots]
    parts = [pl.ds(lo, hi - lo) for lo, hi in zip(cuts[:-1], cuts[1:])]
    send_dy = Exchange(p, sb_ref, gs_ref, pl.ds(0, slots), ysend, yrecv)
    sends = [Exchange(p, sa_ref, buf_ref, s, tsend.at[i], trecv.at[i]) for i, s in enumerate(parts)]
    backs = [Exchange(p, sa_ref, rgrad_ref, s, rsend.at[i], rrecv.at[i]) for i, s in enumerate(parts)]
    outs = Exchange(p, sb_ref, ro_ref, pl.ds(0, slots), osend, orecv)
    own_saves = [
        pltpu.make_async_copy(own.at[t], full.at[t, p.dp], ksem.at[t * 2 + w])
        for t in range(TILES)
        for w, (own, full) in enumerate(((wt_ref, wi_hbm), (wback_ref, wb_hbm)))
    ]
    parked = []

    def forward(tok_ref, x_ref, mixed_ref, probs_ref, att_ref, res_ref, info_ref):
        tok_ref[...] = jnp.zeros_like(tok_ref)
        info_ref[...] = jnp.zeros_like(info_ref)
        for i in range(images):
            info_ref[i, 0:1, :seq] = priority_ref[i : i + 1, :].astype(f32)
            info_ref[i, 1:3, :seq] = choices_ref[i].astype(f32)
            route(info_ref[i], place_ref, i, cap, slots, experts, seq)
            tok_ref[i * lanes : i * lanes + rows, :] = padded(cot_ref[:, i, :].astype(f32), rows).astype(bf16)

        def dispatch(out_ref, lo, hi, upto):
            for e in range(experts):
                out_ref[e, lo:hi, :] = dot(
                    place_ref[e * slots + lo : e * slots + hi, :upto], tok_ref[:upto, :]
                ).astype(bf16)

        dispatch(sb_ref, 0, slots, images * lanes)

        def line_done(n):
            for cp in lines[n]:
                cp.wait_recv()
            if n == TILES:
                tall = zsm_ref.shape[1]
                sg_ref[p.dp] = dot(regroup(per, group, nz, tall, 0), zsm_ref[...].reshape(nz * tall, 128)).astype(bf16)
            else:
                flat = zs_ref[n].reshape(nz * block, thin)
                for j in range(fold):
                    big_ref[n, p.chip, p.core, :, j * thin : (j + 1) * thin] = dot(
                        regroup(per, group, nz, block, j), flat
                    ).astype(bf16)
            layer_units[n].start()

        order = (TILES,) + tuple(range(TILES))
        for n in order:
            line_done(n)
        send_dy.start()
        for i, n in enumerate(order[:-1]):
            layer_units[n].middle()
            if i >= 1:
                layer_units[order[i - 1]].last()
        layer_units[order[-1]].middle()
        layer_units[order[-2]].last()
        layer_units[order[-1]].last()
        for u in expert_units[:2]:
            u.middle()
        for t in range(TILES):
            for n in (2 * t, 2 * t + 1):
                if t > 0:
                    expert_units[n].start()
                own_saves[n].start()
        for u in expert_units[:2]:
            u.last()

        layer_units[TILES].arrive()
        gains = jnp.transpose(sg_ref[...].reshape(d, 128).astype(f32))
        gain_one, gain_two = gains[experts : experts + 1, :], gains[experts + 1 : experts + 2, :]
        normed = []
        for i in range(images):
            x_ref[i] = padded(img_ref[:, i, :].astype(f32), rows)
            normed.append((norm_parts(x_ref[i])[0] * gain_one).astype(bf16))
            mixed_ref[i, rows:, :] = jnp.zeros((lanes - rows, 3 * d), bf16)
        first = jnp.concatenate(normed, axis=0)
        for n in range(TILES):
            layer_units[n].arrive()
            parked.append(save(big_ref.at[n], wl_hbm.at[n]))
            got = dot(first, big_ref[n].reshape(d, width)[:, :d]).astype(bf16)
            mixed_ref[:, :rows, n * d : (n + 1) * d] = got.reshape(images, rows, d)

        valid = lax.broadcasted_iota(jnp.int32, (1, lanes), 1) < seq
        parked.append(save(mixed_ref, mixed_hbm))

        for i in range(images):

            @pl.loop(0, TILES)
            def _(t):
                for u in range(some):
                    n = t * some + u
                    at = lambda part: pl.ds(pl.multiple_of(t * d + (part * some + u) * 128, 128), 128)
                    q, k, v = mixed_ref[i, :rows, at(0)], mixed_ref[i, :, at(1)], mixed_ref[i, :, at(2)]
                    got = []
                    for h in range(2):
                        mask = low_half if h == 0 else ~low_half
                        scores = dot_nt(jnp.where(mask, q, jnp.zeros_like(q)), k) * HEAD_DIM**-0.5
                        scores = jnp.where(valid, scores, -1e30)
                        e = jnp.exp(scores - jnp.max(scores, axis=-1, keepdims=True))
                        prob = (e * (1.0 / jnp.sum(e, axis=-1, keepdims=True))).astype(bf16)
                        probs_ref[i, n * 2 + h] = prob
                        got.append(dot(prob, v))
                    att_ref[i, :, pl.ds(pl.multiple_of(n * 128, 128), 128)] = jnp.where(low_half, got[0], got[1]).astype(bf16)

            added = [dot(att_ref[i], big_ref[t].reshape(d, width)[:, d:]) for t in range(TILES)]
            residual = x_ref[i] + jnp.concatenate(added, axis=1)
            res_ref[i] = residual
            tok_ref[i * lanes : i * lanes + rows, :] = (norm_parts(residual)[0] * gain_two).astype(bf16)
            dispatch(sa_ref, cuts[i], cuts[i + 1], (i + 1) * lanes)
            sends[i].start()
            parked.append(save(probs_ref.at[i], probs_hbm.at[i]))
            parked.append(save(att_ref.at[i], att_hbm.at[i]))
            parked.append(save(res_ref.at[i], res_hbm.at[i]))

        for cp in parked:
            cp.wait()

    pl.run_scoped(
        forward,
        pltpu.VMEM((images * lanes, d), bf16),
        pltpu.VMEM((images, rows, d), f32),
        pltpu.VMEM(mixed_hbm.shape, bf16),
        pltpu.VMEM(probs_hbm.shape, bf16),
        pltpu.VMEM(att_hbm.shape, bf16),
        pltpu.VMEM(res_hbm.shape, f32),
        pltpu.VMEM((images, 8, lanes), f32),
    )

    wr = sg_ref[...].reshape(d, 128)
    expert_sums = []
    for t in range(TILES):
        for w, (mine, sib, got, out) in enumerate(
            ((big_ref, sin_ref, xin_ref, gi_ref), (pback_ref, sback_ref, xback_ref, gb_ref))
        ):
            n = t * 2 + w
            expert_sums.append(
                PlaneScatter(
                    p, mine.at[t], sib.at[t], got.at[t], out.at[t],
                    lambda i, n=n: esend.at[n, i], lambda i, n=n: erecv.at[n, i],
                )
            )
    both = lambda t: expert_sums[2 * t : 2 * t + 2]

    def expert_part(wi_ref, wb_ref, act_ref, gh_ref):
        def fetch(t):
            copies = []
            for w, (src, dst) in enumerate(((wi_hbm, wi_ref), (wb_hbm, wb_ref))):
                n = t * 2 + w
                expert_units[n].arrive()
                own_saves[n].wait()
                copies.append(pltpu.make_async_copy(src.at[t], dst.at[t], isem.at[n]))
                copies[-1].start()
            for cp in copies:
                cp.wait()

        def weight_grads(t):
            flat = lambda v: v.reshape(nz * slots, v.shape[-1])
            got = dot_tn(flat(buf_ref[...]), flat(gh_ref[t]))
            big_ref[t] = got.astype(bf16).reshape(chips, 2, per, width)
            both(t)[0].start()
            got = dot_tn(flat(act_ref[t]), flat(gs_ref[...]))
            pback_ref[t] = got.astype(bf16).reshape(chips, 2, per_back, d)
            both(t)[1].start()

        for u in expert_units[2:]:
            u.middle()
        send_dy.wait()
        gr_ref[...] = jnp.zeros_like(gr_ref)
        for i, (lo, hi) in enumerate(zip(cuts[:-1], cuts[1:])):
            sends[i].wait()
            expert_gates(p, experts, lo, hi, buf_ref, gs_ref, wr)
            for t in range(TILES):
                if i == 0:
                    if t >= 1:
                        for u in expert_units[2 * t : 2 * t + 2]:
                            u.last()
                    fetch(t)
                expert_tile(t, lo, hi, wi_ref, wb_ref, buf_ref, gs_ref, act_ref, gh_ref)
                if i == images - 1 and t == 0:
                    for u in layer_units + expert_units:
                        u.leave()
                    weight_grads(0)
                if i == images - 1 and t == 1:
                    PlaneScatter.middle(*both(0))
            expert_back(
                p, experts, lo, hi, wi_ref, wb_ref, buf_ref, gs_ref, act_ref, gh_ref, wr, sb_ref, sa_ref, gr_ref
            )
            backs[i].start()
        PlaneScatter.last(*both(0))
        for t in range(1, TILES):
            weight_grads(t)
            if t >= 2:
                PlaneScatter.middle(*both(t - 1))
        for u in both(0):
            u.finish()

    pl.run_scoped(
        expert_part,
        pltpu.VMEM((TILES, ndp, per, width), bf16),
        pltpu.VMEM((TILES, ndp, per_back, d), bf16),
        pltpu.VMEM((TILES, nz, slots, width), bf16),
        pltpu.VMEM((TILES, nz, slots, width), bf16),
    )

    def backward(
        wl_ref, mixed_ref, probs_ref, att_ref, res_ref, gres_ref, branch_ref, gatt_ref, first_ref, tot_ref, lpart_ref,
        psm_ref, tsm_ref, zsent_ref, vec_ref,
    ):
        layer_sums, sum_lines = [], []
        for n in range(TILES + 1):
            mine, sib, got, tot, zs, zg = (
                (lpart_ref.at[n], lsin_ref.at[n], lxin_ref.at[n], tot_ref.at[n], zsent_ref.at[n], zs_ref.at[n])
                if n < TILES
                else (psm_ref, ssm_ref, xsm_ref, tsm_ref, zssm_ref, zgsm_ref)
            )
            layer_sums.append(
                PlaneScatter(p, mine, sib, got, tot, lambda i, n=n: ssend.at[n, i], lambda i, n=n: srecv.at[n, i])
            )
            sum_lines.append(LineScatter(p, fold if n < TILES else 1, zs, zg, usend.at[n], urecv.at[n]))

        copies = [
            pltpu.make_async_copy(src, dst, isem.at[n])
            for n, (src, dst) in enumerate(
                (
                    (res_hbm, res_ref), (wl_hbm, wl_ref), (att_hbm, att_ref), (mixed_hbm, mixed_ref),
                    (probs_hbm, probs_ref),
                )
            )
        ]
        for cp in copies:
            cp.start()
        PlaneScatter.middle(*both(TILES - 1))
        gains = jnp.transpose(wr.astype(f32))
        gain_one, gain_two = gains[experts : experts + 1, :], gains[experts + 1 : experts + 2, :]
        normed_one = lambda i: norm_parts(padded(img_ref[:, i, :].astype(f32), rows))
        for i in range(images):
            first_ref[i] = (normed_one(i)[0] * gain_one).astype(bf16)
        for cp in copies:
            cp.wait()
        for ex in backs:
            ex.wait()
        outs.start()
        vec_two = jnp.zeros((1, d), f32)
        for i in range(images):
            hits = place_ref[:, i * lanes : (i + 1) * lanes]
            grad_second = dot_tn(hits, rgrad_ref[...].reshape(experts * slots, d))[:rows]
            normed, inverse = norm_parts(res_ref[i])
            vec_two += jnp.sum(grad_second * normed, axis=0, keepdims=True)
            grad = padded(cot_ref[:, i, :].astype(f32), rows) + norm_back(grad_second * gain_two, normed, inverse)
            gres_ref[i] = grad
            branch = grad.astype(bf16)
            branch_ref[i] = branch
            gatt_ref[i] = sum(
                dot_nt(branch[:, t * part : (t + 1) * part], wl_ref[t].reshape(d, width)[:, d:])
                for t in range(TILES)
            ).astype(bf16)

        scale = HEAD_DIM**-0.5

        PlaneScatter.last(*both(TILES - 2))
        flat = lambda v: v.reshape(images * rows, v.shape[-1])
        for t in range(TILES):

            @pl.loop(0, some)
            def _(u):
                at = lambda j: pl.ds(pl.multiple_of(t * d + j * part + u * 128, 128), 128)
                here = pl.ds(pl.multiple_of(t * part + u * 128, 128), 128)
                for i in range(images):
                    q, k, v = mixed_ref[i, :rows, at(0)], mixed_ref[i, :, at(1)], mixed_ref[i, :, at(2)]
                    ga = gatt_ref[i, :, here]
                    gq, gk, gv = [], [], []
                    for h in range(2):
                        mask = low_half if h == 0 else ~low_half
                        prob = probs_ref[i, (t * some + u) * 2 + h]
                        gv.append(dot_tn(prob, ga)[:rows])
                        weighting = dot_nt(jnp.where(mask, ga, jnp.zeros_like(ga)), v)
                        wide = prob.astype(f32)
                        scores = wide * (weighting - jnp.sum(wide * weighting, axis=-1, keepdims=True))
                        scores = scores.astype(bf16)
                        gq.append(dot(scores, k))
                        gk.append(dot_tn(scores, q)[:rows])
                    pick = lambda pair, by: jnp.where(low_half, pair[0], pair[1]) * by
                    mixed_ref[i, :rows, at(0)] = pick(gq, scale).astype(bf16)
                    mixed_ref[i, :rows, at(1)] = pick(gk, scale).astype(bf16)
                    mixed_ref[i, :rows, at(2)] = pick(gv, 1.0).astype(bf16)

            got = dot_tn(flat(first_ref[...]), flat(mixed_ref[:, :rows, t * d : (t + 1) * d]))
            lpart_ref[t, :, :, :, :d] = got.astype(bf16).reshape(chips, 2, per, d)
            more = dot_tn(flat(att_ref[...]), flat(branch_ref[:, :, t * part : (t + 1) * part]))
            lpart_ref[t, :, :, :, d:] = more.astype(bf16).reshape(chips, 2, per, part)
            layer_sums[t].start()
            if t == 1:
                PlaneScatter.last(*both(TILES - 1))
            if t >= 1:
                PlaneScatter.middle(layer_sums[t - 1])
            if t >= 2:
                PlaneScatter.last(layer_sums[t - 2])

        def to_line(n):
            layer_sums[n].finish()
            ref = tot_ref.at[n] if n < TILES else tsm_ref
            if n < TILES:
                sum_lines[n].start(ref[...], group)
            else:
                for k in range(nz):
                    zssm_ref[k, :group, :] = tsm_ref[k * group : (k + 1) * group, :]
                for cp in sum_lines[n].copies:
                    cp.start()

        vec_one = jnp.zeros((1, d), f32)
        for i in range(images):
            grad_first = sum(
                dot_nt(mixed_ref[i, :rows, t * d : (t + 1) * d], wl_ref[t].reshape(d, width)[:, :d])
                for t in range(TILES)
            )
            normed, inverse = normed_one(i)
            vec_one += jnp.sum(grad_first * normed, axis=0, keepdims=True)
            gres_ref[i] += norm_back(grad_first * gain_one, normed, inverse)
            save(gres_ref.at[i], gin_hbm.at[i])
            if i == 0:
                PlaneScatter.middle(layer_sums[TILES - 1])
                PlaneScatter.last(layer_sums[TILES - 2])
                to_line(0)

        for n in range(1, TILES):
            for u in both(n):
                u.finish()
        vec_ref[0:1, :] = vec_one
        vec_ref[1:2, :] = vec_two
        cols = jnp.transpose(vec_ref[...])
        small = jnp.where(
            lane == experts, cols[:, 0:1], jnp.where(lane == experts + 1, cols[:, 1:2], gr_ref[...])
        )
        psm_ref[...] = small.reshape(chips, 2, per, 128)
        layer_sums[TILES].start()
        PlaneScatter.last(layer_sums[TILES - 1])
        PlaneScatter.middle(layer_sums[TILES])
        for n in range(1, TILES - 1):
            to_line(n)
        outs.wait()

        def output(i):
            second = (norm_parts(res_ref[i])[0] * gain_two).astype(bf16)
            rp = router_softmax(second, wr, experts)
            total = res_ref[i]
            for e in range(experts):
                hits = place_ref[e * slots : (e + 1) * slots, i * lanes : (i + 1) * lanes]
                gate = jnp.sum(jnp.where(lane == e, rp, 0.0), axis=-1, keepdims=True)
                total = total + gate * dot_tn(hits, ro_ref[e])[:rows]
            gatt_ref[i] = total.astype(bf16)
            save(gatt_ref.at[i], out_hbm.at[i])

        output(0)
        PlaneScatter.last(layer_sums[TILES])
        to_line(TILES - 1)
        to_line(TILES)
        for i in range(1, images):
            output(i)
        for n in range(TILES):
            gl_ref[:, n * width : (n + 1) * width] = sum_lines[n].finish(group)[:group]
        gsm_ref[...] = sum_lines[TILES].finish(zssm_ref.shape[1])[:group]

        for group_of in lines:
            for cp in group_of:
                cp.wait_send()
        for cp in saves:
            if not any(cp is done for done in parked):
                cp.wait()

    pl.run_scoped(
        backward,
        pltpu.VMEM(wl_hbm.shape, bf16),
        pltpu.VMEM(mixed_hbm.shape, bf16),
        pltpu.VMEM(probs_hbm.shape, bf16),
        pltpu.VMEM(att_hbm.shape, bf16),
        pltpu.VMEM(res_hbm.shape, f32),
        pltpu.VMEM((images, rows, d), f32),
        pltpu.VMEM((images, rows, d), bf16),
        pltpu.VMEM((images, rows, d), bf16),
        pltpu.VMEM((images, rows, d), bf16),
        pltpu.VMEM((TILES, per, width), f32),
        pltpu.VMEM((TILES, chips, 2, per, width), bf16),
        pltpu.VMEM((chips, 2, per, 128), f32),
        pltpu.VMEM((per, 128), f32),
        pltpu.VMEM(zs_ref.shape, bf16),
        pltpu.VMEM((8, d), f32),
    )


def block(ndp, nz, cap, slots, images, cotangent, priority, choices, router, gain_one, gain_two, wqkv, wout, win, wback):
    seq, count, d = images.shape
    experts = router.shape[0]
    rows, lanes = up(seq, 16), up(seq, 128)
    group, per, width = wqkv.shape[0], d // ndp, 4 * d // TILES
    per_back, chips = wback.shape[1], ndp // 2
    fold = 16 // math.gcd(group, 16)
    if width // fold % 128:
        fold = 1
    tall, short = up(group, 16), up(group, 8)
    line = fold * group if fold * group % 16 == 0 else tall
    shape, vm = jax.ShapeDtypeStruct, pltpu.VMEM
    dma = lambda *dims: [pltpu.SemaphoreType.DMA(dims)] * 2
    ng, ns, nb = PlaneGather.sems(ndp), PlaneScatter.sems(ndp), chips - 1
    return pl.pallas_call(
        partial(block_kernel, ndp, nz, cap, experts, fold),
        out_shape=(
            shape((TILES, ndp, per, width), bf16),
            shape((TILES, ndp, per_back, d), bf16),
            shape((TILES, chips, 2, per, width), bf16),
            shape((count, lanes, 3 * d), bf16),
            shape((count, d // HEAD_DIM, rows, lanes), bf16),
            shape((count, rows, d), bf16),
            shape((count, rows, d), f32),
            shape((count, rows, d), bf16),
            shape((count, rows, d), f32),
            shape((group, 4 * d), f32),
            shape((group, 128), f32),
            shape((TILES, per, width), f32),
            shape((TILES, per_back, d), f32),
        ),
        in_specs=[VM] * 11,
        out_specs=(ANY,) * 9 + (VM,) * 4,
        scratch_shapes=[
            vm((TILES, nz, line, width // fold), bf16),
            vm((nz, tall, 128), bf16),
            vm((TILES, chips, 2, per, width), bf16),
            vm((TILES, per, width), bf16),
            vm((ndp, per, 128), bf16),
        ]
        + [vm((nz, slots, d), bf16)] * 6
        + [
            vm((experts * slots, count * lanes), bf16),
            vm((TILES, chips, 2, per_back, d), bf16),
            vm((TILES, chips, per, width), bf16),
            vm((TILES, chips, per_back, d), bf16),
            vm((TILES, nb, per, width), bf16),
            vm((TILES, nb, per_back, d), bf16),
            vm((TILES, chips, per, width), bf16),
            vm((TILES, nb, per, width), bf16),
            vm((d, 128), f32),
            vm((chips, per, 128), f32),
            vm((nb, per, 128), f32),
            vm((nz, short, 128), f32),
            vm((nz, short, 128), f32),
        ]
        + dma(TILES + 1, ng) + dma(TILES + 1, nz) + dma(2 * TILES, ng) + dma(count, nz) + dma(nz)
        + dma(count, nz) + dma(nz) + dma(2 * TILES, ns) + dma(TILES + 1, ns) + dma(TILES + 1, nz)
        + [
            pltpu.SemaphoreType.DMA((3 * TILES + 1 + 5 * count,)),
            pltpu.SemaphoreType.DMA((2 * TILES,)),
        ],
        compiler_params=pltpu.CompilerParams(
            collective_id=0, has_side_effects=True, vmem_limit_bytes=VMEM_BYTES
        ),
        name="block",
    )(images, cotangent, priority, choices, router, gain_one, gain_two, wqkv, wout, win, wback)


def settle_kernel(
    experts,
    out_ref, gin_ref, gl_ref, gsm_ref, gi_ref, gb_ref,
    output_ref, input_grad_ref, gain_one_ref, qkv_ref, wout_ref, gain_two_ref, router_ref, in_ref, back_ref,
):
    group, d = wout_ref.shape
    part = d // TILES
    ndp, chunk = d // in_ref.shape[0], in_ref.shape[1] // (d // in_ref.shape[0]) // TILES
    seq, images, _ = output_ref.shape
    for i in range(images):
        output_ref[:, i, :] = out_ref[i].astype(f32)[:seq].astype(bf16)
        input_grad_ref[:, i, :] = gin_ref[i, :seq]
    for t in range(TILES):
        for j in range(4):
            piece = gl_ref[:, t * 4 * part + j * part : t * 4 * part + (j + 1) * part]
            if j < 3:
                qkv_ref[:, j * d + t * part : j * d + (t + 1) * part] = piece
            else:
                wout_ref[:, t * part : (t + 1) * part] = piece
        for i in range(ndp):
            in_ref[:, (i * TILES + t) * chunk : (i * TILES + t + 1) * chunk] = gi_ref[
                t, :, i * chunk : (i + 1) * chunk
            ]
    small = jnp.transpose(padded(gsm_ref[...], 128))[:, :group]
    router_ref[...] = small[:experts]
    gain_one_ref[...] = small[experts : experts + 1]
    gain_two_ref[...] = small[experts + 1 : experts + 2]
    back_ref[...] = gb_ref[...]


def settle(experts, seq, out, gin, gl, gsm, gi, gb):
    group, d, count = gl.shape[0], out.shape[2], out.shape[0]
    shape = jax.ShapeDtypeStruct
    return pl.pallas_call(
        partial(settle_kernel, experts),
        out_shape=(
            shape((seq, count, d), bf16), shape((seq, count, d), f32), shape((1, group), f32),
            shape((group, 3 * d), f32), shape((group, d), f32), shape((1, group), f32), shape((experts, group), f32),
            shape((gi.shape[1], gi.shape[0] * gi.shape[2]), f32), shape(gb.shape, f32),
        ),
        in_specs=[VM] * 6,
        out_specs=(VM,) * 9,
        compiler_params=pltpu.CompilerParams(vmem_limit_bytes=VMEM_BYTES),
        name="settle",
    )(out, gin, gl, gsm, gi, gb)


def per_device(ndp, nz, images, gain_one, w_qkv, w_out, gain_two, w_router, w_in, w_back, choices, priority, cotangent):
    count, seq, d = images.shape
    group, experts = w_router.shape
    ff = w_in.shape[2]
    cap = (42 * seq + 20 * experts - 1) // (20 * experts)
    slots = up(count * cap, 16)
    chunk = ff // ndp // TILES
    images, cotangent = images.transpose(1, 0, 2), cotangent.transpose(1, 0, 2)
    out, gin, gl, gsm, gi, gb = block(
        ndp, nz, cap, slots, images, cotangent, priority, choices.transpose(0, 2, 1),
        w_router.T, gain_one[None], gain_two[None],
        w_qkv, w_out, w_in[0], w_back[0].reshape(TILES, chunk, d),
    )[7:]
    out, gin, gain_one, qkv, wout, gain_two, router, gi, gb = settle(
        experts, seq, out, gin, gl, gsm, gi, gb
    )
    return (
        out.transpose(1, 0, 2), gin.transpose(1, 0, 2), gain_one[0], qkv, wout, gain_two[0], router.T,
        gi.reshape(1, d // ndp, ff), gb.reshape(1, ff // ndp, d),
    )


def solution(mesh):
    ndp, nz = mesh.shape["dp"], mesh.shape["fsdp"]
    both = ("dp", "fsdp")
    tokens, rows, expert_rows = P(both, None, None), P(both, None), P("fsdp", "dp", None)
    return jax.shard_map(
        partial(per_device, ndp, nz),
        mesh=mesh,
        in_specs=(tokens, P(both), rows, rows, P(both), rows, expert_rows, expert_rows, tokens, rows, tokens),
        out_specs=(tokens, tokens, P(both), rows, rows, P(both), rows, expert_rows, expert_rows),
        check_vma=False,
    )
```

```python
import math
from functools import partial

import jax
import jax.numpy as jnp
from jax import lax
from jax.experimental import pallas as pl
from jax.experimental.pallas import tpu as pltpu
from jax.sharding import PartitionSpec as P

f32, bf16 = jnp.float32, jnp.bfloat16
MESH = pl.DeviceIdType.MESH
ANY = pl.BlockSpec(memory_space=pl.ANY)
VM = pl.BlockSpec(memory_space=pltpu.VMEM)
HEAD_DIM = 64
EPS = 1e-6
TILES = 3
VMEM_BYTES = 63 << 20


def up(value, unit):
    return -(-value // unit) * unit


class Place:
    def __init__(self, ndp, nz):
        self.ndp, self.nz, self.chips = ndp, nz, ndp // 2
        self.dp = lax.axis_index("dp")
        self.z = lax.axis_index("fsdp")
        self.core = lax.rem(self.dp, 2)
        self.chip = self.dp // 2
        self.square = self.chips == 4
        if self.square:
            a, b, c = self.chip // 2, lax.rem(self.chip, 2), self.core
            self.near = lax.rem(a + 1 - c, 2) * 2 + lax.rem(b + c, 2)
            self.side = lax.rem(a + c, 2) * 2 + lax.rem(b + 1 - c, 2)
            self.far = (1 - a) * 2 + (1 - b)
            self.mates = [self.near, self.side, self.far]
        else:
            self.mates = [lax.rem(self.chip + k, self.chips) for k in range(1, self.chips)]

        self.other = 1 - self.core
        self.sib = (self.chip * 2 + self.other, self.z)
        self.mate_devs = [(m * 2 + self.core, self.z) for m in self.mates]
        self.plane = [self.sib] + (self.mate_devs[:2] if self.square else self.mate_devs)
        self.behind = [lax.rem(self.chip + self.chips - k, self.chips) for k in range(1, self.chips)]
        self.line = [(self.dp, lax.rem(self.z + k, nz)) for k in range(nz)]
        self.line_from = [lax.rem(self.z + nz - k, nz) for k in range(nz)]

    def greet(self):
        bar = pltpu.get_barrier_semaphore()
        there = self.plane + self.line[1:]
        for dev in there:
            pl.semaphore_signal(bar, inc=1, device_id=dev, device_id_type=MESH)
        pl.semaphore_wait(bar, len(there))


def remote(src, dst, send, recv, dev):
    return pltpu.make_async_remote_copy(
        src_ref=src, dst_ref=dst, send_sem=send, recv_sem=recv, device_id=dev, device_id_type=MESH
    )


class PlaneGather:
    def __init__(self, place, own, slot, send, recv):
        self.p = p = place
        mine = slot(p.chip, p.core)
        self.to_sib = remote(own, mine, send(0), recv(0), p.sib)
        if p.square:
            self.first = [
                remote(own, mine, send(1 + i), recv(1 + i), p.mate_devs[i]) for i in range(2)
            ]
            side = slot(p.side, p.core)
            self.relay = remote(side, side, send(3), recv(3), p.mate_devs[0])
            back, n = p.mates, 4
        else:
            self.first = [
                remote(own, mine, send(1 + i), recv(1 + i), dev) for i, dev in enumerate(p.mate_devs)
            ]
            back, n = p.behind, 1 + len(p.mates)
        self.share = [
            remote(slot(m, p.core), slot(m, p.core), send(n + i), recv(n + i), p.sib)
            for i, m in enumerate(back)
        ]

    @staticmethod
    def sems(ndp):
        chips = ndp // 2
        return 7 if chips == 4 else 1 + 2 * (chips - 1)

    def start(self):
        for cp in self.first:
            cp.start()
        self.to_sib.start()

    def middle(self):
        if self.p.square:
            self.first[1].wait_recv()
            self.relay.start()
            self.share[1].start()
            self.first[0].wait_recv()
            self.share[0].start()
        else:
            for f, s in zip(self.first, self.share):
                f.wait_recv()
                s.start()

    def last(self):
        if self.p.square:
            self.relay.wait_recv()
            self.share[2].start()

    def arrive(self):
        self.to_sib.wait_recv()
        for s in self.share:
            s.wait_recv()

    def leave(self):
        for cp in [self.to_sib] + self.share + self.first + ([self.relay] if self.p.square else []):
            cp.wait_send()


class PlaneScatter:
    def __init__(self, place, part, sib, got, out, send, recv):
        self.p, self.part, self.sib, self.got, self.out = place, part, sib, got, out
        p = place
        self.pair = remote(part.at[:, p.other], sib, send(0), recv(0), p.sib)
        at = lambda m: part.at[m, p.core]
        if p.square:
            self.first = [
                remote(at(p.far), got.at[0], send(1), recv(1), p.mate_devs[0]),
                remote(at(p.near), got.at[1], send(2), recv(2), p.mate_devs[0]),
            ]
            self.second = remote(at(p.side), got.at[2], send(3), recv(3), p.mate_devs[1])
        else:
            self.first = [
                remote(at(m), got.at[i], send(1 + i), recv(1 + i), p.mate_devs[i])
                for i, m in enumerate(p.mates)
            ]

    @staticmethod
    def sems(ndp):
        chips = ndp // 2
        return 4 if chips == 4 else chips

    def add(self, m, more):
        here = self.part.at[m, self.p.core]
        here[...] = (here[...].astype(f32) + more.astype(f32)).astype(here.dtype)

    def start(self):
        self.pair.start()

    @staticmethod
    def middle(*units):
        p = units[0].p
        for u in units:
            u.pair.wait_recv()
        if p.square:
            for n, m in enumerate((p.far, p.near)):
                for u in units:
                    u.add(m, u.sib[m])
                    u.first[n].start()
            for u in units:
                u.add(p.side, u.sib[p.side])
        else:
            for n, m in enumerate(p.mates):
                for u in units:
                    u.add(m, u.sib[m])
                    u.first[n].start()

    @staticmethod
    def last(*units):
        p = units[0].p
        if p.square:
            for u in units:
                u.first[0].wait_recv()
                u.add(p.side, u.got[0])
                u.second.start()

    def finish(self):
        p = self.p
        total = self.part[p.chip, p.core].astype(f32) + self.sib[p.chip].astype(f32)
        if p.square:
            self.first[1].wait_recv()
            total += self.got[1].astype(f32)
            self.second.wait_recv()
            total += self.got[2].astype(f32)
        else:
            for i, cp in enumerate(self.first):
                cp.wait_recv()
                total += self.got[i].astype(f32)
        self.out[...] = total
        for cp in [self.pair] + self.first + ([self.second] if p.square else []):
            cp.wait_send()


class Exchange:
    def __init__(self, p, src, dst, rows, send, recv):
        self.p, self.src, self.dst, self.rows = p, src, dst, rows
        self.copies = [
            remote(src.at[dev[1], rows], dst.at[p.z, rows], send.at[k], recv.at[k], dev)
            for k, dev in enumerate(p.line)
            if k > 0
        ]

    def start(self):
        for cp in self.copies:
            cp.start()
        self.dst[self.p.z, self.rows] = self.src[self.p.z, self.rows]

    def wait(self):
        for cp in self.copies:
            cp.wait()


def dot(a, b):
    return lax.dot_general(a, b, (((1,), (0,)), ((), ())), preferred_element_type=f32)


def dot_nt(a, b):
    return lax.dot_general(a, b, (((1,), (1,)), ((), ())), preferred_element_type=f32)


def dot_tn(a, b):
    return lax.dot_general(a, b, (((0,), (0,)), ((), ())), preferred_element_type=f32)


def norm_parts(rows):
    centred = rows - jnp.mean(rows, axis=-1, keepdims=True)
    inverse = lax.rsqrt(jnp.mean(centred * centred, axis=-1, keepdims=True) + EPS)
    return centred * inverse, inverse


def norm_back(grad, normed, inverse):
    first = jnp.mean(grad, axis=-1, keepdims=True)
    second = normed * jnp.mean(grad * normed, axis=-1, keepdims=True)
    return inverse * (grad - first - second)


def regroup(per, group, nz, block, j):
    row = lax.broadcasted_iota(jnp.int32, (per, nz * block), 0).astype(f32)
    col = lax.broadcasted_iota(jnp.int32, (per, nz * block), 1).astype(f32)
    plane = jnp.floor((row + 0.5) * (1.0 / group))
    return jnp.where(col == row + plane * (block - group) + j * group, 1.0, 0.0).astype(bf16)


def router_softmax(rows, wr, experts):
    lane = lax.broadcasted_iota(jnp.int32, (1, 128), 1)
    logits = jnp.where(lane < experts, dot(rows, wr), -1e30)
    ex = jnp.exp(logits - jnp.max(logits, axis=-1, keepdims=True))
    return ex / jnp.sum(ex, axis=-1, keepdims=True)


def padded(value, rows):
    return jnp.concatenate([value, jnp.zeros((rows - value.shape[0], value.shape[1]), value.dtype)], axis=0)


def layer_tile(wqkv_ref, wout_ref, t):
    d = wout_ref.shape[1]
    part = d // TILES
    return jnp.concatenate(
        [wqkv_ref[:, j * d + t * part : j * d + (t + 1) * part] for j in range(3)]
        + [wout_ref[:, t * part : (t + 1) * part]],
        axis=1,
    )


def route(info, place_ref, image, cap, slots, experts, seq):
    lanes = info.shape[1]
    row = lax.broadcasted_iota(jnp.int32, info.shape, 0)
    lane = lax.broadcasted_iota(jnp.int32, info.shape, 1)
    info = jnp.where(lane < seq, info, jnp.where(row == 0, 1e6, -1.0 - row.astype(f32)))
    cols = jnp.transpose(info)
    rank_c, one_c, two_c = cols[:, 0:1], cols[:, 1:2], cols[:, 2:3]
    rank_r, one_r, two_r = info[0:1, :], info[1:2, :], info[2:3, :]
    earlier = rank_c < rank_r
    count = lambda m: jnp.sum(jnp.where(m, 1.0, 0.0), axis=0, keepdims=True)
    pos_one = count(earlier & (one_c == one_r))
    pos_two = count(earlier & (two_c == two_r)) + count(one_c == two_r)
    code = lambda pos, pick: jnp.where(
        (pos < cap) & (pick >= 0), pick * slots + (pos + image * cap), -1.0
    ).astype(jnp.int32)
    code_one, code_two = code(pos_one, one_r), code(pos_two, two_r)
    for e in range(experts):
        slot = lax.broadcasted_iota(jnp.int32, (slots, lanes), 0) + e * slots
        hit = (slot == code_one) | (slot == code_two)
        place_ref[e * slots : (e + 1) * slots, image * lanes : (image + 1) * lanes] = jnp.where(
            hit, 1.0, 0.0
        ).astype(bf16)


class LineScatter:
    def __init__(self, place, fold, sent, got, send, recv):
        self.p, self.fold, self.sent, self.got = place, fold, sent, got
        self.copies = []
        for k in range(1, place.nz):
            dev = place.line[k]
            self.copies.append(remote(sent.at[dev[1]], got.at[place.z], send.at[k], recv.at[k], dev))

    def start(self, total, group):
        per, thin = total.shape[0], total.shape[1] // self.fold
        nz, block = self.sent.shape[0], self.sent.shape[1]
        low = total.astype(bf16)
        acc = None
        for j in range(self.fold):
            more = dot_tn(regroup(per, group, nz, block, j), low[:, j * thin : (j + 1) * thin])
            acc = more if acc is None else acc + more
        self.sent[...] = acc.astype(bf16).reshape(self.sent.shape)
        for cp in self.copies:
            cp.start()

    def finish(self, group):
        p = self.p
        for cp in self.copies:
            cp.wait()
        total = self.sent[p.z].astype(f32)
        for k in range(1, p.nz):
            total += self.got[p.line_from[k]].astype(f32)
        return jnp.concatenate([total[j * group : (j + 1) * group] for j in range(self.fold)], axis=1)


def expert_gates(p, experts, lo, hi, buf_ref, gs_ref, wr):
    nz, _, d = buf_ref.shape
    count = nz * (hi - lo)
    lane = lax.broadcasted_iota(jnp.int32, (1, 128), 1)
    rp = router_softmax(buf_ref[:, lo:hi, :].reshape(count, d), wr, experts)
    gate = jnp.sum(jnp.where(lane == p.z, rp, 0.0), axis=-1, keepdims=True)
    rows = gs_ref[:, lo:hi, :].reshape(count, d).astype(f32)
    gs_ref[:, lo:hi, :] = (gate * rows).astype(bf16).reshape(nz, hi - lo, d)


def expert_tile(t, lo, hi, wi_ref, wb_ref, buf_ref, gs_ref, act_ref, gh_ref):
    nz, _, d = buf_ref.shape
    count, width = nz * (hi - lo), act_ref.shape[3]
    step = min(256, width)
    k0, k1 = 0.7978845608028654, 0.044715 * 0.7978845608028654
    wi = wi_ref[t].reshape(d, width)
    wb = wb_ref[t].reshape(width, d)
    put = lambda v: v.astype(bf16).reshape(nz, hi - lo, step)
    for n in range(width // step):
        cols = slice(n * step, (n + 1) * step)
        h = dot(buf_ref[:, lo:hi, :].reshape(count, d), wi[:, cols])
        grad = dot_nt(gs_ref[:, lo:hi, :].reshape(count, d), wb[cols])
        h2 = h * h
        th = jnp.tanh(h * (k0 + k1 * h2))
        half = 0.5 * (1.0 + th)
        act_ref[t, :, lo:hi, cols] = put(h * half)
        slope = half + 0.5 * h * (1.0 - th * th) * (k0 + 3.0 * k1 * h2)
        gh_ref[t, :, lo:hi, cols] = put(grad * slope)


def expert_back(
    p, experts, lo, hi, wi_ref, wb_ref, buf_ref, gs_ref, act_ref, gh_ref, wr, eo_ref, sgrad_ref, gr_ref
):
    nz, _, d = buf_ref.shape
    count, width = nz * (hi - lo), act_ref.shape[3]
    lane = lax.broadcasted_iota(jnp.int32, (1, 128), 1)
    mine = jnp.where(lane == p.z, 1.0, 0.0)
    part = lambda ref, *at: ref[at + (slice(None), slice(lo, hi))].reshape(count, ref.shape[-1])
    out = sum(dot(part(act_ref, t), wb_ref[t].reshape(width, d)) for t in range(TILES)).astype(bf16)
    eo_ref[:, lo:hi, :] = out.reshape(nz, hi - lo, d)
    both = jnp.sum(out.astype(f32) * part(gs_ref).astype(f32), axis=-1, keepdims=True)
    contrib = both * (mine - router_softmax(part(buf_ref), wr, experts))
    top = contrib.astype(bf16)
    low = (contrib - top.astype(f32)).astype(bf16)
    grad = sum(dot_nt(part(gh_ref, t), wi_ref[t].reshape(d, width)) for t in range(TILES))
    grad = grad + dot_nt(top, wr) + dot_nt(low, wr)
    sgrad_ref[:, lo:hi, :] = grad.astype(bf16).reshape(nz, hi - lo, d)
    gr_ref[...] += dot_tn(part(buf_ref), top) + dot_tn(part(buf_ref), low)


def block_kernel(
    ndp, nz, cap, experts, fold,
    img_ref, cot_ref, priority_ref, choices_ref, router_ref, gain_one_ref, gain_two_ref,
    wqkv_ref, wout_ref, win_ref, wback_ref,
    wi_hbm, wb_hbm, wl_hbm, mixed_hbm, probs_hbm, att_hbm, res_hbm, out_hbm, gin_hbm, gl_ref, gsm_ref, gi_ref, gb_ref,
    zs_ref, zsm_ref, big_ref, wt_ref, sg_ref, sa_ref, sb_ref, buf_ref, gs_ref, rgrad_ref, ro_ref,
    place_ref,
    pback_ref, sin_ref, sback_ref, xin_ref, xback_ref, lsin_ref, lxin_ref,
    gr_ref, ssm_ref, xsm_ref, zssm_ref, zgsm_ref,
    lsend, lrecv, zsend, zrecv, gsend, grecv, tsend, trecv, ysend, yrecv,
    rsend, rrecv, osend, orecv, esend, erecv, ssend, srecv, usend, urecv, ksem, isem,
):
    p = Place(ndp, nz)
    seq, images, d = img_ref.shape
    rows, lanes = res_hbm.shape[1], place_ref.shape[1] // images
    slots = sa_ref.shape[1]
    chips, part = ndp // 2, d // TILES
    some = d // 128 // TILES
    group, per = wqkv_ref.shape[0], d // ndp
    width = big_ref.shape[4]
    per_back = wback_ref.shape[1]
    lane = lax.broadcasted_iota(jnp.int32, (1, 128), 1)
    low_half = lane < HEAD_DIM
    thin, block = width // fold, zs_ref.shape[2]
    chunk = width // ndp
    saves = []

    def save(src, dst):
        cp = pltpu.make_async_copy(src, dst, ksem.at[2 * TILES + len(saves)])
        cp.start()
        saves.append(cp)
        return cp

    small_ref = gr_ref.at[:128]
    small_ref[...] = jnp.zeros((128, 128), f32)
    small_ref[:experts, :group] = router_ref[...].astype(f32)
    small_ref[experts : experts + 1, :group] = gain_one_ref[...].astype(f32)
    small_ref[experts + 1 : experts + 2, :group] = gain_two_ref[...].astype(f32)
    zsm_ref[p.z] = jnp.transpose(small_ref[...])[: zsm_ref.shape[1]].astype(bf16)
    for n in range(TILES):
        tile = layer_tile(wqkv_ref, wout_ref, n)
        if block == fold * group:
            tile = tile.astype(f32)
            pieces = [tile[:, j * thin : (j + 1) * thin] for j in range(fold)]
            zs_ref[n, p.z] = jnp.concatenate(pieces, axis=0).astype(bf16)
        else:
            zs_ref[n, p.z] = jnp.zeros((block, thin), bf16)
            zs_ref[n, p.z, :group] = tile
    p.greet()

    lines = []
    for n in range(TILES + 1):
        ref = zs_ref.at[n] if n < TILES else zsm_ref
        lines.append(
            [remote(ref.at[p.z], ref.at[p.z], zsend.at[n, k], zrecv.at[n, k], p.line[k]) for k in range(1, nz)]
        )
    for n in (TILES,) + tuple(range(TILES)):
        for cp in lines[n]:
            cp.start()

    layer_units = []
    for n in range(TILES + 1):
        if n < TILES:
            slot = lambda chip, core, n=n: big_ref.at[n, chip, core]
        else:
            slot = lambda chip, core: sg_ref.at[chip * 2 + core]
        layer_units.append(
            PlaneGather(
                p, slot(p.chip, p.core), slot,
                lambda i, n=n: lsend.at[n, i], lambda i, n=n: lrecv.at[n, i],
            )
        )
    expert_units = []
    for t in range(TILES):
        for w, (own, full) in enumerate(((wt_ref, wi_hbm), (wback_ref, wb_hbm))):
            n = t * 2 + w
            expert_units.append(
                PlaneGather(
                    p, own.at[t], lambda chip, core, full=full, t=t: full.at[t, chip * 2 + core],
                    lambda i, n=n: gsend.at[n, i], lambda i, n=n: grecv.at[n, i],
                )
            )
    for t in range(TILES):
        for i in range(ndp):
            wt_ref[t, :, i * chunk : (i + 1) * chunk] = win_ref[
                :, (i * TILES + t) * chunk : (i * TILES + t + 1) * chunk
            ]

    cuts = [i * cap // 16 * 16 for i in range(images)] + [slots]
    parts = [pl.ds(lo, hi - lo) for lo, hi in zip(cuts[:-1], cuts[1:])]
    send_dy = Exchange(p, sb_ref, gs_ref, pl.ds(0, slots), ysend, yrecv)
    sends = [Exchange(p, sa_ref, buf_ref, s, tsend.at[i], trecv.at[i]) for i, s in enumerate(parts)]
    backs = [Exchange(p, sa_ref, rgrad_ref, s, rsend.at[i], rrecv.at[i]) for i, s in enumerate(parts)]
    outs = Exchange(p, sb_ref, ro_ref, pl.ds(0, slots), osend, orecv)
    own_saves = [
        pltpu.make_async_copy(own.at[t], full.at[t, p.dp], ksem.at[t * 2 + w])
        for t in range(TILES)
        for w, (own, full) in enumerate(((wt_ref, wi_hbm), (wback_ref, wb_hbm)))
    ]
    parked = []

    def forward(tok_ref, x_ref, mixed_ref, probs_ref, att_ref, res_ref, info_ref):
        tok_ref[...] = jnp.zeros_like(tok_ref)
        info_ref[...] = jnp.zeros_like(info_ref)
        for i in range(images):
            info_ref[i, 0:1, :seq] = priority_ref[i : i + 1, :].astype(f32)
            info_ref[i, 1:3, :seq] = choices_ref[i].astype(f32)
            route(info_ref[i], place_ref, i, cap, slots, experts, seq)
            tok_ref[i * lanes : i * lanes + rows, :] = padded(cot_ref[:, i, :].astype(f32), rows).astype(bf16)

        def dispatch(out_ref, lo, hi, upto):
            for e in range(experts):
                out_ref[e, lo:hi, :] = dot(
                    place_ref[e * slots + lo : e * slots + hi, :upto], tok_ref[:upto, :]
                ).astype(bf16)

        dispatch(sb_ref, 0, slots, images * lanes)

        def line_done(n):
            for cp in lines[n]:
                cp.wait_recv()
            if n == TILES:
                tall = zsm_ref.shape[1]
                sg_ref[p.dp] = dot(regroup(per, group, nz, tall, 0), zsm_ref[...].reshape(nz * tall, 128)).astype(bf16)
            else:
                flat = zs_ref[n].reshape(nz * block, thin)
                for j in range(fold):
                    big_ref[n, p.chip, p.core, :, j * thin : (j + 1) * thin] = dot(
                        regroup(per, group, nz, block, j), flat
                    ).astype(bf16)
            layer_units[n].start()

        order = (TILES,) + tuple(range(TILES))
        for n in order:
            line_done(n)
        send_dy.start()
        for i, n in enumerate(order[:-1]):
            layer_units[n].middle()
            if i >= 1:
                layer_units[order[i - 1]].last()
        layer_units[order[-1]].middle()
        layer_units[order[-2]].last()
        layer_units[order[-1]].last()
        for t in range(TILES):
            for n in (2 * t, 2 * t + 1):
                expert_units[n].start()
                own_saves[n].start()

        layer_units[TILES].arrive()
        gains = jnp.transpose(sg_ref[...].reshape(d, 128).astype(f32))
        gain_one, gain_two = gains[experts : experts + 1, :], gains[experts + 1 : experts + 2, :]
        normed = []
        for i in range(images):
            x_ref[i] = padded(img_ref[:, i, :].astype(f32), rows)
            normed.append((norm_parts(x_ref[i])[0] * gain_one).astype(bf16))
            mixed_ref[i, rows:, :] = jnp.zeros((lanes - rows, 3 * d), bf16)
        first = jnp.concatenate(normed, axis=0)
        for n in range(TILES):
            layer_units[n].arrive()
            parked.append(save(big_ref.at[n], wl_hbm.at[n]))
            got = dot(first, big_ref[n].reshape(d, width)[:, :d]).astype(bf16)
            mixed_ref[:, :rows, n * d : (n + 1) * d] = got.reshape(images, rows, d)

        valid = lax.broadcasted_iota(jnp.int32, (1, lanes), 1) < seq
        parked.append(save(mixed_ref, mixed_hbm))

        for i in range(images):

            @pl.loop(0, TILES)
            def _(t):
                for u in range(some):
                    n = t * some + u
                    at = lambda part: pl.ds(pl.multiple_of(t * d + (part * some + u) * 128, 128), 128)
                    q, k, v = mixed_ref[i, :rows, at(0)], mixed_ref[i, :, at(1)], mixed_ref[i, :, at(2)]
                    got = []
                    for h in range(2):
                        mask = low_half if h == 0 else ~low_half
                        scores = dot_nt(jnp.where(mask, q, jnp.zeros_like(q)), k) * HEAD_DIM**-0.5
                        scores = jnp.where(valid, scores, -1e30)
                        e = jnp.exp(scores - jnp.max(scores, axis=-1, keepdims=True))
                        prob = (e * (1.0 / jnp.sum(e, axis=-1, keepdims=True))).astype(bf16)
                        probs_ref[i, n * 2 + h] = prob
                        got.append(dot(prob, v))
                    att_ref[i, :, pl.ds(pl.multiple_of(n * 128, 128), 128)] = jnp.where(low_half, got[0], got[1]).astype(bf16)

            added = [dot(att_ref[i], big_ref[t].reshape(d, width)[:, d:]) for t in range(TILES)]
            residual = x_ref[i] + jnp.concatenate(added, axis=1)
            res_ref[i] = residual
            tok_ref[i * lanes : i * lanes + rows, :] = (norm_parts(residual)[0] * gain_two).astype(bf16)
            dispatch(sa_ref, cuts[i], cuts[i + 1], (i + 1) * lanes)
            sends[i].start()
            parked.append(save(probs_ref.at[i], probs_hbm.at[i]))
            parked.append(save(att_ref.at[i], att_hbm.at[i]))
            parked.append(save(res_ref.at[i], res_hbm.at[i]))

        for cp in parked:
            cp.wait()

    pl.run_scoped(
        forward,
        pltpu.VMEM((images * lanes, d), bf16),
        pltpu.VMEM((images, rows, d), f32),
        pltpu.VMEM(mixed_hbm.shape, bf16),
        pltpu.VMEM(probs_hbm.shape, bf16),
        pltpu.VMEM(att_hbm.shape, bf16),
        pltpu.VMEM(res_hbm.shape, f32),
        pltpu.VMEM((images, 8, lanes), f32),
    )

    wr = sg_ref[...].reshape(d, 128)
    expert_sums = []
    for t in range(TILES):
        for w, (mine, sib, got, out) in enumerate(
            ((big_ref, sin_ref, xin_ref, gi_ref), (pback_ref, sback_ref, xback_ref, gb_ref))
        ):
            n = t * 2 + w
            expert_sums.append(
                PlaneScatter(
                    p, mine.at[t], sib.at[t], got.at[t], out.at[t],
                    lambda i, n=n: esend.at[n, i], lambda i, n=n: erecv.at[n, i],
                )
            )
    both = lambda t: expert_sums[2 * t : 2 * t + 2]

    def expert_part(wi_ref, wb_ref, act_ref, gh_ref):
        def fetch(t):
            copies = []
            for w, (src, dst) in enumerate(((wi_hbm, wi_ref), (wb_hbm, wb_ref))):
                n = t * 2 + w
                expert_units[n].arrive()
                own_saves[n].wait()
                copies.append(pltpu.make_async_copy(src.at[t], dst.at[t], isem.at[n]))
                copies[-1].start()
            for cp in copies:
                cp.wait()

        def weight_grads(t):
            flat = lambda v: v.reshape(nz * slots, v.shape[-1])
            got = dot_tn(flat(buf_ref[...]), flat(gh_ref[t]))
            big_ref[t] = got.astype(bf16).reshape(chips, 2, per, width)
            both(t)[0].start()
            got = dot_tn(flat(act_ref[t]), flat(gs_ref[...]))
            pback_ref[t] = got.astype(bf16).reshape(chips, 2, per_back, d)
            both(t)[1].start()

        for u in expert_units:
            u.middle()
        send_dy.wait()
        gr_ref[...] = jnp.zeros_like(gr_ref)
        def forth_and_back(i, lo, hi):
            expert_back(
                p, experts, lo, hi, wi_ref, wb_ref, buf_ref, gs_ref, act_ref, gh_ref, wr, sb_ref, sa_ref, gr_ref
            )
            backs[i].start()

        for i, (lo, hi) in enumerate(zip(cuts[:-1], cuts[1:])):
            sends[i].wait()
            expert_gates(p, experts, lo, hi, buf_ref, gs_ref, wr)
            for t in range(TILES):
                if i == 0:
                    for u in expert_units[2 * t : 2 * t + 2]:
                        u.last()
                    fetch(t)
                expert_tile(t, lo, hi, wi_ref, wb_ref, buf_ref, gs_ref, act_ref, gh_ref)
                if i == images - 1 and t == 0:
                    for u in layer_units + expert_units:
                        u.leave()
                    weight_grads(0)
            if i < images - 1:
                forth_and_back(i, lo, hi)
        PlaneScatter.middle(*both(0))
        weight_grads(1)
        forth_and_back(images - 1, cuts[images - 1], cuts[images])
        PlaneScatter.last(*both(0))
        PlaneScatter.middle(*both(1))
        weight_grads(2)
        for u in both(0):
            u.finish()

    pl.run_scoped(
        expert_part,
        pltpu.VMEM((TILES, ndp, per, width), bf16),
        pltpu.VMEM((TILES, ndp, per_back, d), bf16),
        pltpu.VMEM((TILES, nz, slots, width), bf16),
        pltpu.VMEM((TILES, nz, slots, width), bf16),
    )

    def backward(
        wl_ref, mixed_ref, probs_ref, att_ref, res_ref, gres_ref, branch_ref, gatt_ref, first_ref, tot_ref, lpart_ref,
        psm_ref, tsm_ref, zsent_ref, vec_ref,
    ):
        layer_sums, sum_lines = [], []
        for n in range(TILES + 1):
            mine, sib, got, tot, zs, zg = (
                (lpart_ref.at[n], lsin_ref.at[n], lxin_ref.at[n], tot_ref.at[n], zsent_ref.at[n], zs_ref.at[n])
                if n < TILES
                else (psm_ref, ssm_ref, xsm_ref, tsm_ref, zssm_ref, zgsm_ref)
            )
            layer_sums.append(
                PlaneScatter(p, mine, sib, got, tot, lambda i, n=n: ssend.at[n, i], lambda i, n=n: srecv.at[n, i])
            )
            sum_lines.append(LineScatter(p, fold if n < TILES else 1, zs, zg, usend.at[n], urecv.at[n]))

        copies = [
            pltpu.make_async_copy(src, dst, isem.at[n])
            for n, (src, dst) in enumerate(
                (
                    (res_hbm, res_ref), (wl_hbm, wl_ref), (att_hbm, att_ref), (mixed_hbm, mixed_ref),
                    (probs_hbm, probs_ref),
                )
            )
        ]
        for cp in copies:
            cp.start()
        PlaneScatter.middle(*both(TILES - 1))
        gains = jnp.transpose(wr.astype(f32))
        gain_one, gain_two = gains[experts : experts + 1, :], gains[experts + 1 : experts + 2, :]
        normed_one = lambda i: norm_parts(padded(img_ref[:, i, :].astype(f32), rows))
        for i in range(images):
            first_ref[i] = (normed_one(i)[0] * gain_one).astype(bf16)
        for cp in copies:
            cp.wait()
        for ex in backs:
            ex.wait()
        outs.start()
        vec_two = jnp.zeros((1, d), f32)
        for i in range(images):
            hits = place_ref[:, i * lanes : (i + 1) * lanes]
            grad_second = dot_tn(hits, rgrad_ref[...].reshape(experts * slots, d))[:rows]
            normed, inverse = norm_parts(res_ref[i])
            vec_two += jnp.sum(grad_second * normed, axis=0, keepdims=True)
            grad = padded(cot_ref[:, i, :].astype(f32), rows) + norm_back(grad_second * gain_two, normed, inverse)
            gres_ref[i] = grad
            branch = grad.astype(bf16)
            branch_ref[i] = branch
            gatt_ref[i] = sum(
                dot_nt(branch[:, t * part : (t + 1) * part], wl_ref[t].reshape(d, width)[:, d:])
                for t in range(TILES)
            ).astype(bf16)

        scale = HEAD_DIM**-0.5

        PlaneScatter.last(*both(TILES - 2))
        flat = lambda v: v.reshape(images * rows, v.shape[-1])
        for t in range(TILES):

            @pl.loop(0, some)
            def _(u):
                at = lambda j: pl.ds(pl.multiple_of(t * d + j * part + u * 128, 128), 128)
                here = pl.ds(pl.multiple_of(t * part + u * 128, 128), 128)
                for i in range(images):
                    q, k, v = mixed_ref[i, :rows, at(0)], mixed_ref[i, :, at(1)], mixed_ref[i, :, at(2)]
                    ga = gatt_ref[i, :, here]
                    gq, gk, gv = [], [], []
                    for h in range(2):
                        mask = low_half if h == 0 else ~low_half
                        prob = probs_ref[i, (t * some + u) * 2 + h]
                        gv.append(dot_tn(prob, ga)[:rows])
                        weighting = dot_nt(jnp.where(mask, ga, jnp.zeros_like(ga)), v)
                        wide = prob.astype(f32)
                        scores = wide * (weighting - jnp.sum(wide * weighting, axis=-1, keepdims=True))
                        scores = scores.astype(bf16)
                        gq.append(dot(scores, k))
                        gk.append(dot_tn(scores, q)[:rows])
                    pick = lambda pair, by: jnp.where(low_half, pair[0], pair[1]) * by
                    mixed_ref[i, :rows, at(0)] = pick(gq, scale).astype(bf16)
                    mixed_ref[i, :rows, at(1)] = pick(gk, scale).astype(bf16)
                    mixed_ref[i, :rows, at(2)] = pick(gv, 1.0).astype(bf16)

            got = dot_tn(flat(first_ref[...]), flat(mixed_ref[:, :rows, t * d : (t + 1) * d]))
            lpart_ref[t, :, :, :, :d] = got.astype(bf16).reshape(chips, 2, per, d)
            more = dot_tn(flat(att_ref[...]), flat(branch_ref[:, :, t * part : (t + 1) * part]))
            lpart_ref[t, :, :, :, d:] = more.astype(bf16).reshape(chips, 2, per, part)
            layer_sums[t].start()
            if t == 0:
                PlaneScatter.last(*both(TILES - 1))
            if t >= 1:
                PlaneScatter.middle(layer_sums[t - 1])
            if t >= 2:
                PlaneScatter.last(layer_sums[t - 2])

        def to_line(n):
            layer_sums[n].finish()
            ref = tot_ref.at[n] if n < TILES else tsm_ref
            if n < TILES:
                sum_lines[n].start(ref[...], group)
            else:
                for k in range(nz):
                    zssm_ref[k, :group, :] = tsm_ref[k * group : (k + 1) * group, :]
                for cp in sum_lines[n].copies:
                    cp.start()

        vec_one = jnp.zeros((1, d), f32)
        for i in range(images):
            grad_first = sum(
                dot_nt(mixed_ref[i, :rows, t * d : (t + 1) * d], wl_ref[t].reshape(d, width)[:, :d])
                for t in range(TILES)
            )
            normed, inverse = normed_one(i)
            vec_one += jnp.sum(grad_first * normed, axis=0, keepdims=True)
            gres_ref[i] += norm_back(grad_first * gain_one, normed, inverse)
            save(gres_ref.at[i], gin_hbm.at[i])
            if i == 0:
                PlaneScatter.middle(layer_sums[TILES - 1])
                PlaneScatter.last(layer_sums[TILES - 2])
                to_line(0)

        for n in range(1, TILES):
            for u in both(n):
                u.finish()
        vec_ref[0:1, :] = vec_one
        vec_ref[1:2, :] = vec_two
        cols = jnp.transpose(vec_ref[...])
        small = jnp.where(
            lane == experts, cols[:, 0:1], jnp.where(lane == experts + 1, cols[:, 1:2], gr_ref[...])
        )
        psm_ref[...] = small.reshape(chips, 2, per, 128)
        layer_sums[TILES].start()
        PlaneScatter.last(layer_sums[TILES - 1])
        PlaneScatter.middle(layer_sums[TILES])
        for n in range(1, TILES - 1):
            to_line(n)
        outs.wait()

        def output(i):
            second = (norm_parts(res_ref[i])[0] * gain_two).astype(bf16)
            rp = router_softmax(second, wr, experts)
            total = res_ref[i]
            for e in range(experts):
                hits = place_ref[e * slots : (e + 1) * slots, i * lanes : (i + 1) * lanes]
                gate = jnp.sum(jnp.where(lane == e, rp, 0.0), axis=-1, keepdims=True)
                total = total + gate * dot_tn(hits, ro_ref[e])[:rows]
            gatt_ref[i] = total.astype(bf16)
            save(gatt_ref.at[i], out_hbm.at[i])

        output(0)
        PlaneScatter.last(layer_sums[TILES])
        to_line(TILES - 1)
        to_line(TILES)
        for i in range(1, images):
            output(i)
        for n in range(TILES):
            gl_ref[:, n * width : (n + 1) * width] = sum_lines[n].finish(group)[:group]
        gsm_ref[...] = sum_lines[TILES].finish(zssm_ref.shape[1])[:group]

        for group_of in lines:
            for cp in group_of:
                cp.wait_send()
        for cp in saves:
            if not any(cp is done for done in parked):
                cp.wait()

    pl.run_scoped(
        backward,
        pltpu.VMEM(wl_hbm.shape, bf16),
        pltpu.VMEM(mixed_hbm.shape, bf16),
        pltpu.VMEM(probs_hbm.shape, bf16),
        pltpu.VMEM(att_hbm.shape, bf16),
        pltpu.VMEM(res_hbm.shape, f32),
        pltpu.VMEM((images, rows, d), f32),
        pltpu.VMEM((images, rows, d), bf16),
        pltpu.VMEM((images, rows, d), bf16),
        pltpu.VMEM((images, rows, d), bf16),
        pltpu.VMEM((TILES, per, width), f32),
        pltpu.VMEM((TILES, chips, 2, per, width), bf16),
        pltpu.VMEM((chips, 2, per, 128), f32),
        pltpu.VMEM((per, 128), f32),
        pltpu.VMEM(zs_ref.shape, bf16),
        pltpu.VMEM((8, d), f32),
    )


def block(ndp, nz, cap, slots, images, cotangent, priority, choices, router, gain_one, gain_two, wqkv, wout, win, wback):
    seq, count, d = images.shape
    experts = router.shape[0]
    rows, lanes = up(seq, 16), up(seq, 128)
    group, per, width = wqkv.shape[0], d // ndp, 4 * d // TILES
    per_back, chips = wback.shape[1], ndp // 2
    fold = 16 // math.gcd(group, 16)
    if width // fold % 128:
        fold = 1
    tall, short = up(group, 16), up(group, 8)
    line = fold * group if fold * group % 16 == 0 else tall
    shape, vm = jax.ShapeDtypeStruct, pltpu.VMEM
    dma = lambda *dims: [pltpu.SemaphoreType.DMA(dims)] * 2
    ng, ns, nb = PlaneGather.sems(ndp), PlaneScatter.sems(ndp), chips - 1
    return pl.pallas_call(
        partial(block_kernel, ndp, nz, cap, experts, fold),
        out_shape=(
            shape((TILES, ndp, per, width), bf16),
            shape((TILES, ndp, per_back, d), bf16),
            shape((TILES, chips, 2, per, width), bf16),
            shape((count, lanes, 3 * d), bf16),
            shape((count, d // HEAD_DIM, rows, lanes), bf16),
            shape((count, rows, d), bf16),
            shape((count, rows, d), f32),
            shape((count, rows, d), bf16),
            shape((count, rows, d), f32),
            shape((group, 4 * d), f32),
            shape((group, 128), f32),
            shape((TILES, per, width), f32),
            shape((TILES, per_back, d), f32),
        ),
        in_specs=[VM] * 11,
        out_specs=(ANY,) * 9 + (VM,) * 4,
        scratch_shapes=[
            vm((TILES, nz, line, width // fold), bf16),
            vm((nz, tall, 128), bf16),
            vm((TILES, chips, 2, per, width), bf16),
            vm((TILES, per, width), bf16),
            vm((ndp, per, 128), bf16),
        ]
        + [vm((nz, slots, d), bf16)] * 6
        + [
            vm((experts * slots, count * lanes), bf16),
            vm((TILES, chips, 2, per_back, d), bf16),
            vm((TILES, chips, per, width), bf16),
            vm((TILES, chips, per_back, d), bf16),
            vm((TILES, nb, per, width), bf16),
            vm((TILES, nb, per_back, d), bf16),
            vm((TILES, chips, per, width), bf16),
            vm((TILES, nb, per, width), bf16),
            vm((d, 128), f32),
            vm((chips, per, 128), f32),
            vm((nb, per, 128), f32),
            vm((nz, short, 128), f32),
            vm((nz, short, 128), f32),
        ]
        + dma(TILES + 1, ng) + dma(TILES + 1, nz) + dma(2 * TILES, ng) + dma(count, nz) + dma(nz)
        + dma(count, nz) + dma(nz) + dma(2 * TILES, ns) + dma(TILES + 1, ns) + dma(TILES + 1, nz)
        + [
            pltpu.SemaphoreType.DMA((3 * TILES + 1 + 5 * count,)),
            pltpu.SemaphoreType.DMA((2 * TILES,)),
        ],
        compiler_params=pltpu.CompilerParams(
            collective_id=0, has_side_effects=True, vmem_limit_bytes=VMEM_BYTES
        ),
        name="block",
    )(images, cotangent, priority, choices, router, gain_one, gain_two, wqkv, wout, win, wback)


def settle_kernel(
    experts,
    out_ref, gin_ref, gl_ref, gsm_ref, gi_ref, gb_ref,
    output_ref, input_grad_ref, gain_one_ref, qkv_ref, wout_ref, gain_two_ref, router_ref, in_ref, back_ref,
):
    group, d = wout_ref.shape
    part = d // TILES
    ndp, chunk = d // in_ref.shape[0], in_ref.shape[1] // (d // in_ref.shape[0]) // TILES
    seq, images, _ = output_ref.shape
    for i in range(images):
        output_ref[:, i, :] = out_ref[i].astype(f32)[:seq].astype(bf16)
        input_grad_ref[:, i, :] = gin_ref[i, :seq]
    for t in range(TILES):
        for j in range(4):
            piece = gl_ref[:, t * 4 * part + j * part : t * 4 * part + (j + 1) * part]
            if j < 3:
                qkv_ref[:, j * d + t * part : j * d + (t + 1) * part] = piece
            else:
                wout_ref[:, t * part : (t + 1) * part] = piece
        for i in range(ndp):
            in_ref[:, (i * TILES + t) * chunk : (i * TILES + t + 1) * chunk] = gi_ref[
                t, :, i * chunk : (i + 1) * chunk
            ]
    small = jnp.transpose(padded(gsm_ref[...], 128))[:, :group]
    router_ref[...] = small[:experts]
    gain_one_ref[...] = small[experts : experts + 1]
    gain_two_ref[...] = small[experts + 1 : experts + 2]
    back_ref[...] = gb_ref[...]


def settle(experts, seq, out, gin, gl, gsm, gi, gb):
    group, d, count = gl.shape[0], out.shape[2], out.shape[0]
    shape = jax.ShapeDtypeStruct
    return pl.pallas_call(
        partial(settle_kernel, experts),
        out_shape=(
            shape((seq, count, d), bf16), shape((seq, count, d), f32), shape((1, group), f32),
            shape((group, 3 * d), f32), shape((group, d), f32), shape((1, group), f32), shape((experts, group), f32),
            shape((gi.shape[1], gi.shape[0] * gi.shape[2]), f32), shape(gb.shape, f32),
        ),
        in_specs=[VM] * 6,
        out_specs=(VM,) * 9,
        compiler_params=pltpu.CompilerParams(vmem_limit_bytes=VMEM_BYTES),
        name="settle",
    )(out, gin, gl, gsm, gi, gb)


def per_device(ndp, nz, images, gain_one, w_qkv, w_out, gain_two, w_router, w_in, w_back, choices, priority, cotangent):
    count, seq, d = images.shape
    group, experts = w_router.shape
    ff = w_in.shape[2]
    cap = (42 * seq + 20 * experts - 1) // (20 * experts)
    slots = up(count * cap, 16)
    chunk = ff // ndp // TILES
    images, cotangent = images.transpose(1, 0, 2), cotangent.transpose(1, 0, 2)
    out, gin, gl, gsm, gi, gb = block(
        ndp, nz, cap, slots, images, cotangent, priority, choices.transpose(0, 2, 1),
        w_router.T, gain_one[None], gain_two[None],
        w_qkv, w_out, w_in[0], w_back[0].reshape(TILES, chunk, d),
    )[7:]
    out, gin, gain_one, qkv, wout, gain_two, router, gi, gb = settle(
        experts, seq, out, gin, gl, gsm, gi, gb
    )
    return (
        out.transpose(1, 0, 2), gin.transpose(1, 0, 2), gain_one[0], qkv, wout, gain_two[0], router.T,
        gi.reshape(1, d // ndp, ff), gb.reshape(1, ff // ndp, d),
    )


def solution(mesh):
    ndp, nz = mesh.shape["dp"], mesh.shape["fsdp"]
    both = ("dp", "fsdp")
    tokens, rows, expert_rows = P(both, None, None), P(both, None), P("fsdp", "dp", None)
    return jax.shard_map(
        partial(per_device, ndp, nz),
        mesh=mesh,
        in_specs=(tokens, P(both), rows, rows, P(both), rows, expert_rows, expert_rows, tokens, rows, tokens),
        out_specs=(tokens, tokens, P(both), rows, rows, P(both), rows, expert_rows, expert_rows),
        check_vma=False,
    )
```

```python
import math
from functools import partial

import jax
import jax.numpy as jnp
from jax import lax
from jax.experimental import pallas as pl
from jax.experimental.pallas import tpu as pltpu
from jax.sharding import PartitionSpec as P

f32, bf16 = jnp.float32, jnp.bfloat16
MESH = pl.DeviceIdType.MESH
ANY = pl.BlockSpec(memory_space=pl.ANY)
VM = pl.BlockSpec(memory_space=pltpu.VMEM)
HEAD_DIM = 64
EPS = 1e-6
TILES = 3
VMEM_BYTES = 63 << 20


def up(value, unit):
    return -(-value // unit) * unit


class Place:
    def __init__(self, ndp, nz):
        self.ndp, self.nz, self.chips = ndp, nz, ndp // 2
        self.dp = lax.axis_index("dp")
        self.z = lax.axis_index("fsdp")
        self.core = lax.rem(self.dp, 2)
        self.chip = self.dp // 2
        self.square = self.chips == 4
        if self.square:
            a, b, c = self.chip // 2, lax.rem(self.chip, 2), self.core
            self.near = lax.rem(a + 1 - c, 2) * 2 + lax.rem(b + c, 2)
            self.side = lax.rem(a + c, 2) * 2 + lax.rem(b + 1 - c, 2)
            self.far = (1 - a) * 2 + (1 - b)
            self.mates = [self.near, self.side, self.far]
        else:
            self.mates = [lax.rem(self.chip + k, self.chips) for k in range(1, self.chips)]

        self.other = 1 - self.core
        self.sib = (self.chip * 2 + self.other, self.z)
        self.mate_devs = [(m * 2 + self.core, self.z) for m in self.mates]
        self.plane = [self.sib] + (self.mate_devs[:2] if self.square else self.mate_devs)
        self.behind = [lax.rem(self.chip + self.chips - k, self.chips) for k in range(1, self.chips)]
        self.line = [(self.dp, lax.rem(self.z + k, nz)) for k in range(nz)]
        self.line_from = [lax.rem(self.z + nz - k, nz) for k in range(nz)]

    def greet(self):
        bar = pltpu.get_barrier_semaphore()
        there = self.plane + self.line[1:]
        for dev in there:
            pl.semaphore_signal(bar, inc=1, device_id=dev, device_id_type=MESH)
        pl.semaphore_wait(bar, len(there))


def remote(src, dst, send, recv, dev):
    return pltpu.make_async_remote_copy(
        src_ref=src, dst_ref=dst, send_sem=send, recv_sem=recv, device_id=dev, device_id_type=MESH
    )


class PlaneGather:
    def __init__(self, place, own, slot, send, recv):
        self.p = p = place
        mine = slot(p.chip, p.core)
        self.to_sib = remote(own, mine, send(0), recv(0), p.sib)
        if p.square:
            self.first = [
                remote(own, mine, send(1 + i), recv(1 + i), p.mate_devs[i]) for i in range(2)
            ]
            side = slot(p.side, p.core)
            self.relay = remote(side, side, send(3), recv(3), p.mate_devs[0])
            back, n = p.mates, 4
        else:
            self.first = [
                remote(own, mine, send(1 + i), recv(1 + i), dev) for i, dev in enumerate(p.mate_devs)
            ]
            back, n = p.behind, 1 + len(p.mates)
        self.share = [
            remote(slot(m, p.core), slot(m, p.core), send(n + i), recv(n + i), p.sib)
            for i, m in enumerate(back)
        ]

    @staticmethod
    def sems(ndp):
        chips = ndp // 2
        return 7 if chips == 4 else 1 + 2 * (chips - 1)

    def start(self):
        for cp in self.first:
            cp.start()
        self.to_sib.start()

    def middle(self):
        if self.p.square:
            self.first[1].wait_recv()
            self.relay.start()
            self.share[1].start()
            self.first[0].wait_recv()
            self.share[0].start()
        else:
            for f, s in zip(self.first, self.share):
                f.wait_recv()
                s.start()

    def last(self):
        if self.p.square:
            self.relay.wait_recv()
            self.share[2].start()

    def arrive(self):
        self.to_sib.wait_recv()
        for s in self.share:
            s.wait_recv()

    def leave(self):
        for cp in [self.to_sib] + self.share + self.first + ([self.relay] if self.p.square else []):
            cp.wait_send()


class PlaneScatter:
    def __init__(self, place, part, sib, got, out, send, recv):
        self.p, self.part, self.sib, self.got, self.out = place, part, sib, got, out
        p = place
        self.pair = remote(part.at[:, p.other], sib, send(0), recv(0), p.sib)
        at = lambda m: part.at[m, p.core]
        if p.square:
            self.first = [
                remote(at(p.far), got.at[0], send(1), recv(1), p.mate_devs[0]),
                remote(at(p.near), got.at[1], send(2), recv(2), p.mate_devs[0]),
            ]
            self.second = remote(at(p.side), got.at[2], send(3), recv(3), p.mate_devs[1])
        else:
            self.first = [
                remote(at(m), got.at[i], send(1 + i), recv(1 + i), p.mate_devs[i])
                for i, m in enumerate(p.mates)
            ]

    @staticmethod
    def sems(ndp):
        chips = ndp // 2
        return 4 if chips == 4 else chips

    def add(self, m, more):
        here = self.part.at[m, self.p.core]
        here[...] = (here[...].astype(f32) + more.astype(f32)).astype(here.dtype)

    def start(self):
        self.pair.start()

    @staticmethod
    def middle(*units):
        p = units[0].p
        for u in units:
            u.pair.wait_recv()
        if p.square:
            for n, m in enumerate((p.far, p.near)):
                for u in units:
                    u.add(m, u.sib[m])
                    u.first[n].start()
            for u in units:
                u.add(p.side, u.sib[p.side])
        else:
            for n, m in enumerate(p.mates):
                for u in units:
                    u.add(m, u.sib[m])
                    u.first[n].start()

    @staticmethod
    def last(*units):
        p = units[0].p
        if p.square:
            for u in units:
                u.first[0].wait_recv()
                u.add(p.side, u.got[0])
                u.second.start()

    def finish(self):
        p = self.p
        total = self.part[p.chip, p.core].astype(f32) + self.sib[p.chip].astype(f32)
        if p.square:
            self.first[1].wait_recv()
            total += self.got[1].astype(f32)
            self.second.wait_recv()
            total += self.got[2].astype(f32)
        else:
            for i, cp in enumerate(self.first):
                cp.wait_recv()
                total += self.got[i].astype(f32)
        self.out[...] = total
        for cp in [self.pair] + self.first + ([self.second] if p.square else []):
            cp.wait_send()


class Exchange:
    def __init__(self, p, src, dst, rows, send, recv):
        self.p, self.src, self.dst, self.rows = p, src, dst, rows
        self.copies = [
            remote(src.at[dev[1], rows], dst.at[p.z, rows], send.at[k], recv.at[k], dev)
            for k, dev in enumerate(p.line)
            if k > 0
        ]

    def start(self):
        for cp in self.copies:
            cp.start()
        self.dst[self.p.z, self.rows] = self.src[self.p.z, self.rows]

    def wait(self):
        for cp in self.copies:
            cp.wait()


def dot(a, b):
    return lax.dot_general(a, b, (((1,), (0,)), ((), ())), preferred_element_type=f32)


def dot_nt(a, b):
    return lax.dot_general(a, b, (((1,), (1,)), ((), ())), preferred_element_type=f32)


def dot_tn(a, b):
    return lax.dot_general(a, b, (((0,), (0,)), ((), ())), preferred_element_type=f32)


def norm_parts(rows):
    centred = rows - jnp.mean(rows, axis=-1, keepdims=True)
    inverse = lax.rsqrt(jnp.mean(centred * centred, axis=-1, keepdims=True) + EPS)
    return centred * inverse, inverse


def norm_back(grad, normed, inverse):
    first = jnp.mean(grad, axis=-1, keepdims=True)
    second = normed * jnp.mean(grad * normed, axis=-1, keepdims=True)
    return inverse * (grad - first - second)


def regroup(per, group, nz, block, j):
    row = lax.broadcasted_iota(jnp.int32, (per, nz * block), 0).astype(f32)
    col = lax.broadcasted_iota(jnp.int32, (per, nz * block), 1).astype(f32)
    plane = jnp.floor((row + 0.5) * (1.0 / group))
    return jnp.where(col == row + plane * (block - group) + j * group, 1.0, 0.0).astype(bf16)


def router_softmax(rows, wr, experts):
    lane = lax.broadcasted_iota(jnp.int32, (1, 128), 1)
    logits = jnp.where(lane < experts, dot(rows, wr), -1e30)
    ex = jnp.exp(logits - jnp.max(logits, axis=-1, keepdims=True))
    return ex / jnp.sum(ex, axis=-1, keepdims=True)


def padded(value, rows):
    return jnp.concatenate([value, jnp.zeros((rows - value.shape[0], value.shape[1]), value.dtype)], axis=0)


def layer_tile(wqkv_ref, wout_ref, t):
    d = wout_ref.shape[1]
    part = d // TILES
    return jnp.concatenate(
        [wqkv_ref[:, j * d + t * part : j * d + (t + 1) * part] for j in range(3)]
        + [wout_ref[:, t * part : (t + 1) * part]],
        axis=1,
    )


def route(info, place_ref, image, cap, slots, experts, seq):
    lanes = info.shape[1]
    row = lax.broadcasted_iota(jnp.int32, info.shape, 0)
    lane = lax.broadcasted_iota(jnp.int32, info.shape, 1)
    info = jnp.where(lane < seq, info, jnp.where(row == 0, 1e6, -1.0 - row.astype(f32)))
    cols = jnp.transpose(info)
    rank_c, one_c, two_c = cols[:, 0:1], cols[:, 1:2], cols[:, 2:3]
    rank_r, one_r, two_r = info[0:1, :], info[1:2, :], info[2:3, :]
    earlier = rank_c < rank_r
    count = lambda m: jnp.sum(jnp.where(m, 1.0, 0.0), axis=0, keepdims=True)
    pos_one = count(earlier & (one_c == one_r))
    pos_two = count(earlier & (two_c == two_r)) + count(one_c == two_r)
    code = lambda pos, pick: jnp.where(
        (pos < cap) & (pick >= 0), pick * slots + (pos + image * cap), -1.0
    ).astype(jnp.int32)
    code_one, code_two = code(pos_one, one_r), code(pos_two, two_r)
    for e in range(experts):
        slot = lax.broadcasted_iota(jnp.int32, (slots, lanes), 0) + e * slots
        hit = (slot == code_one) | (slot == code_two)
        place_ref[e * slots : (e + 1) * slots, image * lanes : (image + 1) * lanes] = jnp.where(
            hit, 1.0, 0.0
        ).astype(bf16)


class LineScatter:
    def __init__(self, place, fold, sent, got, send, recv):
        self.p, self.fold, self.sent, self.got = place, fold, sent, got
        self.copies = []
        for k in range(1, place.nz):
            dev = place.line[k]
            self.copies.append(remote(sent.at[dev[1]], got.at[place.z], send.at[k], recv.at[k], dev))

    def start(self, total, group):
        per, thin = total.shape[0], total.shape[1] // self.fold
        nz, block = self.sent.shape[0], self.sent.shape[1]
        low = total.astype(bf16)
        acc = None
        for j in range(self.fold):
            more = dot_tn(regroup(per, group, nz, block, j), low[:, j * thin : (j + 1) * thin])
            acc = more if acc is None else acc + more
        self.sent[...] = acc.astype(bf16).reshape(self.sent.shape)
        for cp in self.copies:
            cp.start()

    def finish(self, group):
        p = self.p
        for cp in self.copies:
            cp.wait()
        total = self.sent[p.z].astype(f32)
        for k in range(1, p.nz):
            total += self.got[p.line_from[k]].astype(f32)
        return jnp.concatenate([total[j * group : (j + 1) * group] for j in range(self.fold)], axis=1)


def expert_gates(p, experts, lo, hi, buf_ref, gs_ref, wr):
    nz, _, d = buf_ref.shape
    count = nz * (hi - lo)
    lane = lax.broadcasted_iota(jnp.int32, (1, 128), 1)
    rp = router_softmax(buf_ref[:, lo:hi, :].reshape(count, d), wr, experts)
    gate = jnp.sum(jnp.where(lane == p.z, rp, 0.0), axis=-1, keepdims=True)
    rows = gs_ref[:, lo:hi, :].reshape(count, d).astype(f32)
    gs_ref[:, lo:hi, :] = (gate * rows).astype(bf16).reshape(nz, hi - lo, d)


def expert_tile(t, lo, hi, wi_ref, wb_ref, buf_ref, gs_ref, act_ref, gh_ref):
    nz, _, d = buf_ref.shape
    count, width = nz * (hi - lo), act_ref.shape[3]
    step = min(256, width)
    k0, k1 = 0.7978845608028654, 0.044715 * 0.7978845608028654
    wi = wi_ref[t].reshape(d, width)
    wb = wb_ref[t].reshape(width, d)
    put = lambda v: v.astype(bf16).reshape(nz, hi - lo, step)
    for n in range(width // step):
        cols = slice(n * step, (n + 1) * step)
        h = dot(buf_ref[:, lo:hi, :].reshape(count, d), wi[:, cols])
        grad = dot_nt(gs_ref[:, lo:hi, :].reshape(count, d), wb[cols])
        h2 = h * h
        th = jnp.tanh(h * (k0 + k1 * h2))
        half = 0.5 * (1.0 + th)
        act_ref[t, :, lo:hi, cols] = put(h * half)
        slope = half + 0.5 * h * (1.0 - th * th) * (k0 + 3.0 * k1 * h2)
        gh_ref[t, :, lo:hi, cols] = put(grad * slope)


def expert_back(
    p, experts, lo, hi, wi_ref, wb_ref, buf_ref, gs_ref, act_ref, gh_ref, wr, eo_ref, sgrad_ref, gr_ref
):
    nz, _, d = buf_ref.shape
    count, width = nz * (hi - lo), act_ref.shape[3]
    lane = lax.broadcasted_iota(jnp.int32, (1, 128), 1)
    mine = jnp.where(lane == p.z, 1.0, 0.0)
    part = lambda ref, *at: ref[at + (slice(None), slice(lo, hi))].reshape(count, ref.shape[-1])
    out = sum(dot(part(act_ref, t), wb_ref[t].reshape(width, d)) for t in range(TILES)).astype(bf16)
    eo_ref[:, lo:hi, :] = out.reshape(nz, hi - lo, d)
    both = jnp.sum(out.astype(f32) * part(gs_ref).astype(f32), axis=-1, keepdims=True)
    contrib = both * (mine - router_softmax(part(buf_ref), wr, experts))
    top = contrib.astype(bf16)
    low = (contrib - top.astype(f32)).astype(bf16)
    grad = sum(dot_nt(part(gh_ref, t), wi_ref[t].reshape(d, width)) for t in range(TILES))
    grad = grad + dot_nt(top, wr) + dot_nt(low, wr)
    sgrad_ref[:, lo:hi, :] = grad.astype(bf16).reshape(nz, hi - lo, d)
    gr_ref[...] += dot_tn(part(buf_ref), top) + dot_tn(part(buf_ref), low)


def block_kernel(
    ndp, nz, cap, experts, fold,
    img_ref, cot_ref, priority_ref, choices_ref, router_ref, gain_one_ref, gain_two_ref,
    wqkv_ref, wout_ref, win_ref, wback_ref,
    wi_hbm, wb_hbm, wl_hbm, mixed_hbm, probs_hbm, att_hbm, res_hbm, out_hbm, gin_hbm, gl_ref, gsm_ref, gi_ref, gb_ref,
    zs_ref, zsm_ref, big_ref, wt_ref, sg_ref, sa_ref, sb_ref, buf_ref, gs_ref, rgrad_ref, ro_ref,
    place_ref,
    pback_ref, sin_ref, sback_ref, xin_ref, xback_ref, lsin_ref, lxin_ref,
    gr_ref, ssm_ref, xsm_ref, zssm_ref, zgsm_ref,
    lsend, lrecv, zsend, zrecv, gsend, grecv, tsend, trecv, ysend, yrecv,
    rsend, rrecv, osend, orecv, esend, erecv, ssend, srecv, usend, urecv, ksem, isem,
):
    p = Place(ndp, nz)
    seq, images, d = img_ref.shape
    rows, lanes = res_hbm.shape[1], place_ref.shape[1] // images
    slots = sa_ref.shape[1]
    chips, part = ndp // 2, d // TILES
    some = d // 128 // TILES
    group, per = wqkv_ref.shape[0], d // ndp
    width = big_ref.shape[4]
    per_back = wback_ref.shape[1]
    lane = lax.broadcasted_iota(jnp.int32, (1, 128), 1)
    low_half = lane < HEAD_DIM
    thin, block = width // fold, zs_ref.shape[2]
    chunk = width // ndp
    saves = []

    def save(src, dst):
        cp = pltpu.make_async_copy(src, dst, ksem.at[2 * TILES + len(saves)])
        cp.start()
        saves.append(cp)
        return cp

    small_ref = gr_ref.at[:128]
    small_ref[...] = jnp.zeros((128, 128), f32)
    small_ref[:experts, :group] = router_ref[...].astype(f32)
    small_ref[experts : experts + 1, :group] = gain_one_ref[...].astype(f32)
    small_ref[experts + 1 : experts + 2, :group] = gain_two_ref[...].astype(f32)
    zsm_ref[p.z] = jnp.transpose(small_ref[...])[: zsm_ref.shape[1]].astype(bf16)
    for n in range(TILES):
        tile = layer_tile(wqkv_ref, wout_ref, n)
        if block == fold * group:
            tile = tile.astype(f32)
            pieces = [tile[:, j * thin : (j + 1) * thin] for j in range(fold)]
            zs_ref[n, p.z] = jnp.concatenate(pieces, axis=0).astype(bf16)
        else:
            zs_ref[n, p.z] = jnp.zeros((block, thin), bf16)
            zs_ref[n, p.z, :group] = tile
    p.greet()

    lines = []
    for n in range(TILES + 1):
        ref = zs_ref.at[n] if n < TILES else zsm_ref
        lines.append(
            [remote(ref.at[p.z], ref.at[p.z], zsend.at[n, k], zrecv.at[n, k], p.line[k]) for k in range(1, nz)]
        )
    for n in (TILES,) + tuple(range(TILES)):
        for cp in lines[n]:
            cp.start()

    layer_units = []
    for n in range(TILES + 1):
        if n < TILES:
            slot = lambda chip, core, n=n: big_ref.at[n, chip, core]
        else:
            slot = lambda chip, core: sg_ref.at[chip * 2 + core]
        layer_units.append(
            PlaneGather(
                p, slot(p.chip, p.core), slot,
                lambda i, n=n: lsend.at[n, i], lambda i, n=n: lrecv.at[n, i],
            )
        )
    expert_units = []
    for t in range(TILES):
        for w, (own, full) in enumerate(((wt_ref, wi_hbm), (wback_ref, wb_hbm))):
            n = t * 2 + w
            expert_units.append(
                PlaneGather(
                    p, own.at[t], lambda chip, core, full=full, t=t: full.at[t, chip * 2 + core],
                    lambda i, n=n: gsend.at[n, i], lambda i, n=n: grecv.at[n, i],
                )
            )
    for t in range(TILES):
        for i in range(ndp):
            wt_ref[t, :, i * chunk : (i + 1) * chunk] = win_ref[
                :, (i * TILES + t) * chunk : (i * TILES + t + 1) * chunk
            ]

    cuts = [i * cap // 16 * 16 for i in range(images)] + [slots]
    parts = [pl.ds(lo, hi - lo) for lo, hi in zip(cuts[:-1], cuts[1:])]
    send_dy = Exchange(p, sb_ref, gs_ref, pl.ds(0, slots), ysend, yrecv)
    sends = [Exchange(p, sa_ref, buf_ref, s, tsend.at[i], trecv.at[i]) for i, s in enumerate(parts)]
    backs = [Exchange(p, sa_ref, rgrad_ref, s, rsend.at[i], rrecv.at[i]) for i, s in enumerate(parts)]
    outs = Exchange(p, sb_ref, ro_ref, pl.ds(0, slots), osend, orecv)
    own_saves = [
        pltpu.make_async_copy(own.at[t], full.at[t, p.dp], ksem.at[t * 2 + w])
        for t in range(TILES)
        for w, (own, full) in enumerate(((wt_ref, wi_hbm), (wback_ref, wb_hbm)))
    ]
    parked = []

    def forward(tok_ref, x_ref, mixed_ref, probs_ref, att_ref, res_ref, info_ref):
        tok_ref[...] = jnp.zeros_like(tok_ref)
        info_ref[...] = jnp.zeros_like(info_ref)
        for i in range(images):
            info_ref[i, 0:1, :seq] = priority_ref[i : i + 1, :].astype(f32)
            info_ref[i, 1:3, :seq] = choices_ref[i].astype(f32)
            route(info_ref[i], place_ref, i, cap, slots, experts, seq)
            tok_ref[i * lanes : i * lanes + rows, :] = padded(cot_ref[:, i, :].astype(f32), rows).astype(bf16)

        def dispatch(out_ref, lo, hi, upto):
            for e in range(experts):
                out_ref[e, lo:hi, :] = dot(
                    place_ref[e * slots + lo : e * slots + hi, :upto], tok_ref[:upto, :]
                ).astype(bf16)

        dispatch(sb_ref, 0, slots, images * lanes)

        def line_done(n):
            for cp in lines[n]:
                cp.wait_recv()
            if n == TILES:
                tall = zsm_ref.shape[1]
                sg_ref[p.dp] = dot(regroup(per, group, nz, tall, 0), zsm_ref[...].reshape(nz * tall, 128)).astype(bf16)
            else:
                flat = zs_ref[n].reshape(nz * block, thin)
                for j in range(fold):
                    big_ref[n, p.chip, p.core, :, j * thin : (j + 1) * thin] = dot(
                        regroup(per, group, nz, block, j), flat
                    ).astype(bf16)
            layer_units[n].start()

        order = (TILES,) + tuple(range(TILES))
        for n in order:
            line_done(n)
        send_dy.start()
        for i, n in enumerate(order[:-1]):
            layer_units[n].middle()
            if i >= 1:
                layer_units[order[i - 1]].last()
        layer_units[order[-1]].middle()
        layer_units[order[-2]].last()
        layer_units[order[-1]].last()
        for t in range(TILES):
            for n in (2 * t, 2 * t + 1):
                expert_units[n].start()
                own_saves[n].start()

        layer_units[TILES].arrive()
        gains = jnp.transpose(sg_ref[...].reshape(d, 128).astype(f32))
        gain_one, gain_two = gains[experts : experts + 1, :], gains[experts + 1 : experts + 2, :]
        normed = []
        for i in range(images):
            x_ref[i] = padded(img_ref[:, i, :].astype(f32), rows)
            normed.append((norm_parts(x_ref[i])[0] * gain_one).astype(bf16))
            mixed_ref[i, rows:, :] = jnp.zeros((lanes - rows, 3 * d), bf16)
        first = jnp.concatenate(normed, axis=0)
        for n in range(TILES):
            layer_units[n].arrive()
            parked.append(save(big_ref.at[n], wl_hbm.at[n]))
            got = dot(first, big_ref[n].reshape(d, width)[:, :d]).astype(bf16)
            mixed_ref[:, :rows, n * d : (n + 1) * d] = got.reshape(images, rows, d)

        valid = lax.broadcasted_iota(jnp.int32, (1, lanes), 1) < seq
        parked.append(save(mixed_ref, mixed_hbm))

        for i in range(images):

            @pl.loop(0, TILES)
            def _(t):
                for u in range(some):
                    n = t * some + u
                    at = lambda part: pl.ds(pl.multiple_of(t * d + (part * some + u) * 128, 128), 128)
                    q, k, v = mixed_ref[i, :rows, at(0)], mixed_ref[i, :, at(1)], mixed_ref[i, :, at(2)]
                    got = []
                    for h in range(2):
                        mask = low_half if h == 0 else ~low_half
                        scores = dot_nt(jnp.where(mask, q, jnp.zeros_like(q)), k) * HEAD_DIM**-0.5
                        scores = jnp.where(valid, scores, -1e30)
                        e = jnp.exp(scores - jnp.max(scores, axis=-1, keepdims=True))
                        prob = (e * (1.0 / jnp.sum(e, axis=-1, keepdims=True))).astype(bf16)
                        probs_ref[i, n * 2 + h] = prob
                        got.append(dot(prob, v))
                    att_ref[i, :, pl.ds(pl.multiple_of(n * 128, 128), 128)] = jnp.where(low_half, got[0], got[1]).astype(bf16)

            added = [dot(att_ref[i], big_ref[t].reshape(d, width)[:, d:]) for t in range(TILES)]
            residual = x_ref[i] + jnp.concatenate(added, axis=1)
            res_ref[i] = residual
            tok_ref[i * lanes : i * lanes + rows, :] = (norm_parts(residual)[0] * gain_two).astype(bf16)
            dispatch(sa_ref, cuts[i], cuts[i + 1], (i + 1) * lanes)
            sends[i].start()
            if i < images - 1:
                for u in expert_units[:2]:
                    u.middle()
            parked.append(save(probs_ref.at[i], probs_hbm.at[i]))
            parked.append(save(att_ref.at[i], att_hbm.at[i]))
            parked.append(save(res_ref.at[i], res_hbm.at[i]))

        for cp in parked:
            cp.wait()

    pl.run_scoped(
        forward,
        pltpu.VMEM((images * lanes, d), bf16),
        pltpu.VMEM((images, rows, d), f32),
        pltpu.VMEM(mixed_hbm.shape, bf16),
        pltpu.VMEM(probs_hbm.shape, bf16),
        pltpu.VMEM(att_hbm.shape, bf16),
        pltpu.VMEM(res_hbm.shape, f32),
        pltpu.VMEM((images, 8, lanes), f32),
    )

    wr = sg_ref[...].reshape(d, 128)
    expert_sums = []
    for t in range(TILES):
        for w, (mine, sib, got, out) in enumerate(
            ((big_ref, sin_ref, xin_ref, gi_ref), (pback_ref, sback_ref, xback_ref, gb_ref))
        ):
            n = t * 2 + w
            expert_sums.append(
                PlaneScatter(
                    p, mine.at[t], sib.at[t], got.at[t], out.at[t],
                    lambda i, n=n: esend.at[n, i], lambda i, n=n: erecv.at[n, i],
                )
            )
    both = lambda t: expert_sums[2 * t : 2 * t + 2]

    def expert_part(wi_ref, wb_ref, act_ref, gh_ref):
        def fetch(t):
            copies = []
            for w, (src, dst) in enumerate(((wi_hbm, wi_ref), (wb_hbm, wb_ref))):
                n = t * 2 + w
                expert_units[n].arrive()
                own_saves[n].wait()
                copies.append(pltpu.make_async_copy(src.at[t], dst.at[t], isem.at[n]))
                copies[-1].start()
            for cp in copies:
                cp.wait()

        def weight_grads(t):
            flat = lambda v: v.reshape(nz * slots, v.shape[-1])
            got = dot_tn(flat(buf_ref[...]), flat(gh_ref[t]))
            big_ref[t] = got.astype(bf16).reshape(chips, 2, per, width)
            both(t)[0].start()
            got = dot_tn(flat(act_ref[t]), flat(gs_ref[...]))
            pback_ref[t] = got.astype(bf16).reshape(chips, 2, per_back, d)
            both(t)[1].start()

        for u in expert_units[2:]:
            u.middle()
        send_dy.wait()
        gr_ref[...] = jnp.zeros_like(gr_ref)
        def forth_and_back(i, lo, hi):
            expert_back(
                p, experts, lo, hi, wi_ref, wb_ref, buf_ref, gs_ref, act_ref, gh_ref, wr, sb_ref, sa_ref, gr_ref
            )
            backs[i].start()

        for i, (lo, hi) in enumerate(zip(cuts[:-1], cuts[1:])):
            sends[i].wait()
            expert_gates(p, experts, lo, hi, buf_ref, gs_ref, wr)
            for t in range(TILES):
                if i == 0:
                    for u in expert_units[2 * t : 2 * t + 2]:
                        u.last()
                    fetch(t)
                expert_tile(t, lo, hi, wi_ref, wb_ref, buf_ref, gs_ref, act_ref, gh_ref)
                if i == images - 1 and t == 0:
                    for u in layer_units + expert_units:
                        u.leave()
                    weight_grads(0)
            if i < images - 1:
                forth_and_back(i, lo, hi)
        PlaneScatter.middle(*both(0))
        weight_grads(1)
        forth_and_back(images - 1, cuts[images - 1], cuts[images])
        PlaneScatter.last(*both(0))
        PlaneScatter.middle(*both(1))
        weight_grads(2)
        for u in both(0):
            u.finish()

    pl.run_scoped(
        expert_part,
        pltpu.VMEM((TILES, ndp, per, width), bf16),
        pltpu.VMEM((TILES, ndp, per_back, d), bf16),
        pltpu.VMEM((TILES, nz, slots, width), bf16),
        pltpu.VMEM((TILES, nz, slots, width), bf16),
    )

    def backward(
        wl_ref, mixed_ref, probs_ref, att_ref, res_ref, gres_ref, branch_ref, gatt_ref, first_ref, tot_ref, lpart_ref,
        psm_ref, tsm_ref, zsent_ref, vec_ref,
    ):
        layer_sums, sum_lines = [], []
        for n in range(TILES + 1):
            mine, sib, got, tot, zs, zg = (
                (lpart_ref.at[n], lsin_ref.at[n], lxin_ref.at[n], tot_ref.at[n], zsent_ref.at[n], zs_ref.at[n])
                if n < TILES
                else (psm_ref, ssm_ref, xsm_ref, tsm_ref, zssm_ref, zgsm_ref)
            )
            layer_sums.append(
                PlaneScatter(p, mine, sib, got, tot, lambda i, n=n: ssend.at[n, i], lambda i, n=n: srecv.at[n, i])
            )
            sum_lines.append(LineScatter(p, fold if n < TILES else 1, zs, zg, usend.at[n], urecv.at[n]))

        copies = [
            pltpu.make_async_copy(src, dst, isem.at[n])
            for n, (src, dst) in enumerate(
                (
                    (res_hbm, res_ref), (wl_hbm, wl_ref), (att_hbm, att_ref), (mixed_hbm, mixed_ref),
                    (probs_hbm, probs_ref),
                )
            )
        ]
        for cp in copies:
            cp.start()
        PlaneScatter.middle(*both(TILES - 1))
        gains = jnp.transpose(wr.astype(f32))
        gain_one, gain_two = gains[experts : experts + 1, :], gains[experts + 1 : experts + 2, :]
        normed_one = lambda i: norm_parts(padded(img_ref[:, i, :].astype(f32), rows))
        for i in range(images):
            first_ref[i] = (normed_one(i)[0] * gain_one).astype(bf16)
        for cp in copies:
            cp.wait()
        PlaneScatter.last(*both(TILES - 2))
        for ex in backs:
            ex.wait()
        outs.start()
        vec_two = jnp.zeros((1, d), f32)
        for i in range(images):
            hits = place_ref[:, i * lanes : (i + 1) * lanes]
            grad_second = dot_tn(hits, rgrad_ref[...].reshape(experts * slots, d))[:rows]
            normed, inverse = norm_parts(res_ref[i])
            vec_two += jnp.sum(grad_second * normed, axis=0, keepdims=True)
            grad = padded(cot_ref[:, i, :].astype(f32), rows) + norm_back(grad_second * gain_two, normed, inverse)
            gres_ref[i] = grad
            branch = grad.astype(bf16)
            branch_ref[i] = branch
            gatt_ref[i] = sum(
                dot_nt(branch[:, t * part : (t + 1) * part], wl_ref[t].reshape(d, width)[:, d:])
                for t in range(TILES)
            ).astype(bf16)

        scale = HEAD_DIM**-0.5

        flat = lambda v: v.reshape(images * rows, v.shape[-1])
        for t in range(TILES):

            @pl.loop(0, some)
            def _(u):
                at = lambda j: pl.ds(pl.multiple_of(t * d + j * part + u * 128, 128), 128)
                here = pl.ds(pl.multiple_of(t * part + u * 128, 128), 128)
                for i in range(images):
                    q, k, v = mixed_ref[i, :rows, at(0)], mixed_ref[i, :, at(1)], mixed_ref[i, :, at(2)]
                    ga = gatt_ref[i, :, here]
                    gq, gk, gv = [], [], []
                    for h in range(2):
                        mask = low_half if h == 0 else ~low_half
                        prob = probs_ref[i, (t * some + u) * 2 + h]
                        gv.append(dot_tn(prob, ga)[:rows])
                        weighting = dot_nt(jnp.where(mask, ga, jnp.zeros_like(ga)), v)
                        wide = prob.astype(f32)
                        scores = wide * (weighting - jnp.sum(wide * weighting, axis=-1, keepdims=True))
                        scores = scores.astype(bf16)
                        gq.append(dot(scores, k))
                        gk.append(dot_tn(scores, q)[:rows])
                    pick = lambda pair, by: jnp.where(low_half, pair[0], pair[1]) * by
                    mixed_ref[i, :rows, at(0)] = pick(gq, scale).astype(bf16)
                    mixed_ref[i, :rows, at(1)] = pick(gk, scale).astype(bf16)
                    mixed_ref[i, :rows, at(2)] = pick(gv, 1.0).astype(bf16)

            got = dot_tn(flat(first_ref[...]), flat(mixed_ref[:, :rows, t * d : (t + 1) * d]))
            lpart_ref[t, :, :, :, :d] = got.astype(bf16).reshape(chips, 2, per, d)
            more = dot_tn(flat(att_ref[...]), flat(branch_ref[:, :, t * part : (t + 1) * part]))
            lpart_ref[t, :, :, :, d:] = more.astype(bf16).reshape(chips, 2, per, part)
            layer_sums[t].start()
            if t == 0:
                PlaneScatter.last(*both(TILES - 1))
            if t >= 1:
                PlaneScatter.middle(layer_sums[t - 1])
            if t >= 2:
                PlaneScatter.last(layer_sums[t - 2])

        def to_line(n):
            layer_sums[n].finish()
            ref = tot_ref.at[n] if n < TILES else tsm_ref
            if n < TILES:
                sum_lines[n].start(ref[...], group)
            else:
                for k in range(nz):
                    zssm_ref[k, :group, :] = tsm_ref[k * group : (k + 1) * group, :]
                for cp in sum_lines[n].copies:
                    cp.start()

        vec_one = jnp.zeros((1, d), f32)
        for i in range(images):
            grad_first = sum(
                dot_nt(mixed_ref[i, :rows, t * d : (t + 1) * d], wl_ref[t].reshape(d, width)[:, :d])
                for t in range(TILES)
            )
            normed, inverse = normed_one(i)
            vec_one += jnp.sum(grad_first * normed, axis=0, keepdims=True)
            gres_ref[i] += norm_back(grad_first * gain_one, normed, inverse)
            save(gres_ref.at[i], gin_hbm.at[i])
            if i == 0:
                PlaneScatter.middle(layer_sums[TILES - 1])
                PlaneScatter.last(layer_sums[TILES - 2])
                to_line(0)

        vec_ref[0:1, :] = vec_one
        vec_ref[1:2, :] = vec_two
        cols = jnp.transpose(vec_ref[...])
        small = jnp.where(
            lane == experts, cols[:, 0:1], jnp.where(lane == experts + 1, cols[:, 1:2], gr_ref[...])
        )
        psm_ref[...] = small.reshape(chips, 2, per, 128)
        layer_sums[TILES].start()
        PlaneScatter.last(layer_sums[TILES - 1])
        PlaneScatter.middle(layer_sums[TILES])
        for n in range(1, TILES - 1):
            to_line(n)
        PlaneScatter.last(layer_sums[TILES])
        to_line(TILES - 1)
        to_line(TILES)
        for n in range(1, TILES):
            for u in both(n):
                u.finish()

        def output(i):
            second = (norm_parts(res_ref[i])[0] * gain_two).astype(bf16)
            rp = router_softmax(second, wr, experts)
            total = res_ref[i]
            for e in range(experts):
                hits = place_ref[e * slots : (e + 1) * slots, i * lanes : (i + 1) * lanes]
                gate = jnp.sum(jnp.where(lane == e, rp, 0.0), axis=-1, keepdims=True)
                total = total + gate * dot_tn(hits, ro_ref[e])[:rows]
            gatt_ref[i] = total.astype(bf16)
            save(gatt_ref.at[i], out_hbm.at[i])

        outs.wait()
        for i in range(images):
            output(i)
        for n in range(TILES):
            gl_ref[:, n * width : (n + 1) * width] = sum_lines[n].finish(group)[:group]
        gsm_ref[...] = sum_lines[TILES].finish(zssm_ref.shape[1])[:group]

        for group_of in lines:
            for cp in group_of:
                cp.wait_send()
        for cp in saves:
            if not any(cp is done for done in parked):
                cp.wait()

    pl.run_scoped(
        backward,
        pltpu.VMEM(wl_hbm.shape, bf16),
        pltpu.VMEM(mixed_hbm.shape, bf16),
        pltpu.VMEM(probs_hbm.shape, bf16),
        pltpu.VMEM(att_hbm.shape, bf16),
        pltpu.VMEM(res_hbm.shape, f32),
        pltpu.VMEM((images, rows, d), f32),
        pltpu.VMEM((images, rows, d), bf16),
        pltpu.VMEM((images, rows, d), bf16),
        pltpu.VMEM((images, rows, d), bf16),
        pltpu.VMEM((TILES, per, width), f32),
        pltpu.VMEM((TILES, chips, 2, per, width), bf16),
        pltpu.VMEM((chips, 2, per, 128), f32),
        pltpu.VMEM((per, 128), f32),
        pltpu.VMEM(zs_ref.shape, bf16),
        pltpu.VMEM((8, d), f32),
    )


def block(ndp, nz, cap, slots, images, cotangent, priority, choices, router, gain_one, gain_two, wqkv, wout, win, wback):
    seq, count, d = images.shape
    experts = router.shape[0]
    rows, lanes = up(seq, 16), up(seq, 128)
    group, per, width = wqkv.shape[0], d // ndp, 4 * d // TILES
    per_back, chips = wback.shape[1], ndp // 2
    fold = 16 // math.gcd(group, 16)
    if width // fold % 128:
        fold = 1
    tall, short = up(group, 16), up(group, 8)
    line = fold * group if fold * group % 16 == 0 else tall
    shape, vm = jax.ShapeDtypeStruct, pltpu.VMEM
    dma = lambda *dims: [pltpu.SemaphoreType.DMA(dims)] * 2
    ng, ns, nb = PlaneGather.sems(ndp), PlaneScatter.sems(ndp), chips - 1
    return pl.pallas_call(
        partial(block_kernel, ndp, nz, cap, experts, fold),
        out_shape=(
            shape((TILES, ndp, per, width), bf16),
            shape((TILES, ndp, per_back, d), bf16),
            shape((TILES, chips, 2, per, width), bf16),
            shape((count, lanes, 3 * d), bf16),
            shape((count, d // HEAD_DIM, rows, lanes), bf16),
            shape((count, rows, d), bf16),
            shape((count, rows, d), f32),
            shape((count, rows, d), bf16),
            shape((count, rows, d), f32),
            shape((group, 4 * d), f32),
            shape((group, 128), f32),
            shape((TILES, per, width), f32),
            shape((TILES, per_back, d), f32),
        ),
        in_specs=[VM] * 11,
        out_specs=(ANY,) * 9 + (VM,) * 4,
        scratch_shapes=[
            vm((TILES, nz, line, width // fold), bf16),
            vm((nz, tall, 128), bf16),
            vm((TILES, chips, 2, per, width), bf16),
            vm((TILES, per, width), bf16),
            vm((ndp, per, 128), bf16),
        ]
        + [vm((nz, slots, d), bf16)] * 6
        + [
            vm((experts * slots, count * lanes), bf16),
            vm((TILES, chips, 2, per_back, d), bf16),
            vm((TILES, chips, per, width), bf16),
            vm((TILES, chips, per_back, d), bf16),
            vm((TILES, nb, per, width), bf16),
            vm((TILES, nb, per_back, d), bf16),
            vm((TILES, chips, per, width), bf16),
            vm((TILES, nb, per, width), bf16),
            vm((d, 128), f32),
            vm((chips, per, 128), f32),
            vm((nb, per, 128), f32),
            vm((nz, short, 128), f32),
            vm((nz, short, 128), f32),
        ]
        + dma(TILES + 1, ng) + dma(TILES + 1, nz) + dma(2 * TILES, ng) + dma(count, nz) + dma(nz)
        + dma(count, nz) + dma(nz) + dma(2 * TILES, ns) + dma(TILES + 1, ns) + dma(TILES + 1, nz)
        + [
            pltpu.SemaphoreType.DMA((3 * TILES + 1 + 5 * count,)),
            pltpu.SemaphoreType.DMA((2 * TILES,)),
        ],
        compiler_params=pltpu.CompilerParams(
            collective_id=0, has_side_effects=True, vmem_limit_bytes=VMEM_BYTES
        ),
        name="block",
    )(images, cotangent, priority, choices, router, gain_one, gain_two, wqkv, wout, win, wback)


def settle_kernel(
    experts, ndp,
    out_ref, gin_ref, gl_ref, gsm_ref, gi_ref, gb_ref,
    output_ref, input_grad_ref, gain_one_ref, qkv_ref, wout_ref, gain_two_ref, router_ref, in_ref, back_ref,
):
    group, d = wout_ref.shape
    part = d // TILES
    chunk = in_ref.shape[1] // ndp // TILES
    for i in range(out_ref.shape[0]):
        output_ref[:, i, :] = out_ref[i].astype(f32).astype(bf16)
        input_grad_ref[:, i, :] = gin_ref[i]
    for t in range(TILES):
        for i in range(ndp):
            in_ref[:, (i * TILES + t) * chunk : (i * TILES + t + 1) * chunk] = gi_ref[
                t, :, i * chunk : (i + 1) * chunk
            ]
    back_ref[...] = gb_ref[...]

    @pl.when(pl.program_id(0) == 0)
    def _():
        for t in range(TILES):
            for j in range(4):
                piece = gl_ref[:, t * 4 * part + j * part : t * 4 * part + (j + 1) * part]
                if j < 3:
                    qkv_ref[:, j * d + t * part : j * d + (t + 1) * part] = piece
                else:
                    wout_ref[:, t * part : (t + 1) * part] = piece
        small = jnp.transpose(padded(gsm_ref[...], 128))[:, :group]
        router_ref[...] = small[:experts]
        gain_one_ref[...] = small[experts : experts + 1]
        gain_two_ref[...] = small[experts + 1 : experts + 2]


def settle(experts, seq, ndp, out, gin, gl, gsm, gi, gb):
    group, d, count = gl.shape[0], out.shape[2], out.shape[0]
    rows, per, per_back = out.shape[1] // 2, gi.shape[1] // 2, gb.shape[1] // 2
    wide = gi.shape[0] * gi.shape[2]
    shape = jax.ShapeDtypeStruct
    whole = lambda *dims: pl.BlockSpec(dims, lambda n: (0,) * len(dims))
    half = lambda dims, axis: pl.BlockSpec(dims, lambda n: tuple(n if a == axis else 0 for a in range(len(dims))))
    return pl.pallas_call(
        partial(settle_kernel, experts, ndp),
        grid=(2,),
        out_shape=(
            shape((seq, count, d), bf16), shape((seq, count, d), f32), shape((1, group), f32),
            shape((group, 3 * d), f32), shape((group, d), f32), shape((1, group), f32), shape((experts, group), f32),
            shape((gi.shape[1], wide), f32), shape(gb.shape, f32),
        ),
        in_specs=[
            half((count, rows, d), 1), half((count, rows, d), 1), whole(group, 4 * d), whole(group, 128),
            half((TILES, per, gi.shape[2]), 1), half((TILES, per_back, d), 1),
        ],
        out_specs=(
            half((rows, count, d), 0), half((rows, count, d), 0), whole(1, group), whole(group, 3 * d),
            whole(group, d), whole(1, group), whole(experts, group), half((per, wide), 0),
            half((TILES, per_back, d), 1),
        ),
        compiler_params=pltpu.CompilerParams(vmem_limit_bytes=VMEM_BYTES),
        name="settle",
    )(out, gin, gl, gsm, gi, gb)


def per_device(ndp, nz, images, gain_one, w_qkv, w_out, gain_two, w_router, w_in, w_back, choices, priority, cotangent):
    count, seq, d = images.shape
    group, experts = w_router.shape
    ff = w_in.shape[2]
    cap = (42 * seq + 20 * experts - 1) // (20 * experts)
    slots = up(count * cap, 16)
    chunk = ff // ndp // TILES
    images, cotangent = images.transpose(1, 0, 2), cotangent.transpose(1, 0, 2)
    out, gin, gl, gsm, gi, gb = block(
        ndp, nz, cap, slots, images, cotangent, priority, choices.transpose(0, 2, 1),
        w_router.T, gain_one[None], gain_two[None],
        w_qkv, w_out, w_in[0], w_back[0].reshape(TILES, chunk, d),
    )[7:]
    out, gin, gain_one, qkv, wout, gain_two, router, gi, gb = settle(
        experts, seq, ndp, out, gin, gl, gsm, gi, gb
    )
    return (
        out.transpose(1, 0, 2), gin.transpose(1, 0, 2), gain_one[0], qkv, wout, gain_two[0], router.T,
        gi.reshape(1, d // ndp, ff), gb.reshape(1, ff // ndp, d),
    )


def solution(mesh):
    ndp, nz = mesh.shape["dp"], mesh.shape["fsdp"]
    both = ("dp", "fsdp")
    tokens, rows, expert_rows = P(both, None, None), P(both, None), P("fsdp", "dp", None)
    return jax.shard_map(
        partial(per_device, ndp, nz),
        mesh=mesh,
        in_specs=(tokens, P(both), rows, rows, P(both), rows, expert_rows, expert_rows, tokens, rows, tokens),
        out_specs=(tokens, tokens, P(both), rows, rows, P(both), rows, expert_rows, expert_rows),
        check_vma=False,
    )
```
